32 devices in a mesh: clips: 16 (over z, y, x), tm: 2 (over core).
Axes of the slice: x: 2, y: 2, z: 4, core: 2. Of those that a mesh axis runs over, the one named last changes fastest.
Arguments:
- tokens: bfloat16 [100352, 384], P(('clips', 'tm')), may hold values from -6 to 6
- frame_clip: int32 [512], P('clips'), may hold values from 0 to 47, as said below
- ln1_gain: bfloat16 [384], replicated, may hold values from 0.25 to 1.75
- ln1_bias: bfloat16 [384], replicated, may hold values from -1 to 1
- w_qkv: bfloat16 [384, 1152], replicated, may hold values from -0.4375 to 0.4375
- qv_bias: bfloat16 [2, 384], replicated, may hold values from -1 to 1
- w_out: bfloat16 [384, 384], replicated, may hold values from -1.75 to 1.75
- b_out: bfloat16 [384], replicated, may hold values from -1 to 1
- ln2_gain: bfloat16 [384], replicated, may hold values from 0.25 to 1.75
- ln2_bias: bfloat16 [384], replicated, may hold values from -1 to 1
- w_fc1: bfloat16 [384, 1536], replicated, may hold values from -0.3125 to 0.3125
- b_fc1: bfloat16 [1536], replicated, may hold values from -1.5 to 1.5
- w_fc2: bfloat16 [1536, 384], replicated, may hold values from -0.3125 to 0.3125
- b_fc2: bfloat16 [384], replicated, may hold values from -1 to 1
- cotangent: bfloat16 [100352, 384], P(('clips', 'tm')), may hold values from -6 to 6
Outputs:
- block_out: bfloat16 [100352, 384], P(('clips', 'tm'))
- input_grad: float32 [100352, 384], P(('clips', 'tm'))
- grad_ln1_gain: float32 [384], replicated
- grad_ln1_bias: float32 [384], replicated
- grad_w_qkv: float32 [384, 1152], replicated
- grad_qv_bias: float32 [2, 384], replicated
- grad_w_out: float32 [384, 384], replicated
- grad_b_out: float32 [384], replicated
- grad_ln2_gain: float32 [384], replicated
- grad_ln2_bias: float32 [384], replicated
- grad_w_fc1: float32 [384, 1536], replicated
- grad_b_fc1: float32 [1536], replicated
- grad_w_fc2: float32 [1536, 384], replicated
- grad_b_fc2: float32 [384], replicated
The draws below stay inside these ranges and needn't reach their ends.
Inputs may be any that keep to these rules, and one draw needn't show every extreme that they name: `frame_clip`: clip numbers never fall along the frames; frames of different groups of 32 frames carry different numbers; in every group one clip runs from inside its first 16 frames into its last 16 frames.
All inputs are finite; a program needn't handle non-finite values.
Results may differ from the reference program's by a relative error of at most 0.012.
The reference program's roundings to bfloat16 on the way count: a program that leaves them out, or rounds other values in their place, can miss the bound.
Values may be sent and summed in bfloat16 or wider, within the bound.
A program may use at most 192 MiB of HBM per device.

```python
import math
import jax
import jax.numpy as jnp
from jax import lax

D = 384
HEADS = 6
FF = 1536
FRAME = 196
FR_DEV = 16
GROUP_FR = 32
NFRAMES = 512
TOKENS = 100352


def draw_frame_clip(key, part):
    key = jax.random.fold_in(key, 11)
    groups = NFRAMES // GROUP_FR
    half_span = FR_DEV // 2
    first_key, second_key = jax.random.split(key)
    starts = jax.random.randint(first_key, (groups, 1), FR_DEV - half_span, FR_DEV)
    stops = jax.random.randint(second_key, (groups, 1), GROUP_FR - FR_DEV + 1, GROUP_FR - FR_DEV + half_span + 1)
    position = jnp.arange(GROUP_FR, dtype=jnp.int32)[None, :]
    within = (position >= starts).astype(jnp.int32) + (position >= stops).astype(jnp.int32)
    return (3 * jnp.arange(groups, dtype=jnp.int32)[:, None] + within).reshape(NFRAMES)


def block_levels(rng, extent, pieces, smallest, high):
    gain, own = 1.0, jax.random.fold_in(rng, 6)
    for dim, blocks in pieces:
        steps = jnp.exp(jax.random.uniform(jax.random.fold_in(own, dim), (blocks,), jnp.float32, smallest / len(pieces), high / len(pieces)))
        gain = gain * jnp.repeat(steps, extent[dim] // blocks).reshape([-1 if axis == dim else 1 for axis in range(len(extent))])
    return gain


def gaussian(own_key, dims, scale, limit, cuts=(), kind=jnp.bfloat16):
    drawn = scale * jax.random.normal(own_key, dims, jnp.float32)
    if cuts:
        drawn = drawn * block_levels(own_key, dims, cuts, -0.22, 0.18)
    return jnp.clip(drawn, -limit, limit).astype(kind)


def setup_inputs(seed: int = 0) -> dict:
    streams_of = jax.random.split(jax.random.key(seed), 16)
    tokens = gaussian(streams_of[0], (TOKENS, D), 1.0, 6.0, ((0, 32),))
    frame_clip = draw_frame_clip(jax.random.fold_in(streams_of[15], 71), 0)
    ln1_gain = jnp.clip(1.0 + 0.15 * jax.random.normal(streams_of[2], (D,), jnp.float32), 0.25, 1.75).astype(jnp.bfloat16)
    ln1_bias = gaussian(streams_of[3], (D,), 0.2, 1.0)
    w_qkv = gaussian(streams_of[4], (D, 3 * D), (D // 2) ** -0.5, 0.4375)
    qv_bias = gaussian(streams_of[5], (2, D), 0.2, 1.0)
    w_out = gaussian(streams_of[6], (D, D), (D // 32) ** -0.5, 1.75)
    b_out = gaussian(streams_of[7], (D,), 0.2, 1.0)
    ln2_gain = jnp.clip(1.0 + 0.15 * jax.random.normal(streams_of[8], (D,), jnp.float32), 0.25, 1.75).astype(jnp.bfloat16)
    ln2_bias = gaussian(streams_of[9], (D,), 0.2, 1.0)
    w_fc1 = gaussian(streams_of[10], (D, FF), D ** -0.5, 0.3125)
    b_fc1 = gaussian(streams_of[11], (FF,), 0.3, 1.5)
    w_fc2 = gaussian(streams_of[12], (FF, D), (FF // 4) ** -0.5, 0.3125)
    b_fc2 = gaussian(streams_of[13], (D,), 0.2, 1.0)
    cotangent = gaussian(streams_of[14], (TOKENS, D), 1.0, 6.0, ((0, 32),))
    return dict(tokens=tokens, frame_clip=frame_clip, ln1_gain=ln1_gain, ln1_bias=ln1_bias, w_qkv=w_qkv, qv_bias=qv_bias, w_out=w_out, b_out=b_out, ln2_gain=ln2_gain, ln2_bias=ln2_bias, w_fc1=w_fc1, b_fc1=b_fc1, w_fc2=w_fc2, b_fc2=b_fc2, cotangent=cotangent)


@jax.custom_vjp
def low(v):
    return lax.optimization_barrier(v.astype(jnp.bfloat16)).astype(jnp.float32)

@jax.custom_vjp
def low_back(v):
    return v

def low_keep(v):
    return (low(v), None)

def low_pass(kept, grad):
    return (grad,)

def back_keep(v):
    return (v, None)

def back_low(kept, grad):
    return (low(grad),)
low.defvjp(low_keep, low_pass)
low_back.defvjp(back_keep, back_low)

def layer_norm(values, gain_vec, shift_vec):
    row_mean = lax.optimization_barrier(jnp.mean(values, axis=-1, keepdims=True))
    centred = values - row_mean
    variance = lax.optimization_barrier(jnp.mean(centred * centred, axis=-1, keepdims=True))
    return centred * lax.rsqrt(variance + 1e-06) * gain_vec + shift_vec

def product(left_arr, right_arr):
    return jnp.einsum('...c,ce->...e', left_arr, right_arr, precision=lax.Precision.HIGHEST)

def group_layer(inputs, clip_ids, params):
    ln1_gain, ln1_bias, w_qkv, qv_bias, w_out, b_out, ln2_gain, ln2_bias, w_fc1, b_fc1, w_fc2, b_fc2 = params
    frames = inputs.shape[0]
    feat_width = inputs.shape[-1]
    head_dim = feat_width // HEADS
    attn_in = low(layer_norm(inputs, ln1_gain, ln1_bias))
    bias_full = jnp.concatenate([qv_bias[0], jnp.zeros((feat_width,), jnp.float32), qv_bias[1]])
    qkv = low(low_back(product(attn_in, w_qkv) + bias_full))
    queries = qkv[..., :feat_width].reshape(frames, FRAME, HEADS, head_dim)
    kv_pad = jnp.pad(qkv[..., feat_width:], ((1, 1), (0, 0), (0, 0)))
    kv_three = jnp.concatenate([kv_pad[:-2], kv_pad[1:-1], kv_pad[2:]], axis=1)
    keys = kv_three[..., :feat_width].reshape(frames, 3 * FRAME, HEADS, head_dim)
    values = kv_three[..., feat_width:].reshape(frames, 3 * FRAME, HEADS, head_dim)
    ids_pad = jnp.pad(clip_ids, 1, constant_values=-1)
    frame_ok = jnp.stack([ids_pad[:-2] == clip_ids, ids_pad[1:-1] == clip_ids, ids_pad[2:] == clip_ids], axis=1)
    key_ok = jnp.repeat(frame_ok, FRAME, axis=1)
    score_scale = 1.0 / math.sqrt(head_dim)
    scores = low_back(jnp.einsum('gihd,gjhd->ghij', queries, keys, precision=lax.Precision.HIGHEST) * score_scale)
    scores = jnp.where(key_ok[:, None, None, :], scores, -1e+30)
    row_max = lax.optimization_barrier(jnp.max(scores, axis=-1, keepdims=True))
    powered = jnp.exp(scores - row_max)
    prob_vals = powered / lax.optimization_barrier(jnp.sum(powered, axis=-1, keepdims=True))
    attended = jnp.einsum('ghij,gjhd->gihd', low(prob_vals), values, precision=lax.Precision.HIGHEST)
    attended = low(low_back(attended.reshape(frames, FRAME, feat_width)))
    resid = inputs + low_back(product(attended, w_out) + b_out)
    mlp_in = low(layer_norm(resid, ln2_gain, ln2_bias))
    pre_act = low_back(product(mlp_in, w_fc1) + b_fc1)
    hidden = low(jax.nn.gelu(pre_act, approximate=False))
    return resid + product(hidden, w_fc2) + b_fc2

def reference(tokens, frame_clip, ln1_gain, ln1_bias, w_qkv, qv_bias, w_out, b_out, ln2_gain, ln2_bias, w_fc1, b_fc1, w_fc2, b_fc2, cotangent):
    groups = NFRAMES // GROUP_FR
    inputs = tokens.astype(jnp.float32).reshape(groups, GROUP_FR, FRAME, D)
    clip_ids = frame_clip.reshape(groups, GROUP_FR)
    params = tuple((weight_arr.astype(jnp.float32) for weight_arr in (ln1_gain, ln1_bias, w_qkv, qv_bias, w_out, b_out, ln2_gain, ln2_bias, w_fc1, b_fc1, w_fc2, b_fc2)))
    checked = jax.checkpoint(group_layer)

    def forward(group_inputs, group_params):
        return lax.map(lambda group_pair: checked(group_pair[0], group_pair[1], group_params), (group_inputs, clip_ids))
    outputs, pullback = jax.vjp(forward, inputs, params)
    input_grad, grads = pullback(cotangent.astype(jnp.float32).reshape(groups, GROUP_FR, FRAME, D))
    return (outputs.reshape(TOKENS, D).astype(jnp.bfloat16), input_grad.reshape(TOKENS, D), grads[0], grads[1], grads[2], grads[3], grads[4], grads[5], grads[6], grads[7], grads[8], grads[9], grads[10], grads[11])
```

```python
import functools
import math

import jax
import jax.numpy as jnp
from jax import lax
from jax.experimental import pallas as pl
from jax.experimental.pallas import tpu as pltpu
from jax.sharding import PartitionSpec as P

HEADS = 6
FRAME = 196
ROWS = 208
WIN = 640
EPS = 1e-6
LOG2E = math.log2(math.e)

bf16 = jnp.bfloat16
f32 = jnp.float32


def mm(a, b):
    return jnp.dot(a, b, preferred_element_type=f32)


def mm_nt(a, b):
    return lax.dot_general(a, b, (((1,), (1,)), ((), ())), preferred_element_type=f32)


def mm_tn(a, b):
    return lax.dot_general(a, b, (((0,), (0,)), ((), ())), preferred_element_type=f32)


def normed_of(x):
    mean = jnp.mean(x, axis=-1, keepdims=True)
    centred = x - mean
    var = jnp.mean(centred * centred, axis=-1, keepdims=True)
    inverse = lax.rsqrt(var + EPS)
    return centred * inverse, inverse


def norm_back(upstream, normed, inverse, gain):
    scaled = upstream * gain
    mean = jnp.mean(scaled, axis=-1, keepdims=True)
    along = jnp.mean(scaled * normed, axis=-1, keepdims=True)
    return inverse * (scaled - mean - normed * along)


def fold8(v):
    rows, cols = v.shape
    return jnp.sum(v.reshape(rows // 8, 8, cols), axis=0)


def forward_kernel(
    clip_ref,
    x_ref,
    ghost_ref,
    cot_ref,
    g1_ref,
    s1_ref,
    wqkv_ref,
    bqkv_ref,
    wout_ref,
    bout_ref,
    g2_ref,
    s2_ref,
    w1_ref,
    b1_ref,
    w2_ref,
    b2_ref,
    q_ref,
    kv_ref,
    prob_ref,
    out_ref,
    gatt_ref,
    gres_ref,
    gw1_ref,
    gw2_ref,
    gwo_ref,
    sb1_ref,
    s384_ref,
):
    step = pl.program_id(0)
    steps = pl.num_programs(0)
    frames = 2 * steps
    width = x_ref.shape[-1]
    hidden = w1_ref.shape[-1]
    tm = lax.axis_index("tm")

    @pl.when(step == 0)
    def _():
        gw1_ref[...] = jnp.zeros_like(gw1_ref)
        gw2_ref[...] = jnp.zeros_like(gw2_ref)
        gwo_ref[...] = jnp.zeros_like(gwo_ref)
        sb1_ref[...] = jnp.zeros_like(sb1_ref)
        s384_ref[...] = jnp.zeros_like(s384_ref)
        gain = g1_ref[...].astype(f32)
        shift = s1_ref[...].astype(f32)
        bias = bqkv_ref[...]
        zero_slot = jnp.where(tm == 0, 0, frames + 1)
        ghost_slot = frames + 1 - zero_slot
        kv_ref[pl.ds(pl.multiple_of(zero_slot * ROWS, 16), ROWS), :] = jnp.zeros((ROWS, 2 * width), bf16)
        kv_ref[(frames + 2) * ROWS :, :] = jnp.zeros((WIN - 3 * ROWS, 2 * width), bf16)

        x = ghost_ref[...].astype(f32)
        n, _ = normed_of(x)
        kv = mm((n * gain + shift).astype(bf16), wqkv_ref[:, width:]) + bias[:, width:]
        kv_ref[pl.ds(pl.multiple_of(ghost_slot * ROWS, 16), ROWS), :] = kv.astype(bf16)

        def project(i, carry):
            x = x_ref[pl.ds(2 * i, 2)].reshape(2 * ROWS, width).astype(f32)
            n, _ = normed_of(x)
            qkv = (mm((n * gain + shift).astype(bf16), wqkv_ref[...]) + bias).astype(bf16)
            q_ref[pl.ds(2 * i, 2)] = qkv[:, :width].reshape(2, ROWS, width)
            kv_ref[pl.ds(pl.multiple_of((2 * i + 1) * ROWS, 16), 2 * ROWS), :] = qkv[:, width:]
            return carry

        lax.fori_loop(0, frames // 2, project, 0)

    lane = lax.broadcasted_iota(jnp.int32, (ROWS, 128), 1)
    low_half = lane < 64
    col = lax.broadcasted_iota(jnp.int32, (1, WIN), 1)
    scale = LOG2E / math.sqrt(width // HEADS)
    attended = []
    for sub in range(2):
        frame = 2 * step + sub
        here = tm * frames + frame
        own = clip_ref[here]
        before = jnp.where(here > 0, clip_ref[jnp.maximum(here - 1, 0)], -1)
        after = jnp.where(here < 2 * frames - 1, clip_ref[jnp.minimum(here + 1, 2 * frames - 1)], -1)
        lo = jnp.where(before == own, 0, ROWS)
        hi = jnp.where(after == own, 3 * ROWS, 2 * ROWS)
        slot = col // ROWS
        live = (col >= lo) & (col < hi) & (col - slot * ROWS < FRAME)
        mask = jnp.where(live, 0.0, -1e30).astype(f32)
        window = pl.ds(pl.multiple_of(frame * ROWS, 16), WIN)
        for pair in range(HEADS // 2):
            q = q_ref[frame, :, 128 * pair : 128 * pair + 128]
            k = kv_ref[window, 128 * pair : 128 * pair + 128]
            v = kv_ref[window, width + 128 * pair : width + 128 * pair + 128]
            parts = []
            for half in range(2):
                mine = low_half if half == 0 else ~low_half
                s = mm_nt(jnp.where(mine, q, jnp.zeros_like(q)), k) + mask
                top = jnp.max(s, axis=-1, keepdims=True)
                e = jnp.exp2((s - top) * scale)
                total = jnp.sum(e, axis=-1, keepdims=True)
                prob = (e * (1.0 / total)).astype(bf16)
                prob_ref[sub, 2 * pair + half] = prob
                parts.append(mm(prob, v))
            attended.append(jnp.where(low_half, parts[0], parts[1]).astype(bf16))
    att = jnp.concatenate(
        [
            jnp.concatenate([attended[p], attended[HEADS // 2 + p]], axis=0)
            for p in range(HEADS // 2)
        ],
        axis=1,
    )
    x = x_ref[pl.ds(2 * step, 2)].reshape(2 * ROWS, width).astype(f32)
    resid = x + mm(att, wout_ref[...]) + bout_ref[...].astype(f32)
    n2, inv2 = normed_of(resid)
    mlp_in = (n2 * g2_ref[...].astype(f32) + s2_ref[...].astype(f32)).astype(bf16)
    cot = cot_ref[...].reshape(2 * ROWS, width)
    out = resid + b2_ref[...].astype(f32)
    up = jnp.zeros((2 * ROWS, width), f32)
    chunk = 512
    for c in range(hidden // chunk):
        cols = slice(c * chunk, (c + 1) * chunk)
        pre = mm(mlp_in, w1_ref[:, cols]) + b1_ref[:, cols].astype(f32)
        cdf = 0.5 * (1.0 + lax.erf(pre * (1.0 / math.sqrt(2.0))))
        hid = (pre * cdf).astype(bf16)
        dens = jnp.exp2(pre * pre * (-0.5 * LOG2E)) * (1.0 / math.sqrt(2.0 * math.pi))
        out = out + mm(hid, w2_ref[cols, :])
        gw2_ref[:, cols] += mm_tn(cot, hid)
        gpre32 = mm_nt(cot, w2_ref[cols, :]) * (cdf + pre * dens)
        gpre = gpre32.astype(bf16)
        sb1_ref[:, cols] += fold8(gpre.astype(f32))
        gw1_ref[:, cols] += mm_tn(mlp_in, gpre)
        up = up + mm_nt(gpre, w1_ref[:, cols])
    out_ref[...] = out.astype(bf16).reshape(2, ROWS, width)
    cot32 = cot.astype(f32)
    gres = cot32 + norm_back(up, n2, inv2, g2_ref[...].astype(f32))
    gres_ref[...] = gres.reshape(2, ROWS, width)
    branch = gres.astype(bf16)
    gwo_ref[...] += mm_tn(att, branch)
    gatt_ref[...] = mm_nt(branch, wout_ref[...]).astype(bf16).reshape(2, ROWS, width)
    s384_ref[0] += fold8(up * n2)
    s384_ref[1] += fold8(up)
    s384_ref[2] += fold8(branch.astype(f32))
    s384_ref[3] += fold8(cot32)


def back_kernel(q_ref, kv_ref, prob_ref, gatt_ref, dq_ref, dkv_ref, edge_ref, acc_ref):
    step = pl.program_id(0)
    steps = pl.num_programs(0)
    frames = 2 * steps
    width = q_ref.shape[-1]
    tm = lax.axis_index("tm")
    inv_scale = 1.0 / math.sqrt(width // HEADS)

    @pl.when(step == 0)
    def _():
        acc_ref[...] = jnp.zeros_like(acc_ref)

    lane = lax.broadcasted_iota(jnp.int32, (ROWS, 128), 1)
    low_half = lane < 64
    for sub in range(2):
        frame = 2 * step + sub
        window = pl.ds(pl.multiple_of(frame * ROWS, 16), WIN)
        for pair in range(HEADS // 2):
            cols = slice(128 * pair, 128 * pair + 128)
            vcols = slice(width + 128 * pair, width + 128 * pair + 128)
            q = q_ref[sub, :, cols]
            g = gatt_ref[sub, :, cols]
            k = kv_ref[window, cols]
            v = kv_ref[window, vcols]
            dq, dk, dv = [], 0.0, 0.0
            for half in range(2):
                mine = low_half if half == 0 else ~low_half
                gm = jnp.where(mine, g, jnp.zeros_like(g))
                qm = jnp.where(mine, q, jnp.zeros_like(q))
                prob_bf = prob_ref[sub, 2 * pair + half]
                prob = prob_bf.astype(f32)
                dp = mm_nt(gm, v)
                dot = jnp.sum(prob * dp, axis=-1, keepdims=True)
                ds = (prob * (dp - dot)).astype(bf16)
                dq.append(mm(ds, k))
                dk = dk + mm_tn(ds, qm)
                dv = dv + mm_tn(prob_bf, gm)
            dq_ref[sub, :, cols] = (jnp.where(low_half, dq[0], dq[1]) * inv_scale).astype(bf16)
            acc_ref[window, cols] += dk
            acc_ref[window, vcols] += dv

    @pl.when(step == steps - 1)
    def _():
        def finish(i, carry):
            rows = pl.ds(pl.multiple_of((i + 1) * ROWS, 16), ROWS)
            dkv_ref[i, :, :width] = (acc_ref[rows, :width] * inv_scale).astype(bf16)
            dkv_ref[i, :, width:] = acc_ref[rows, width:].astype(bf16)
            return carry

        lax.fori_loop(0, frames, finish, 0)
        own = pl.ds(pl.multiple_of(jnp.where(tm == 0, frames, 1) * ROWS, 16), ROWS)
        ghost = pl.ds(pl.multiple_of(jnp.where(tm == 0, frames + 1, 0) * ROWS, 16), ROWS)
        edge_ref[0, :, :width] = acc_ref[own, :width] * inv_scale
        edge_ref[0, :, width:] = acc_ref[own, width:]
        edge_ref[1, :, :width] = acc_ref[ghost, :width] * inv_scale
        edge_ref[1, :, width:] = acc_ref[ghost, width:]


def input_kernel(x_ref, dq_ref, dkv_ref, edge_ref, got_ref, gres_ref, g1_ref, s1_ref, wqkv_ref,
                 out_ref, gw_ref, sq_ref, s384_ref):
    step = pl.program_id(0)
    steps = pl.num_programs(0)
    frames = 2 * steps
    width = x_ref.shape[-1]
    tm = lax.axis_index("tm")

    @pl.when(step == 0)
    def _():
        gw_ref[...] = jnp.zeros_like(gw_ref)
        sq_ref[...] = jnp.zeros_like(sq_ref)
        s384_ref[...] = jnp.zeros_like(s384_ref)

    edge_frame = jnp.where(tm == 0, frames - 1, 0)

    @pl.when(step == edge_frame // 2)
    def _():
        dkv_ref[edge_frame % 2] = (edge_ref[0] + got_ref[...].astype(f32)).astype(bf16)

    x = x_ref[...].reshape(2 * ROWS, width).astype(f32)
    n, inv = normed_of(x)
    gain = g1_ref[...].astype(f32)
    attn_in = (n * gain + s1_ref[...].astype(f32)).astype(bf16)
    dq = dq_ref[...].reshape(2 * ROWS, width)
    dkv = dkv_ref[...].reshape(2 * ROWS, 2 * width)
    gw_ref[:, :width] += mm_tn(attn_in, dq)
    gw_ref[:, width:] += mm_tn(attn_in, dkv)
    sq_ref[:, :width] += fold8(dq.astype(f32))
    sq_ref[:, width:] += fold8(dkv[:, width:].astype(f32))
    up = mm_nt(dq, wqkv_ref[:, :width]) + mm_nt(dkv, wqkv_ref[:, width:])
    gres = gres_ref[...].reshape(2 * ROWS, width)
    out_ref[...] = (gres + norm_back(up, n, inv, gain)).reshape(2, ROWS, width)
    s384_ref[0] += fold8(up * n)
    s384_ref[1] += fold8(up)


def whole(shape):
    return pl.BlockSpec(shape, lambda i: (0,) * len(shape), pipeline_mode=pl.Buffered(1))


def pairs(shape):
    return pl.BlockSpec((2,) + shape, lambda i: (i,) + (0,) * len(shape))


def params():
    return pltpu.CompilerParams(vmem_limit_bytes=60 * 2**20)


def per_device(tokens, frame_clip, ln1_gain, ln1_bias, w_qkv, qv_bias, w_out, b_out, ln2_gain, ln2_bias,
               w_fc1, b_fc1, w_fc2, b_fc2, cotangent):
    count, width = tokens.shape
    hidden = w_fc1.shape[1]
    frames = count // FRAME
    steps = frames // 2
    tm = lax.axis_index("tm")
    pad = ((0, 0), (0, ROWS - FRAME), (0, 0))
    x_pad = jnp.pad(tokens.reshape(frames, FRAME, width), pad)
    cot_pad = jnp.pad(cotangent.reshape(frames, FRAME, width), pad)
    edge = jnp.where(tm == 0, tokens[count - FRAME :], tokens[:FRAME])
    ghost = jnp.pad(lax.ppermute(edge, "tm", [(0, 1), (1, 0)]), pad[1:])
    row = lambda v: v.reshape(1, -1)
    bias_qkv = jnp.concatenate([qv_bias[0], jnp.zeros((width,), bf16), qv_bias[1]]).astype(f32)
    kv_rows = (frames + 2) * ROWS + WIN - 3 * ROWS
    shape = jax.ShapeDtypeStruct
    q, kv, prob, out_pad, gatt, gres, gw1, gw2t, gwo, sb1, s2 = pl.pallas_call(
        forward_kernel,
        grid=(steps,),
        in_specs=[
            pl.BlockSpec(memory_space=pltpu.SMEM),
            whole((frames, ROWS, width)),
            whole((ROWS, width)),
            pairs((ROWS, width)),
            whole((1, width)),
            whole((1, width)),
            whole((width, 3 * width)),
            whole((1, 3 * width)),
            whole((width, width)),
            whole((1, width)),
            whole((1, width)),
            whole((1, width)),
            whole((width, hidden)),
            whole((1, hidden)),
            whole((hidden, width)),
            whole((1, width)),
        ],
        out_specs=[
            whole((frames, ROWS, width)),
            whole((kv_rows, 2 * width)),
            pairs((HEADS, ROWS, WIN)),
            pairs((ROWS, width)),
            pairs((ROWS, width)),
            pairs((ROWS, width)),
            whole((width, hidden)),
            whole((width, hidden)),
            whole((width, width)),
            whole((8, hidden)),
            whole((4, 8, width)),
        ],
        out_shape=[
            shape((frames, ROWS, width), bf16),
            shape((kv_rows, 2 * width), bf16),
            shape((frames, HEADS, ROWS, WIN), bf16),
            shape((frames, ROWS, width), bf16),
            shape((frames, ROWS, width), bf16),
            shape((frames, ROWS, width), f32),
            shape((width, hidden), f32),
            shape((width, hidden), f32),
            shape((width, width), f32),
            shape((8, hidden), f32),
            shape((4, 8, width), f32),
        ],
        compiler_params=params(),
    )(frame_clip, x_pad, ghost, cot_pad, row(ln1_gain), row(ln1_bias), w_qkv, row(bias_qkv), w_out, row(b_out),
      row(ln2_gain), row(ln2_bias), w_fc1, row(b_fc1), w_fc2, row(b_fc2))

    dq, dkv, edges = pl.pallas_call(
        back_kernel,
        grid=(steps,),
        in_specs=[
            pairs((ROWS, width)),
            whole((kv_rows, 2 * width)),
            pairs((HEADS, ROWS, WIN)),
            pairs((ROWS, width)),
        ],
        out_specs=[
            pairs((ROWS, width)),
            whole((frames, ROWS, 2 * width)),
            whole((2, ROWS, 2 * width)),
        ],
        out_shape=[
            shape((frames, ROWS, width), bf16),
            shape((frames, ROWS, 2 * width), bf16),
            shape((2, ROWS, 2 * width), f32),
        ],
        scratch_shapes=[pltpu.VMEM((kv_rows, 2 * width), f32)],
        compiler_params=params(),
    )(q, kv, prob, gatt)

    got = lax.ppermute(edges[1].astype(bf16), "tm", [(0, 1), (1, 0)])

    in_pad, gwqkv, sqkv, s1 = pl.pallas_call(
        input_kernel,
        grid=(steps,),
        in_specs=[
            pairs((ROWS, width)),
            pairs((ROWS, width)),
            pairs((ROWS, 2 * width)),
            whole((2, ROWS, 2 * width)),
            whole((ROWS, 2 * width)),
            pairs((ROWS, width)),
            whole((1, width)),
            whole((1, width)),
            whole((width, 3 * width)),
        ],
        out_specs=[
            pairs((ROWS, width)),
            whole((width, 3 * width)),
            whole((8, 2 * width)),
            whole((2, 8, width)),
        ],
        out_shape=[
            shape((frames, ROWS, width), f32),
            shape((width, 3 * width), f32),
            shape((8, 2 * width), f32),
            shape((2, 8, width), f32),
        ],
        compiler_params=params(),
    )(x_pad, dq, dkv, edges, got, gres, row(ln1_gain), row(ln1_bias), w_qkv)

    block_out = out_pad[:, :FRAME].reshape(count, width)
    input_grad = in_pad[:, :FRAME].reshape(count, width)
    s1 = jnp.sum(s1, axis=1)
    s2 = jnp.sum(s2, axis=1)
    sq = jnp.sum(sqkv, axis=0).reshape(2, width)
    grads = lax.psum(
        (s1[0], s1[1], gwqkv, sq, gwo, s2[2], s2[0], s2[1], gw1, jnp.sum(sb1, axis=0), gw2t.T, s2[3]),
        ("clips", "tm"),
    )
    return (block_out, input_grad) + tuple(grads)


def solution(mesh):
    rows = P(("clips", "tm"), None)
    rep = P()
    return jax.shard_map(
        per_device,
        mesh=mesh,
        in_specs=(rows, P("clips")) + (rep,) * 12 + (rows,),
        out_specs=(rows, rows) + (rep,) * 12,
        check_vma=False,
    )
```

```python
import functools
import math

import jax
import jax.numpy as jnp
from jax import lax
from jax.experimental import pallas as pl
from jax.experimental.pallas import tpu as pltpu
from jax.sharding import PartitionSpec as P

HEADS = 6
FRAME = 196
ROWS = 208
WIN = 640
EPS = 1e-6
LOG2E = math.log2(math.e)

bf16 = jnp.bfloat16
f32 = jnp.float32


def mm(a, b):
    return jnp.dot(a, b, preferred_element_type=f32)


def mm_nt(a, b):
    return lax.dot_general(a, b, (((1,), (1,)), ((), ())), preferred_element_type=f32)


def mm_tn(a, b):
    return lax.dot_general(a, b, (((0,), (0,)), ((), ())), preferred_element_type=f32)


def normed_of(x):
    mean = jnp.mean(x, axis=-1, keepdims=True)
    centred = x - mean
    var = jnp.mean(centred * centred, axis=-1, keepdims=True)
    inverse = lax.rsqrt(var + EPS)
    return centred * inverse, inverse


def norm_back(upstream, normed, inverse, gain):
    scaled = upstream * gain
    mean = jnp.mean(scaled, axis=-1, keepdims=True)
    along = jnp.mean(scaled * normed, axis=-1, keepdims=True)
    return inverse * (scaled - mean - normed * along)


def fold8(v):
    rows, cols = v.shape
    return jnp.sum(v.reshape(rows // 8, 8, cols), axis=0)


MESH = pl.DeviceIdType.MESH


def stages_of(clips):
    stages, stride = [("tm", 1, 2)], 1
    while clips > 1:
        size = 4 if clips % 4 == 0 else (2 if clips % 2 == 0 else clips)
        stages.append(("clips", stride, size))
        stride, clips = stride * size, clips // size
    return stages


def digit(stage):
    axis, stride, size = stage
    return lax.rem(lax.axis_index(axis) // stride, size)


def partner(stage, turn):
    axis, stride, size = stage
    mine = digit(stage)
    return {axis: lax.axis_index(axis) + (lax.rem(mine + turn, size) - mine) * stride}


def greet(stages):
    sem, count = pltpu.get_barrier_semaphore(), 0
    for stage in stages:
        for turn in range(1, stage[2]):
            pl.semaphore_signal(sem, inc=1, device_id=partner(stage, turn), device_id_type=MESH)
            count += 1
    pl.semaphore_wait(sem, count)


class Sum:
    def __init__(self, stages, pack, result, landing, sent, came):
        self.stages, self.pack, self.result, self.landing = stages, pack, result, landing
        self.sent, self.came = sent, came
        self.segments, start, length = [], 0, pack.shape[0]
        for stage in stages:
            self.segments.append((start, length))
            length = length // stage[2]
            start = start + digit(stage) * length
        self.segments.append((start, length))
        self.first = [sum(s[2] - 1 for s in stages[:i]) for i in range(len(stages) + 1)]

    def _scatter(self, i):
        stage, (start, length) = self.stages[i], self.segments[i]
        part = length // stage[2]
        for turn in range(1, stage[2]):
            slot = self.first[i] + turn - 1
            other = lax.rem(digit(stage) + turn, stage[2])
            yield pltpu.make_async_remote_copy(
                src_ref=self.pack.at[pl.ds(start + other * part, part)],
                dst_ref=self.landing[i].at[turn - 1],
                send_sem=self.sent.at[slot],
                recv_sem=self.came.at[slot],
                device_id=partner(stage, turn),
                device_id_type=MESH,
            )

    def _gather(self, i):
        stage, (start, length) = self.stages[i], self.segments[i + 1]
        for turn in range(1, stage[2]):
            slot = self.first[-1] + self.first[i] + turn - 1
            here = self.result.at[pl.ds(start, length)]
            yield pltpu.make_async_remote_copy(
                src_ref=here,
                dst_ref=here,
                send_sem=self.sent.at[slot],
                recv_sem=self.came.at[slot],
                device_id=partner(stage, turn),
                device_id_type=MESH,
            )

    def send(self, i):
        for copy in self._scatter(i):
            copy.start()

    def take(self, i):
        for copy in self._scatter(i):
            copy.wait()
        start, length = self.segments[i + 1]
        into = self.result if i == len(self.stages) - 1 else self.pack
        block = next(b for b in (28, 24, 21, 16, 14, 12, 8, 7, 6, 4, 3, 2, 1) if length % b == 0)

        def add(j, carry):
            total = self.pack[pl.ds(start + j * block, block)].astype(f32)
            for turn in range(1, self.stages[i][2]):
                total = total + self.landing[i][turn - 1, pl.ds(j * block, block)].astype(f32)
            into[pl.ds(start + j * block, block)] = total.astype(bf16)
            return carry

        lax.fori_loop(0, length // block, add, 0)

    def spread(self, i):
        for copy in self._gather(i):
            copy.start()

    def settle(self, i):
        for copy in self._gather(i):
            copy.wait()


def sum_scratch(stages, units):
    shapes, left = [], units
    for stage in stages:
        left //= stage[2]
        shapes.append(pltpu.VMEM((stage[2] - 1, left, 16, 128), bf16))
    copies = 2 * sum(s[2] - 1 for s in stages)
    return shapes + [pltpu.SemaphoreType.DMA((copies,)), pltpu.SemaphoreType.DMA((copies,))]


def pack_matrix(pack, first, value):
    rows, cols = value.shape
    tiles = rows // 16
    for c in range(cols // 128):
        pack[first + c * tiles : first + (c + 1) * tiles] = (
            value[:, 128 * c : 128 * (c + 1)].astype(bf16).reshape(tiles, 16, 128)
        )
    return first + cols // 128 * tiles


def pack_rows(pack, first, vectors):
    rows = [v[:, c : c + 128] for v in vectors for c in range(0, v.shape[1], 128)]
    rows += [jnp.zeros((1, 128), f32)] * (-len(rows) % 16)
    for r in range(0, len(rows), 16):
        pack[first + r // 16] = jnp.concatenate(rows[r : r + 16], axis=0).astype(bf16)
    last = first + len(rows) // 16
    if last < pack.shape[0]:
        pack[last:] = jnp.zeros((pack.shape[0] - last, 16, 128), bf16)


def unpack_matrix(res, first, rows, cols):
    tiles = rows // 16
    part = res[first : first + cols // 128 * tiles].reshape(cols // 128, tiles, 16, 128)
    return part.transpose(1, 2, 0, 3).reshape(rows, cols).astype(f32)


def units_for(needed, devices):
    return -(-needed // devices) * devices


def colsum(v):
    return jnp.sum(v, axis=0, keepdims=True)


def reduce_kernel(stages, pack_ref, res_ref, own_ref, sum_ref, *rest):
    total = Sum(stages, own_ref, sum_ref, rest[: len(stages)], *rest[len(stages) :])
    greet(stages)
    own_ref[...] = pack_ref[...]
    for i in range(len(stages)):
        total.send(i)
        total.take(i)
    for i in reversed(range(len(stages))):
        total.spread(i)
        total.settle(i)
    res_ref[...] = sum_ref[...]


def forward_kernel(
    clip_ref,
    x_ref,
    ghost_ref,
    cot_ref,
    g1_ref,
    s1_ref,
    wqkv_ref,
    bqkv_ref,
    wout_ref,
    bout_ref,
    g2_ref,
    s2_ref,
    w1_ref,
    b1_ref,
    w2_ref,
    b2_ref,
    q_ref,
    kv_ref,
    prob_ref,
    out_ref,
    gatt_ref,
    gres_ref,
    pack_ref,
    gw1_ref,
    gw2_ref,
    gwo_ref,
    sb1_ref,
    s384_ref,
):
    step = pl.program_id(0)
    steps = pl.num_programs(0)
    frames = 2 * steps
    width = x_ref.shape[-1]
    hidden = w1_ref.shape[-1]
    tm = lax.axis_index("tm")

    @pl.when(step == 0)
    def _():
        gw1_ref[...] = jnp.zeros_like(gw1_ref)
        gw2_ref[...] = jnp.zeros_like(gw2_ref)
        gwo_ref[...] = jnp.zeros_like(gwo_ref)
        sb1_ref[...] = jnp.zeros_like(sb1_ref)
        s384_ref[...] = jnp.zeros_like(s384_ref)
        gain = g1_ref[...].astype(f32)
        shift = s1_ref[...].astype(f32)
        bias = bqkv_ref[...]
        zero_slot = jnp.where(tm == 0, 0, frames + 1)
        ghost_slot = frames + 1 - zero_slot
        kv_ref[pl.ds(pl.multiple_of(zero_slot * ROWS, 16), ROWS), :] = jnp.zeros((ROWS, 2 * width), bf16)
        kv_ref[(frames + 2) * ROWS :, :] = jnp.zeros((WIN - 3 * ROWS, 2 * width), bf16)

        x = ghost_ref[...].astype(f32)
        n, _ = normed_of(x)
        kv = mm((n * gain + shift).astype(bf16), wqkv_ref[:, width:]) + bias[:, width:]
        kv_ref[pl.ds(pl.multiple_of(ghost_slot * ROWS, 16), ROWS), :] = kv.astype(bf16)

        def project(i, carry):
            x = x_ref[pl.ds(2 * i, 2)].reshape(2 * ROWS, width).astype(f32)
            n, _ = normed_of(x)
            qkv = (mm((n * gain + shift).astype(bf16), wqkv_ref[...]) + bias).astype(bf16)
            q_ref[pl.ds(2 * i, 2)] = qkv[:, :width].reshape(2, ROWS, width)
            kv_ref[pl.ds(pl.multiple_of((2 * i + 1) * ROWS, 16), 2 * ROWS), :] = qkv[:, width:]
            return carry

        lax.fori_loop(0, frames // 2, project, 0)

    lane = lax.broadcasted_iota(jnp.int32, (ROWS, 128), 1)
    low_half = lane < 64
    col = lax.broadcasted_iota(jnp.int32, (1, WIN), 1)
    scale = LOG2E / math.sqrt(width // HEADS)
    attended = []
    for sub in range(2):
        frame = 2 * step + sub
        here = tm * frames + frame
        own = clip_ref[here]
        before = jnp.where(here > 0, clip_ref[jnp.maximum(here - 1, 0)], -1)
        after = jnp.where(here < 2 * frames - 1, clip_ref[jnp.minimum(here + 1, 2 * frames - 1)], -1)
        lo = jnp.where(before == own, 0, ROWS)
        hi = jnp.where(after == own, 3 * ROWS, 2 * ROWS)
        slot = col // ROWS
        live = (col >= lo) & (col < hi) & (col - slot * ROWS < FRAME)
        mask = jnp.where(live, 0.0, -1e30).astype(f32)
        window = pl.ds(pl.multiple_of(frame * ROWS, 16), WIN)
        for pair in range(HEADS // 2):
            q = q_ref[frame, :, 128 * pair : 128 * pair + 128]
            k = kv_ref[window, 128 * pair : 128 * pair + 128]
            v = kv_ref[window, width + 128 * pair : width + 128 * pair + 128]
            parts = []
            for half in range(2):
                mine = low_half if half == 0 else ~low_half
                s = mm_nt(jnp.where(mine, q, jnp.zeros_like(q)), k) + mask
                top = jnp.max(s, axis=-1, keepdims=True)
                e = jnp.exp2((s - top) * scale)
                total = jnp.sum(e, axis=-1, keepdims=True)
                prob = (e * (1.0 / total)).astype(bf16)
                prob_ref[sub, 2 * pair + half] = prob
                parts.append(mm(prob, v))
            attended.append(jnp.where(low_half, parts[0], parts[1]).astype(bf16))
    att = jnp.concatenate(
        [
            jnp.concatenate([attended[p], attended[HEADS // 2 + p]], axis=0)
            for p in range(HEADS // 2)
        ],
        axis=1,
    )
    x = x_ref[pl.ds(2 * step, 2)].reshape(2 * ROWS, width).astype(f32)
    resid = x + mm(att, wout_ref[...]) + bout_ref[...].astype(f32)
    n2, inv2 = normed_of(resid)
    mlp_in = (n2 * g2_ref[...].astype(f32) + s2_ref[...].astype(f32)).astype(bf16)
    cot = cot_ref[...].reshape(2 * ROWS, width)
    out = resid + b2_ref[...].astype(f32)
    up = jnp.zeros((2 * ROWS, width), f32)
    chunk = 512
    for c in range(hidden // chunk):
        cols = slice(c * chunk, (c + 1) * chunk)
        pre = mm(mlp_in, w1_ref[:, cols]) + b1_ref[:, cols].astype(f32)
        cdf = 0.5 * (1.0 + lax.erf(pre * (1.0 / math.sqrt(2.0))))
        hid = (pre * cdf).astype(bf16)
        dens = jnp.exp2(pre * pre * (-0.5 * LOG2E)) * (1.0 / math.sqrt(2.0 * math.pi))
        out = out + mm(hid, w2_ref[cols, :])
        gw2_ref[:, cols] += mm_tn(cot, hid)
        gpre32 = mm_nt(cot, w2_ref[cols, :]) * (cdf + pre * dens)
        gpre = gpre32.astype(bf16)
        sb1_ref[:, cols] += fold8(gpre.astype(f32))
        gw1_ref[:, cols] += mm_tn(mlp_in, gpre)
        up = up + mm_nt(gpre, w1_ref[:, cols])
    out_ref[...] = out.astype(bf16).reshape(2, ROWS, width)
    cot32 = cot.astype(f32)
    gres = cot32 + norm_back(up, n2, inv2, g2_ref[...].astype(f32))
    gres_ref[...] = gres.reshape(2, ROWS, width)
    branch = gres.astype(bf16)
    gwo_ref[...] += mm_tn(att, branch)
    gatt_ref[...] = mm_nt(branch, wout_ref[...]).astype(bf16).reshape(2, ROWS, width)
    s384_ref[0] += fold8(up * n2)
    s384_ref[1] += fold8(up)
    s384_ref[2] += fold8(branch.astype(f32))
    s384_ref[3] += fold8(cot32)

    @pl.when(step == steps - 1)
    def _():
        at = pack_matrix(pack_ref, 0, gw1_ref[...])
        at = pack_matrix(pack_ref, at, gw2_ref[...])
        at = pack_matrix(pack_ref, at, gwo_ref[...])
        pack_rows(pack_ref, at, [colsum(s384_ref[i]) for i in range(4)] + [colsum(sb1_ref[...])])


def back_kernel(stages, q_ref, kv_ref, prob_ref, gatt_ref, pack_ref, dq_ref, dkv_ref, edge_ref, res_ref,
                acc_ref, own_ref, sum_ref, *rest):
    step = pl.program_id(0)
    steps = pl.num_programs(0)
    frames = 2 * steps
    width = q_ref.shape[-1]
    tm = lax.axis_index("tm")
    inv_scale = 1.0 / math.sqrt(width // HEADS)
    total = Sum(stages, own_ref, sum_ref, rest[: len(stages)], *rest[len(stages) :])
    last = len(stages) - 1

    @pl.when(step == 0)
    def _():
        own_ref[...] = pack_ref[...]
        greet(stages)
        total.send(0)
        acc_ref[...] = jnp.zeros_like(acc_ref)

    def at(when, *todo):
        @pl.when(step == when)
        def _():
            for act, i in todo:
                act(i)

    at(1, (total.take, 0), (total.send, 1))
    if len(stages) == 3:
        at(3, (total.take, 1), (total.send, 2))
        at(4, (total.take, 2), (total.spread, 2))
        at(5, (total.settle, 2), (total.spread, 1))
        at(7, (total.settle, 1), (total.spread, 0))
    else:
        at(3, *[t for i in range(1, last) for t in ((total.take, i), (total.send, i + 1))])
        at(5, (total.take, last), (total.spread, last))
        at(7, *[t for i in range(last, 0, -1) for t in ((total.settle, i), (total.spread, i - 1))])

    lane = lax.broadcasted_iota(jnp.int32, (ROWS, 128), 1)
    low_half = lane < 64
    for sub in range(2):
        frame = 2 * step + sub
        window = pl.ds(pl.multiple_of(frame * ROWS, 16), WIN)
        for pair in range(HEADS // 2):
            cols = slice(128 * pair, 128 * pair + 128)
            vcols = slice(width + 128 * pair, width + 128 * pair + 128)
            q = q_ref[sub, :, cols]
            g = gatt_ref[sub, :, cols]
            k = kv_ref[window, cols]
            v = kv_ref[window, vcols]
            dq, dk, dv = [], 0.0, 0.0
            for half in range(2):
                mine = low_half if half == 0 else ~low_half
                gm = jnp.where(mine, g, jnp.zeros_like(g))
                qm = jnp.where(mine, q, jnp.zeros_like(q))
                prob_bf = prob_ref[sub, 2 * pair + half]
                prob = prob_bf.astype(f32)
                dp = mm_nt(gm, v)
                dot = jnp.sum(prob * dp, axis=-1, keepdims=True)
                ds = (prob * (dp - dot)).astype(bf16)
                dq.append(mm(ds, k))
                dk = dk + mm_tn(ds, qm)
                dv = dv + mm_tn(prob_bf, gm)
            dq_ref[sub, :, cols] = (jnp.where(low_half, dq[0], dq[1]) * inv_scale).astype(bf16)
            acc_ref[window, cols] += dk
            acc_ref[window, vcols] += dv

    @pl.when(step == steps - 1)
    def _():
        def finish(i, carry):
            rows = pl.ds(pl.multiple_of((i + 1) * ROWS, 16), ROWS)
            dkv_ref[i, :, :width] = (acc_ref[rows, :width] * inv_scale).astype(bf16)
            dkv_ref[i, :, width:] = acc_ref[rows, width:].astype(bf16)
            return carry

        lax.fori_loop(0, frames, finish, 0)
        own = pl.ds(pl.multiple_of(jnp.where(tm == 0, frames, 1) * ROWS, 16), ROWS)
        ghost = pl.ds(pl.multiple_of(jnp.where(tm == 0, frames + 1, 0) * ROWS, 16), ROWS)
        edge_ref[0, :, :width] = acc_ref[own, :width] * inv_scale
        edge_ref[0, :, width:] = acc_ref[own, width:]
        edge_ref[1, :, :width] = acc_ref[ghost, :width] * inv_scale
        edge_ref[1, :, width:] = acc_ref[ghost, width:]
        total.settle(0)
        res_ref[...] = sum_ref[...]


def input_kernel(x_ref, dq_ref, dkv_ref, edge_ref, got_ref, gres_ref, g1_ref, s1_ref, wqkv_ref,
                 out_ref, pack_ref, gw_ref, sq_ref, s384_ref):
    step = pl.program_id(0)
    steps = pl.num_programs(0)
    frames = 2 * steps
    width = x_ref.shape[-1]
    tm = lax.axis_index("tm")

    @pl.when(step == 0)
    def _():
        gw_ref[...] = jnp.zeros_like(gw_ref)
        sq_ref[...] = jnp.zeros_like(sq_ref)
        s384_ref[...] = jnp.zeros_like(s384_ref)

    edge_frame = jnp.where(tm == 0, frames - 1, 0)

    @pl.when(step == edge_frame // 2)
    def _():
        dkv_ref[edge_frame % 2] = (edge_ref[0] + got_ref[...].astype(f32)).astype(bf16)

    x = x_ref[...].reshape(2 * ROWS, width).astype(f32)
    n, inv = normed_of(x)
    gain = g1_ref[...].astype(f32)
    attn_in = (n * gain + s1_ref[...].astype(f32)).astype(bf16)
    dq = dq_ref[...].reshape(2 * ROWS, width)
    dkv = dkv_ref[...].reshape(2 * ROWS, 2 * width)
    gw_ref[:, :width] += mm_tn(attn_in, dq)
    gw_ref[:, width:] += mm_tn(attn_in, dkv)
    sq_ref[:, :width] += fold8(dq.astype(f32))
    sq_ref[:, width:] += fold8(dkv[:, width:].astype(f32))
    up = mm_nt(dq, wqkv_ref[:, :width]) + mm_nt(dkv, wqkv_ref[:, width:])
    gres = gres_ref[...].reshape(2 * ROWS, width)
    out_ref[...] = (gres + norm_back(up, n, inv, gain)).reshape(2, ROWS, width)
    s384_ref[0] += fold8(up * n)
    s384_ref[1] += fold8(up)

    @pl.when(step == steps - 1)
    def _():
        at = pack_matrix(pack_ref, 0, gw_ref[...])
        sq = colsum(sq_ref[...])
        pack_rows(pack_ref, at, [colsum(s384_ref[0]), colsum(s384_ref[1]), sq])


def whole(shape):
    return pl.BlockSpec(shape, lambda i: (0,) * len(shape), pipeline_mode=pl.Buffered(1))


def pairs(shape):
    return pl.BlockSpec((2,) + shape, lambda i: (i,) + (0,) * len(shape))


def params(collective=None):
    if collective is None:
        return pltpu.CompilerParams(vmem_limit_bytes=60 * 2**20)
    return pltpu.CompilerParams(vmem_limit_bytes=60 * 2**20, collective_id=collective, has_side_effects=True)


def per_device(tokens, frame_clip, ln1_gain, ln1_bias, w_qkv, qv_bias, w_out, b_out, ln2_gain, ln2_bias,
               w_fc1, b_fc1, w_fc2, b_fc2, cotangent):
    count, width = tokens.shape
    hidden = w_fc1.shape[1]
    frames = count // FRAME
    steps = frames // 2
    tm = lax.axis_index("tm")
    pad = ((0, 0), (0, ROWS - FRAME), (0, 0))
    x_pad = jnp.pad(tokens.reshape(frames, FRAME, width), pad)
    cot_pad = jnp.pad(cotangent.reshape(frames, FRAME, width), pad)
    edge = jnp.where(tm == 0, tokens[count - FRAME :], tokens[:FRAME])
    ghost = jnp.pad(lax.ppermute(edge, "tm", [(0, 1), (1, 0)]), pad[1:])
    row = lambda v: v.reshape(1, -1)
    bias_qkv = jnp.concatenate([qv_bias[0], jnp.zeros((width,), bf16), qv_bias[1]]).astype(f32)
    kv_rows = (frames + 2) * ROWS + WIN - 3 * ROWS
    shape = jax.ShapeDtypeStruct
    stages = stages_of(lax.axis_size("clips"))
    devices = 2 * lax.axis_size("clips")
    tiles = width // 16
    units = units_for((2 * hidden + width) // 128 * tiles + 2, devices)
    units2 = units_for(3 * width // 128 * tiles + 1, devices)
    q, kv, prob, out_pad, gatt, gres, pack = pl.pallas_call(
        forward_kernel,
        grid=(steps,),
        in_specs=[
            pl.BlockSpec(memory_space=pltpu.SMEM),
            whole((frames, ROWS, width)),
            whole((ROWS, width)),
            pairs((ROWS, width)),
            whole((1, width)),
            whole((1, width)),
            whole((width, 3 * width)),
            whole((1, 3 * width)),
            whole((width, width)),
            whole((1, width)),
            whole((1, width)),
            whole((1, width)),
            whole((width, hidden)),
            whole((1, hidden)),
            whole((hidden, width)),
            whole((1, width)),
        ],
        out_specs=[
            whole((frames, ROWS, width)),
            whole((kv_rows, 2 * width)),
            pairs((HEADS, ROWS, WIN)),
            pairs((ROWS, width)),
            pairs((ROWS, width)),
            pairs((ROWS, width)),
            whole((units, 16, 128)),
        ],
        out_shape=[
            shape((frames, ROWS, width), bf16),
            shape((kv_rows, 2 * width), bf16),
            shape((frames, HEADS, ROWS, WIN), bf16),
            shape((frames, ROWS, width), bf16),
            shape((frames, ROWS, width), bf16),
            shape((frames, ROWS, width), f32),
            shape((units, 16, 128), bf16),
        ],
        scratch_shapes=[
            pltpu.VMEM((width, hidden), f32),
            pltpu.VMEM((width, hidden), f32),
            pltpu.VMEM((width, width), f32),
            pltpu.VMEM((8, hidden), f32),
            pltpu.VMEM((4, 8, width), f32),
        ],
        compiler_params=params(),
    )(frame_clip, x_pad, ghost, cot_pad, row(ln1_gain), row(ln1_bias), w_qkv, row(bias_qkv), w_out, row(b_out),
      row(ln2_gain), row(ln2_bias), w_fc1, row(b_fc1), w_fc2, row(b_fc2))

    dq, dkv, edges, res = pl.pallas_call(
        functools.partial(back_kernel, stages),
        grid=(steps,),
        in_specs=[
            pairs((ROWS, width)),
            whole((kv_rows, 2 * width)),
            pairs((HEADS, ROWS, WIN)),
            pairs((ROWS, width)),
            whole((units, 16, 128)),
        ],
        out_specs=[
            pairs((ROWS, width)),
            whole((frames, ROWS, 2 * width)),
            whole((2, ROWS, 2 * width)),
            whole((units, 16, 128)),
        ],
        out_shape=[
            shape((frames, ROWS, width), bf16),
            shape((frames, ROWS, 2 * width), bf16),
            shape((2, ROWS, 2 * width), f32),
            shape((units, 16, 128), bf16),
        ],
        scratch_shapes=[pltpu.VMEM((kv_rows, 2 * width), f32), pltpu.VMEM((units, 16, 128), bf16), pltpu.VMEM((units, 16, 128), bf16)]
        + sum_scratch(stages, units),
        compiler_params=params(0),
    )(q, kv, prob, gatt, pack)

    got = lax.ppermute(edges[1].astype(bf16), "tm", [(0, 1), (1, 0)])

    in_pad, pack2 = pl.pallas_call(
        input_kernel,
        grid=(steps,),
        in_specs=[
            pairs((ROWS, width)),
            pairs((ROWS, width)),
            pairs((ROWS, 2 * width)),
            whole((2, ROWS, 2 * width)),
            whole((ROWS, 2 * width)),
            pairs((ROWS, width)),
            whole((1, width)),
            whole((1, width)),
            whole((width, 3 * width)),
        ],
        out_specs=[
            pairs((ROWS, width)),
            whole((units2, 16, 128)),
        ],
        out_shape=[
            shape((frames, ROWS, width), f32),
            shape((units2, 16, 128), bf16),
        ],
        scratch_shapes=[
            pltpu.VMEM((width, 3 * width), f32),
            pltpu.VMEM((8, 2 * width), f32),
            pltpu.VMEM((2, 8, width), f32),
        ],
        compiler_params=params(),
    )(x_pad, dq, dkv, edges, got, gres, row(ln1_gain), row(ln1_bias), w_qkv)

    in_vmem = pl.BlockSpec(memory_space=pltpu.VMEM)
    res2 = pl.pallas_call(
        functools.partial(reduce_kernel, stages),
        in_specs=[in_vmem],
        out_specs=in_vmem,
        out_shape=shape((units2, 16, 128), bf16),
        scratch_shapes=[pltpu.VMEM((units2, 16, 128), bf16)] * 2 + sum_scratch(stages, units2),
        compiler_params=params(1),
    )(pack2)

    block_out = out_pad[:, :FRAME].reshape(count, width)
    input_grad = in_pad[:, :FRAME].reshape(count, width)
    across = hidden // 128 * tiles
    gw1 = unpack_matrix(res, 0, width, hidden)
    gw2 = unpack_matrix(res, across, width, hidden).T
    gwo = unpack_matrix(res, 2 * across, width, width)
    vec = res[2 * across + width // 128 * tiles :][:2].reshape(-1).astype(f32)
    gwqkv = unpack_matrix(res2, 0, width, 3 * width)
    vec2 = res2[3 * width // 128 * tiles].reshape(-1).astype(f32)
    two = lambda i: vec[i * width : (i + 1) * width]
    one = lambda i: vec2[i * width : (i + 1) * width]
    return (block_out, input_grad, one(0), one(1), gwqkv, vec2[2 * width : 4 * width].reshape(2, width), gwo, two(2),
            two(0), two(1), gw1, vec[4 * width : 4 * width + hidden], gw2, two(3))


def solution(mesh):
    rows = P(("clips", "tm"), None)
    rep = P()
    return jax.shard_map(
        per_device,
        mesh=mesh,
        in_specs=(rows, P("clips")) + (rep,) * 12 + (rows,),
        out_specs=(rows, rows) + (rep,) * 12,
        check_vma=False,
    )
```

```python
import functools
import math

import jax
import jax.numpy as jnp
from jax import lax
from jax.experimental import pallas as pl
from jax.experimental.pallas import tpu as pltpu
from jax.sharding import PartitionSpec as P

HEADS = 6
FRAME = 196
ROWS = 208
WIN = 640
EPS = 1e-6
LOG2E = math.log2(math.e)

bf16 = jnp.bfloat16
f32 = jnp.float32


def mm(a, b):
    return jnp.dot(a, b, preferred_element_type=f32)


def mm_nt(a, b):
    return lax.dot_general(a, b, (((1,), (1,)), ((), ())), preferred_element_type=f32)


def mm_tn(a, b):
    return lax.dot_general(a, b, (((0,), (0,)), ((), ())), preferred_element_type=f32)


def normed_of(x):
    mean = jnp.mean(x, axis=-1, keepdims=True)
    centred = x - mean
    var = jnp.mean(centred * centred, axis=-1, keepdims=True)
    inverse = lax.rsqrt(var + EPS)
    return centred * inverse, inverse


def norm_back(upstream, normed, inverse, gain):
    scaled = upstream * gain
    mean = jnp.mean(scaled, axis=-1, keepdims=True)
    along = jnp.mean(scaled * normed, axis=-1, keepdims=True)
    return inverse * (scaled - mean - normed * along)


def fold8(v):
    rows, cols = v.shape
    return jnp.sum(v.reshape(rows // 8, 8, cols), axis=0)


MESH = pl.DeviceIdType.MESH


def stages_of(clips):
    stages, stride = [("tm", 1, 2)], 1
    while clips > 1:
        size = 4 if clips % 4 == 0 else (2 if clips % 2 == 0 else clips)
        stages.append(("clips", stride, size))
        stride, clips = stride * size, clips // size
    return stages


def digit(stage):
    axis, stride, size = stage
    return lax.rem(lax.axis_index(axis) // stride, size)


def partner(stage, turn):
    axis, stride, size = stage
    mine = digit(stage)
    return {axis: lax.axis_index(axis) + (lax.rem(mine + turn, size) - mine) * stride}


def greet(stages):
    sem, count = pltpu.get_barrier_semaphore(), 0
    for stage in stages:
        for turn in range(1, stage[2]):
            pl.semaphore_signal(sem, inc=1, device_id=partner(stage, turn), device_id_type=MESH)
            count += 1
    pl.semaphore_wait(sem, count)


class Sum:
    def __init__(self, stages, pack, result, landing, sent, came):
        self.stages, self.pack, self.result, self.landing = stages, pack, result, landing
        self.sent, self.came = sent, came
        self.segments, start, length = [], 0, pack.shape[0]
        for stage in stages:
            self.segments.append((start, length))
            length = length // stage[2]
            start = start + digit(stage) * length
        self.segments.append((start, length))
        self.first = [sum(s[2] - 1 for s in stages[:i]) for i in range(len(stages) + 1)]

    def _scatter(self, i):
        stage, (start, length) = self.stages[i], self.segments[i]
        part = length // stage[2]
        for turn in range(1, stage[2]):
            slot = self.first[i] + turn - 1
            other = lax.rem(digit(stage) + turn, stage[2])
            yield pltpu.make_async_remote_copy(
                src_ref=self.pack.at[pl.ds(start + other * part, part)],
                dst_ref=self.landing[i].at[turn - 1],
                send_sem=self.sent.at[slot],
                recv_sem=self.came.at[slot],
                device_id=partner(stage, turn),
                device_id_type=MESH,
            )

    def _gather(self, i):
        stage, (start, length) = self.stages[i], self.segments[i + 1]
        for turn in range(1, stage[2]):
            slot = self.first[-1] + self.first[i] + turn - 1
            here = self.result.at[pl.ds(start, length)]
            yield pltpu.make_async_remote_copy(
                src_ref=here,
                dst_ref=here,
                send_sem=self.sent.at[slot],
                recv_sem=self.came.at[slot],
                device_id=partner(stage, turn),
                device_id_type=MESH,
            )

    def send(self, i):
        for copy in self._scatter(i):
            copy.start()

    def take(self, i):
        for copy in self._scatter(i):
            copy.wait()
        start, length = self.segments[i + 1]
        into = self.result if i == len(self.stages) - 1 else self.pack
        block = next(b for b in (28, 24, 21, 16, 14, 12, 8, 7, 6, 4, 3, 2, 1) if length % b == 0)

        def add(j, carry):
            total = self.pack[pl.ds(start + j * block, block)].astype(f32)
            for turn in range(1, self.stages[i][2]):
                total = total + self.landing[i][turn - 1, pl.ds(j * block, block)].astype(f32)
            into[pl.ds(start + j * block, block)] = total.astype(bf16)
            return carry

        lax.fori_loop(0, length // block, add, 0)

    def spread(self, i):
        for copy in self._gather(i):
            copy.start()

    def settle(self, i):
        for copy in self._gather(i):
            copy.wait()


def sum_scratch(stages, units):
    shapes, left = [], units
    for stage in stages:
        left //= stage[2]
        shapes.append(pltpu.VMEM((stage[2] - 1, left, 16, 128), bf16))
    copies = 2 * sum(s[2] - 1 for s in stages)
    return shapes + [pltpu.SemaphoreType.DMA((copies,)), pltpu.SemaphoreType.DMA((copies,))]


def pack_matrix(pack, first, value):
    rows, cols = value.shape
    tiles = rows // 16
    for c in range(cols // 128):
        pack[first + c * tiles : first + (c + 1) * tiles] = (
            value[:, 128 * c : 128 * (c + 1)].astype(bf16).reshape(tiles, 16, 128)
        )
    return first + cols // 128 * tiles


def pack_rows(pack, first, vectors):
    rows = [v[:, c : c + 128] for v in vectors for c in range(0, v.shape[1], 128)]
    rows += [jnp.zeros((1, 128), f32)] * (-len(rows) % 16)
    for r in range(0, len(rows), 16):
        pack[first + r // 16] = jnp.concatenate(rows[r : r + 16], axis=0).astype(bf16)
    last = first + len(rows) // 16
    if last < pack.shape[0]:
        pack[last:] = jnp.zeros((pack.shape[0] - last, 16, 128), bf16)


def unpack_matrix(res, first, rows, cols):
    tiles = rows // 16
    part = res[first : first + cols // 128 * tiles].reshape(cols // 128, tiles, 16, 128)
    return part.transpose(1, 2, 0, 3).reshape(rows, cols).astype(f32)


def units_for(needed, devices):
    return -(-needed // devices) * devices


def colsum(v):
    return jnp.sum(v, axis=0, keepdims=True)


def widen(ref, group, which):
    start = which * FRAME // 16 * 16
    shift = which * FRAME - start
    v = ref[pl.ds(pl.multiple_of(group * 4 * FRAME + start, 16), ROWS), :].astype(f32)
    if shift:
        v = pltpu.roll(v, ROWS - shift, 0)
    row = lax.broadcasted_iota(jnp.int32, (16, v.shape[1]), 0)
    return v, jnp.where(row < 16 - (ROWS - FRAME), v[ROWS - 16 :], 0.0)


def narrow_into(ref, start, v):
    edge = FRAME // 8 * 8
    over = FRAME - edge
    second = pltpu.roll(v[ROWS:], over, 0)
    row = lax.broadcasted_iota(jnp.int32, (8, v.shape[1]), 0)
    ref[pl.ds(pl.multiple_of(start, 8), edge), :] = v[:edge]
    ref[pl.ds(pl.multiple_of(start + edge, 8), 8), :] = jnp.where(row < over, v[edge : edge + 8], second[:8])
    rest = 2 * FRAME - edge - 8
    ref[pl.ds(pl.multiple_of(start + edge + 8, 8), rest), :] = second[8 : 8 + rest]


def forward_kernel(
    clip_ref,
    tok_ref,
    ghost_ref,
    cot_ref,
    row_ref,
    wqkv_ref,
    wout_ref,
    w1_ref,
    w2_ref,
    x_ref,
    kv_ref,
    prob_ref,
    out_ref,
    qs_ref,
    ga_ref,
    gs_ref,
    gres_ref,
    li_ref,
    pack_ref,
    q_ref,
    cp_ref,
    flag_ref,
    s_ref,
    o_ref,
    flat_ref,
    gw1_ref,
    gw2_ref,
    gwo_ref,
    sb1_ref,
    s384_ref,
):
    step = pl.program_id(0)
    steps = pl.num_programs(0)
    frames = 2 * steps
    width = x_ref.shape[-1]
    hidden = w1_ref.shape[-1]
    tm = lax.axis_index("tm")
    vec = lambda i, n=width: row_ref[:, i * width : i * width + n]
    gain1, shift1, bias3, biaso, gain2, shift2, bias2, bias1 = (
        vec(0), vec(1), vec(2, 3 * width), vec(5), vec(6), vec(7), vec(8), vec(9, hidden))

    @pl.when(step == 0)
    def _():
        gw1_ref[...] = jnp.zeros_like(gw1_ref)
        gw2_ref[...] = jnp.zeros_like(gw2_ref)
        gwo_ref[...] = jnp.zeros_like(gwo_ref)
        sb1_ref[...] = jnp.zeros_like(sb1_ref)
        s384_ref[...] = jnp.zeros_like(s384_ref)
        at = lax.broadcasted_iota(jnp.int32, flag_ref.shape, 0)
        lane = lax.broadcasted_iota(jnp.int32, flag_ref.shape, 1) % 64
        slot = at // ROWS
        flag_ref[...] = jnp.where(
            lane == 0,
            jnp.where(at - slot * ROWS < FRAME, 0.0, -1e30),
            jnp.where(lane == 1 + slot % 4, 1.0, 0.0),
        ).astype(bf16)
        zero_slot = jnp.where(tm == 0, 0, frames + 1)
        ghost_slot = frames + 1 - zero_slot
        kv_ref[pl.ds(pl.multiple_of(zero_slot * ROWS, 16), ROWS), :] = jnp.zeros((ROWS, 2 * width), bf16)
        kv_ref[(frames + 2) * ROWS :, :] = jnp.zeros((WIN - 3 * ROWS, 2 * width), bf16)

        x = ghost_ref[...].astype(f32)
        n, _ = normed_of(x)
        kv = mm((n * gain1 + shift1).astype(bf16), wqkv_ref[:, width:]) + bias3[:, width:]
        kv_ref[pl.ds(pl.multiple_of(ghost_slot * ROWS, 16), ROWS), :] = kv.astype(bf16)

        def pad(i, carry):
            for which in range(4):
                for src, dst in ((tok_ref, x_ref), (cot_ref, cp_ref)):
                    v, end = widen(src, i, which)
                    dst[4 * i + which, : ROWS - 16] = v[: ROWS - 16].astype(bf16)
                    dst[4 * i + which, ROWS - 16 :] = end.astype(bf16)
            return carry

        lax.fori_loop(0, frames // 4, pad, 0)

        def project(i, carry):
            x = x_ref[pl.ds(2 * i, 2)].reshape(2 * ROWS, width).astype(f32)
            n, _ = normed_of(x)
            qkv = (mm((n * gain1 + shift1).astype(bf16), wqkv_ref[...]) + bias3).astype(bf16)
            q_ref[pl.ds(2 * i, 2)] = qkv[:, :width].reshape(2, ROWS, width)
            kv_ref[pl.ds(pl.multiple_of((2 * i + 1) * ROWS, 16), 2 * ROWS), :] = qkv[:, width:]
            return carry

        lax.fori_loop(0, frames // 2, project, 0)

    low = lax.broadcasted_iota(jnp.int32, (ROWS, 128), 1) < 64
    wide_low = lax.broadcasted_iota(jnp.int32, (WIN, 128), 1) < 64
    lane = lax.broadcasted_iota(jnp.int32, (1, 128), 1) % 64
    ones = jnp.ones((WIN, 128), bf16)
    scale = LOG2E / math.sqrt(width // HEADS)
    flags, windows = [], []
    for sub in range(2):
        frame = 2 * step + sub
        here = tm * frames + frame
        own = clip_ref[here]
        before = jnp.where(here > 0, clip_ref[jnp.maximum(here - 1, 0)], -1)
        after = jnp.where(here < 2 * frames - 1, clip_ref[jnp.minimum(here + 1, 2 * frames - 1)], -1)
        none = jnp.float32(-1e30)
        row = jnp.where(lane == 0, 1.0, 0.0)
        row = jnp.where(lane == 1 + frame % 4, jnp.where(before == own, 0.0, none), row)
        row = jnp.where(lane == 1 + (frame + 2) % 4, jnp.where(after == own, 0.0, none), row)
        row = jnp.where(lane == 1 + (frame + 3) % 4, none, row)
        flags.append(jnp.broadcast_to(row.astype(bf16), (ROWS, 128)))
        windows.append(pl.ds(pl.multiple_of(frame * ROWS, 16), WIN))

    def score(t):
        sub, h = divmod(t, HEADS)
        cols = slice(h // 2 * 128, h // 2 * 128 + 128)
        mine, wide = (low, wide_low) if h % 2 == 0 else (~low, ~wide_low)
        q = jnp.where(mine, q_ref[2 * step + sub, :, cols], flags[sub])
        k = jnp.where(wide, kv_ref[windows[sub], cols], flag_ref[windows[sub], :])
        s_ref[t % 3] = mm_nt(q, k)

    def soften(t):
        sub, h = divmod(t, HEADS)
        s = s_ref[t % 3]
        top = jnp.max(s, axis=-1, keepdims=True)
        prob_ref[sub, h] = jnp.exp2((s - top) * scale).astype(bf16)

    parts = {}

    def attend(t):
        sub, h = divmod(t, HEADS)
        at = h // 2 * 128
        wide = wide_low if h % 2 == 0 else ~wide_low
        v = jnp.where(wide, kv_ref[windows[sub], width + at : width + at + 128], ones)
        parts[t] = mm(prob_ref[sub, h], v)
        if h % 2:
            even, odd = parts.pop(t - 1), parts.pop(t)
            total = pltpu.roll(jnp.where(low, odd, even), 64, 1)
            inverse = 1.0 / total
            rows = slice(sub * ROWS, (sub + 1) * ROWS)
            o_ref[rows, at : at + 128] = jnp.where(low, even, odd) * inverse
            li_ref[sub, :, at : at + 128] = inverse

    score(0)
    for t in range(2 * HEADS + 1):
        if t + 1 < 2 * HEADS:
            score(t + 1)
        if t >= 1:
            attend(t - 1)
        if t < 2 * HEADS:
            soften(t)

    att = o_ref[...].astype(bf16)
    both = pl.ds(2 * step, 2)
    x = x_ref[both].reshape(2 * ROWS, width).astype(f32)
    resid = x + mm(att, wout_ref[...]) + biaso
    n2, inv2 = normed_of(resid)
    mlp_in = (n2 * gain2 + shift2).astype(bf16)
    cot = cp_ref[both].reshape(2 * ROWS, width)
    out = resid + bias2
    up = jnp.zeros((2 * ROWS, width), f32)
    chunk = 768
    for c in range(hidden // chunk):
        cols = slice(c * chunk, (c + 1) * chunk)
        pre = mm(mlp_in, w1_ref[:, cols]) + bias1[:, cols]
        cdf = 0.5 * (1.0 + lax.erf(pre * (1.0 / math.sqrt(2.0))))
        hid = (pre * cdf).astype(bf16)
        dens = jnp.exp2(pre * pre * (-0.5 * LOG2E)) * (1.0 / math.sqrt(2.0 * math.pi))
        out = out + mm(hid, w2_ref[cols, :])
        gw2_ref[:, cols] += mm_tn(cot, hid)
        gpre = (mm_nt(cot, w2_ref[cols, :]) * (cdf + pre * dens)).astype(bf16)
        sb1_ref[:, cols] += fold8(gpre.astype(f32))
        gw1_ref[:, cols] += mm_tn(mlp_in, gpre)
        up = up + mm_nt(gpre, w1_ref[:, cols])
    narrow_into(flat_ref, step % 2 * 2 * FRAME, out)

    @pl.when(step % 2 == 1)
    def _():
        out_ref[...] = flat_ref[...].astype(bf16)

    cot32 = cot.astype(f32)
    gres = cot32 + norm_back(up, n2, inv2, gain2)
    gres_ref[...] = gres.reshape(2, ROWS, width)
    branch = gres.astype(bf16)
    gwo_ref[...] += mm_tn(att, branch)
    g = mm_nt(branch, wout_ref[...]).astype(bf16)
    g32 = g.astype(f32)
    inverse = li_ref[...].reshape(2 * ROWS, width)
    gs_ref[...] = (g32 * inverse).astype(bf16).reshape(2, ROWS, width)
    qs_ref[...] = (q_ref[both].reshape(2 * ROWS, width).astype(f32) * inverse).astype(bf16).reshape(2, ROWS, width)
    dots = g32 * o_ref[...]
    low2 = lax.broadcasted_iota(jnp.int32, (2 * ROWS, 128), 1) < 64
    for pair in range(HEADS // 2):
        cols = slice(128 * pair, 128 * pair + 128)
        d = dots[:, cols]
        even = jnp.sum(jnp.where(low2, d, 0.0), axis=-1, keepdims=True)
        odd = jnp.sum(jnp.where(low2, 0.0, d), axis=-1, keepdims=True)
        less = -jnp.where(low2, odd, even)
        one = less.astype(bf16)
        two = (less - one.astype(f32)).astype(bf16)
        three = (less - one.astype(f32) - two.astype(f32)).astype(bf16)
        zero = jnp.zeros_like(one)
        lanes = jnp.broadcast_to(lane, (2 * ROWS, 128))
        tail = jnp.where(lanes == 0, one, jnp.where(lanes == 1, two, jnp.where(lanes == 2, three, zero)))
        gp = g[:, cols]
        ga_ref[:, :, 256 * pair : 256 * pair + 128] = jnp.where(low2, gp, tail).reshape(2, ROWS, 128)
        ga_ref[:, :, 256 * pair + 128 : 256 * pair + 256] = jnp.where(low2, tail, gp).reshape(2, ROWS, 128)
    s384_ref[0] += fold8(up * n2)
    s384_ref[1] += fold8(up)
    s384_ref[2] += fold8(branch.astype(f32))
    s384_ref[3] += fold8(cot32)

    @pl.when(step == steps - 1)
    def _():
        at = pack_matrix(pack_ref, 0, gw1_ref[...])
        at = pack_matrix(pack_ref, at, gw2_ref[...])
        at = pack_matrix(pack_ref, at, gwo_ref[...])
        pack_rows(pack_ref, at, [colsum(s384_ref[i]) for i in range(4)] + [colsum(sb1_ref[...])])


class Rows:
    def __init__(self, stages, boards, sent, came):
        self.stages, self.boards, self.sent, self.came = stages, boards, sent, came
        self.first = [sum(s[2] - 1 for s in stages[:i]) for i in range(len(stages) + 1)]

    def _copies(self, i):
        stage = self.stages[i]
        here = self.boards[i].at[digit(stage)]
        for turn in range(1, stage[2]):
            slot = self.first[i] + turn - 1
            yield pltpu.make_async_remote_copy(
                src_ref=here,
                dst_ref=here,
                send_sem=self.sent.at[slot],
                recv_sem=self.came.at[slot],
                device_id=partner(stage, turn),
                device_id_type=MESH,
            )

    def spread(self, i, tile):
        self.boards[i][digit(self.stages[i])] = tile
        for copy in self._copies(i):
            copy.start()

    def settle(self, i):
        for copy in self._copies(i):
            copy.wait()
        total = self.boards[i][0]
        for j in range(1, self.stages[i][2]):
            total = total + self.boards[i][j]
        return total


def rows_scratch(stages):
    copies = sum(s[2] - 1 for s in stages)
    return [pltpu.VMEM((s[2], 16, 128), f32) for s in stages] + [pltpu.SemaphoreType.DMA((copies,))] * 2


def halves(units, devices):
    first = -(-units // (2 * devices)) * devices
    return first, units - first


def back_kernel(stages, prob_ref, kv_ref, ga_ref, gs_ref, qs_ref, li_ref, x_ref, gres_ref, gain_ref, shift_ref,
                wqkv_ref, pack_hbm, in_ref, res_ref, res2_ref, rows_ref,
                acc_ref, d_ref, ds_ref, dq_ref, gw_ref, sq_ref, s384_ref, own_ref, sum_ref, own2_ref, sum2_ref,
                ghost_ref, got_ref, ghost_sems, load_sem, *rest):
    step = pl.program_id(0)
    width = gs_ref.shape[-1]
    frames = x_ref.shape[0]
    steps = frames + 1 + frames // 2
    tm = lax.axis_index("tm")
    inv_scale = 1.0 / math.sqrt(width // HEADS)
    count = len(stages)
    last = count - 1
    devices = 2
    for stage in stages[1:]:
        devices *= stage[2]
    cut, _ = halves(own_ref.shape[0], devices)
    sums = []
    for n, (own, res) in enumerate(
        ((own_ref.at[:cut], sum_ref.at[:cut]), (own_ref.at[cut:], sum_ref.at[cut:]), (own2_ref, sum2_ref))
    ):
        mine = rest[n * (count + 2) : (n + 1) * (count + 2)]
        sums.append(Sum(stages, own, res, mine[:count], *mine[count:]))
    one, two, tail = sums
    extra = rest[3 * (count + 2) :]
    rows = Rows(stages, extra[:count], *extra[count:])
    load = pltpu.make_async_copy(pack_hbm, own_ref, load_sem)
    swap = pltpu.make_async_remote_copy(
        src_ref=ghost_ref,
        dst_ref=got_ref,
        send_sem=ghost_sems.at[0],
        recv_sem=ghost_sems.at[1],
        device_id=partner(stages[0], 1),
        device_id_type=MESH,
    )

    @pl.when(step == 0)
    def _():
        load.start()
        greet(stages)
        load.wait()
        one.send(0)
        two.send(0)
        acc_ref[...] = jnp.zeros_like(acc_ref)
        gw_ref[...] = jnp.zeros_like(gw_ref)
        sq_ref[...] = jnp.zeros_like(sq_ref)
        s384_ref[...] = jnp.zeros_like(s384_ref)

    def at(when, *todo):
        @pl.when(step == when)
        def _():
            for act, i in todo:
                act(i)

    at(1, (one.take, 0), (two.take, 0), (one.send, 1))
    if count == 3:
        at(5, (one.take, 1), (one.send, 2), (two.send, 1))
        at(8, (one.take, 2), (one.spread, 2))
        at(9, (two.take, 1), (two.send, 2))
        at(11, (one.settle, 2), (one.spread, 1))
        at(13, (two.take, 2), (two.spread, 2))
        at(frames, (one.settle, 1), (two.settle, 2), (one.spread, 0), (two.spread, 1))
    else:
        at(5, *[t for i in range(1, last) for t in ((one.take, i), (one.send, i + 1))], (two.send, 1))
        at(8, (one.take, last), (one.spread, last))
        at(9, *[t for i in range(1, last) for t in ((two.take, i), (two.send, i + 1))])
        at(11, *[t for i in range(last, 1, -1) for t in ((one.settle, i), (one.spread, i - 1))])
        at(13, (two.take, last), (two.spread, last))
        at(frames, (one.settle, 1), *[t for i in range(last, 1, -1) for t in ((two.settle, i), (two.spread, i - 1))],
           (one.spread, 0))

    low = lax.broadcasted_iota(jnp.int32, (ROWS, 128), 1) < 64
    wide_low = lax.broadcasted_iota(jnp.int32, (WIN, 128), 1) < 64
    ones = jnp.ones((WIN, 128), bf16)
    edge_rows = pl.ds(pl.multiple_of(jnp.where(tm == 0, frames, 1) * ROWS, 16), ROWS)
    ghost_rows = pl.ds(pl.multiple_of(jnp.where(tm == 0, frames + 1, 0) * ROWS, 16), ROWS)

    @pl.when(step < frames)
    def _():
        window = pl.ds(pl.multiple_of(step * ROWS, 16), WIN)

        def differ(h):
            at = width + h // 2 * 128
            wide = wide_low if h % 2 == 0 else ~wide_low
            v = jnp.where(wide, kv_ref[window, at : at + 128], ones)
            d_ref[h % 3] = mm_nt(ga_ref[0, :, 128 * h : 128 * h + 128], v)

        def weigh(h):
            ds_ref[h % 3] = (prob_ref[0, h].astype(f32) * d_ref[h % 3]).astype(bf16)

        held = {}

        def spend(h):
            cols = slice(h // 2 * 128, h // 2 * 128 + 128)
            vcols = slice(width + h // 2 * 128, width + h // 2 * 128 + 128)
            mine = slice(h % 2 * 64, h % 2 * 64 + 64)
            ds = ds_ref[h % 3]
            if h % 2 == 0:
                held["qt"], held["gt"] = qs_ref[0, :, cols].T, gs_ref[0, :, cols].T
            held[h] = mm(ds, kv_ref[window, cols]), mm(held["qt"][mine], ds), mm(held["gt"][mine], prob_ref[0, h])
            if h % 2:
                even, odd = held.pop(h - 1), held.pop(h)
                dq = jnp.where(low, even[0], odd[0]) * (li_ref[0, :, cols] * inv_scale)
                dq_ref[pl.ds(pl.multiple_of(step * ROWS, 16), ROWS), cols] = dq.astype(bf16)
                acc_ref[window, cols] += jnp.concatenate([even[1], odd[1]], axis=0).T
                acc_ref[window, vcols] += jnp.concatenate([even[2], odd[2]], axis=0).T

        differ(0)
        for h in range(HEADS + 1):
            if h + 1 < HEADS:
                differ(h + 1)
            if h >= 1:
                spend(h - 1)
            if h < HEADS:
                weigh(h)

    @pl.when(step == frames - 1)
    def _():
        ghost_ref[:, :width] = (acc_ref[ghost_rows, :width] * inv_scale).astype(bf16)
        ghost_ref[:, width:] = acc_ref[ghost_rows, width:].astype(bf16)
        swap.start()

    block = 2 * ROWS

    def block_of(i):
        x = x_ref[pl.ds(2 * i, 2)].reshape(block, width).astype(f32)
        n, inverse = normed_of(x)
        dq = dq_ref[pl.ds(pl.multiple_of(i * block, 16), block), :]
        here = pl.ds(pl.multiple_of(ROWS + i * block, 16), block)
        dk = (acc_ref[here, :width] * inv_scale).astype(bf16)
        dv = acc_ref[here, width:].astype(bf16)
        return n, inverse, jnp.concatenate([dq, dk, dv], axis=1)

    @pl.when(step == frames)
    def _():
        swap.wait()
        got = got_ref[...].astype(f32)
        acc_ref[edge_rows, :width] += got[:, :width] * (1.0 / inv_scale)
        acc_ref[edge_rows, width:] += got[:, width:]

        def weights(i, carry):
            n, _, grads = block_of(i)
            attn_in = (n * gain_ref[...] + shift_ref[...]).astype(bf16)
            gw_ref[...] += mm_tn(attn_in, grads)
            sq_ref[...] += fold8(grads.astype(f32))
            return carry

        lax.fori_loop(0, frames // 2, weights, 0)
        end = pack_matrix(own2_ref, 0, gw_ref[...])
        own2_ref[end:] = jnp.zeros((own2_ref.shape[0] - end, 16, 128), bf16)
        tail.send(0)

    at(frames + 3, (tail.take, 0), (tail.send, 1))

    @pl.when(step > frames)
    def _():
        n, inverse, grads = block_of(step - frames - 1)
        up = mm_nt(grads, wqkv_ref[...])
        gres = gres_ref[...].reshape(block, width)
        narrow_into(in_ref, 0, gres + norm_back(up, n, inverse, gain_ref[...]))
        s384_ref[0] += fold8(up * n)
        s384_ref[1] += fold8(up)

    @pl.when(step == steps - 1)
    def _():
        sq = colsum(sq_ref[...])
        parts = [colsum(s384_ref[0]), colsum(s384_ref[1]), sq[:, :width], sq[:, 2 * width :]]
        lines = [v[:, c : c + 128] for v in parts for c in range(0, width, 128)]
        lines += [jnp.zeros((1, 128), f32)] * (16 - len(lines))
        tile = jnp.concatenate(lines, axis=0)
        for i in range(1, count):
            tail.take(i)
            if i < last:
                tail.send(i + 1)
        for i in range(last, -1, -1):
            tail.spread(i)
            rows.spread(i, tile)
            if i == 1:
                two.settle(1)
                two.spread(0)
            if i == 0:
                one.settle(0)
                two.settle(0)
            tail.settle(i)
            tile = rows.settle(i)
        res_ref[...] = sum_ref[...]
        res2_ref[...] = sum2_ref[...]
        rows_ref[...] = tile


def unpack_kernel(res_ref, res2_ref, rows_ref, gg1, gb1, gqkv, gqv, gwo, gbo, gg2, gb2, gw1, gbf1, gw2, gbf2):
    width, hidden = gw1.shape
    tiles = width // 16
    at = 0
    for c in range(hidden // 128):
        gw1[:, 128 * c : 128 * c + 128] = res_ref[at : at + tiles].reshape(width, 128).astype(f32)
        at += tiles
    for c in range(hidden // 128):
        gw2[128 * c : 128 * c + 128, :] = res_ref[at : at + tiles].reshape(width, 128).astype(f32).T
        at += tiles
    for c in range(width // 128):
        gwo[:, 128 * c : 128 * c + 128] = res_ref[at : at + tiles].reshape(width, 128).astype(f32)
        at += tiles
    row = 0
    for out in (gg2, gb2, gbo, gbf2, gbf1):
        for c in range(out.shape[0] // 128):
            out[128 * c : 128 * c + 128] = res_ref[at + row // 16].astype(f32)[row % 16]
            row += 1
    at = 0
    for c in range(3 * width // 128):
        gqkv[:, 128 * c : 128 * c + 128] = res2_ref[at : at + tiles].reshape(width, 128).astype(f32)
        at += tiles
    rows = rows_ref[...]
    each = width // 128
    for i, out in enumerate((gg1, gb1)):
        for c in range(each):
            out[128 * c : 128 * c + 128] = rows[i * each + c]
    for i in range(2):
        for c in range(each):
            gqv[i : i + 1, 128 * c : 128 * c + 128] = rows[(i + 2) * each + c : (i + 2) * each + c + 1]


def whole(shape):
    return pl.BlockSpec(shape, lambda i: (0,) * len(shape), pipeline_mode=pl.Buffered(1))


def pairs(shape):
    return pl.BlockSpec((2,) + shape, lambda i: (i,) + (0,) * len(shape))


def single(shape):
    return pl.BlockSpec((1,) + shape, lambda i: (i,) + (0,) * len(shape))


def params(collective=None):
    if collective is None:
        return pltpu.CompilerParams(vmem_limit_bytes=60 * 2**20)
    return pltpu.CompilerParams(vmem_limit_bytes=60 * 2**20, collective_id=collective, has_side_effects=True)


def per_device(tokens, frame_clip, ln1_gain, ln1_bias, w_qkv, qv_bias, w_out, b_out, ln2_gain, ln2_bias,
               w_fc1, b_fc1, w_fc2, b_fc2, cotangent):
    count, width = tokens.shape
    hidden = w_fc1.shape[1]
    frames = count // FRAME
    steps = frames // 2
    tm = lax.axis_index("tm")
    edge = jnp.where(tm == 0, tokens[count - FRAME :], tokens[:FRAME])
    ghost = jnp.pad(lax.ppermute(edge, "tm", [(0, 1), (1, 0)]), ((0, ROWS - FRAME), (0, 0)))
    row = jnp.concatenate(
        [ln1_gain, ln1_bias, qv_bias[0], jnp.zeros((width,), bf16), qv_bias[1], b_out, ln2_gain, ln2_bias, b_fc2, b_fc1]
    ).astype(f32)[None]
    kv_rows = (frames + 2) * ROWS + WIN - 3 * ROWS
    shape = jax.ShapeDtypeStruct
    stages = stages_of(lax.axis_size("clips"))
    devices = 2 * lax.axis_size("clips")
    tiles = width // 16
    units = units_for((2 * hidden + width) // 128 * tiles + 2, devices)
    units2 = units_for(3 * width // 128 * tiles + 1, devices)
    x_pad, kv, prob, block_out, qs, ga, gs, gres, li, pack = pl.pallas_call(
        forward_kernel,
        grid=(steps,),
        in_specs=[
            pl.BlockSpec(memory_space=pltpu.SMEM),
            whole((count, width)),
            whole((ROWS, width)),
            whole((count, width)),
            whole(row.shape),
            whole((width, 3 * width)),
            whole((width, width)),
            whole((width, hidden)),
            whole((hidden, width)),
        ],
        out_specs=[
            whole((frames, ROWS, width)),
            whole((kv_rows, 2 * width)),
            pairs((HEADS, ROWS, WIN)),
            pl.BlockSpec((4 * FRAME, width), lambda i: (i // 2, 0)),
            pairs((ROWS, width)),
            pairs((ROWS, 2 * width)),
            pairs((ROWS, width)),
            pairs((ROWS, width)),
            pairs((ROWS, width)),
            whole((units, 16, 128)),
        ],
        out_shape=[
            shape((frames, ROWS, width), bf16),
            shape((kv_rows, 2 * width), bf16),
            shape((frames, HEADS, ROWS, WIN), bf16),
            shape((count, width), bf16),
            shape((frames, ROWS, width), bf16),
            shape((frames, ROWS, 2 * width), bf16),
            shape((frames, ROWS, width), bf16),
            shape((frames, ROWS, width), f32),
            shape((frames, ROWS, width), f32),
            shape((units, 16, 128), bf16),
        ],
        scratch_shapes=[
            pltpu.VMEM((frames, ROWS, width), bf16),
            pltpu.VMEM((frames, ROWS, width), bf16),
            pltpu.VMEM((kv_rows, 128), bf16),
            pltpu.VMEM((3, ROWS, WIN), f32),
            pltpu.VMEM((2 * ROWS, width), f32),
            pltpu.VMEM((4 * FRAME, width), f32),
            pltpu.VMEM((width, hidden), f32),
            pltpu.VMEM((width, hidden), f32),
            pltpu.VMEM((width, width), f32),
            pltpu.VMEM((8, hidden), f32),
            pltpu.VMEM((4, 8, width), f32),
        ],
        compiler_params=params(),
    )(frame_clip, tokens, ghost, cotangent, row, w_qkv, w_out, w_fc1, w_fc2)

    first, second = halves(units, devices)
    early = lambda sh: pl.BlockSpec((1,) + sh, lambda i: (jnp.minimum(i, frames - 1),) + (0,) * len(sh))
    late = lambda i: jnp.maximum(i - frames - 1, 0)
    in_vmem = pl.BlockSpec(memory_space=pltpu.VMEM)
    input_grad, res, res2, sums = pl.pallas_call(
        functools.partial(back_kernel, stages),
        grid=(frames + 1 + steps,),
        in_specs=[
            early((HEADS, ROWS, WIN)),
            whole((kv_rows, 2 * width)),
            early((ROWS, 2 * width)),
            early((ROWS, width)),
            early((ROWS, width)),
            early((ROWS, width)),
            whole((frames, ROWS, width)),
            pl.BlockSpec((2, ROWS, width), lambda i: (late(i), 0, 0)),
            whole((1, width)),
            whole((1, width)),
            whole((width, 3 * width)),
            pl.BlockSpec(memory_space=pl.ANY),
        ],
        out_specs=[
            pl.BlockSpec((2 * FRAME, width), lambda i: (late(i), 0)),
            whole((units, 16, 128)),
            whole((units2, 16, 128)),
            whole((16, 128)),
        ],
        out_shape=[
            shape((count, width), f32),
            shape((units, 16, 128), bf16),
            shape((units2, 16, 128), bf16),
            shape((16, 128), f32),
        ],
        scratch_shapes=[
            pltpu.VMEM((kv_rows, 2 * width), f32),
            pltpu.VMEM((3, ROWS, WIN), f32),
            pltpu.VMEM((3, ROWS, WIN), bf16),
            pltpu.VMEM((frames * ROWS, width), bf16),
            pltpu.VMEM((width, 3 * width), f32),
            pltpu.VMEM((8, 3 * width), f32),
            pltpu.VMEM((2, 8, width), f32),
            pltpu.VMEM((units, 16, 128), bf16),
            pltpu.VMEM((units, 16, 128), bf16),
            pltpu.VMEM((units2, 16, 128), bf16),
            pltpu.VMEM((units2, 16, 128), bf16),
            pltpu.VMEM((ROWS, 2 * width), bf16),
            pltpu.VMEM((ROWS, 2 * width), bf16),
            pltpu.SemaphoreType.DMA((2,)),
            pltpu.SemaphoreType.DMA,
        ]
        + sum_scratch(stages, first)
        + sum_scratch(stages, second)
        + sum_scratch(stages, units2)
        + rows_scratch(stages),
        compiler_params=params(0),
    )(prob, kv, ga, gs, qs, li, x_pad, gres, row[:, :width], row[:, width : 2 * width], w_qkv, pack)

    sizes = [(width,), (width,), (width, 3 * width), (2, width), (width, width), (width,), (width,), (width,),
             (width, hidden), (hidden,), (hidden, width), (width,)]
    grads = pl.pallas_call(
        unpack_kernel,
        in_specs=[in_vmem] * 3,
        out_specs=[in_vmem] * len(sizes),
        out_shape=[shape(s, f32) for s in sizes],
        compiler_params=params(),
    )(res, res2, sums)
    return (block_out, input_grad) + tuple(grads)


def solution(mesh):
    rows = P(("clips", "tm"), None)
    rep = P()
    return jax.shard_map(
        per_device,
        mesh=mesh,
        in_specs=(rows, P("clips")) + (rep,) * 12 + (rows,),
        out_specs=(rows, rows) + (rep,) * 12,
        check_vma=False,
    )
```

```python
import functools
import math

import jax
import jax.numpy as jnp
from jax import lax
from jax.experimental import pallas as pl
from jax.experimental.pallas import tpu as pltpu
from jax.sharding import PartitionSpec as P

HEADS = 6
FRAME = 196
ROWS = 208
WIN = 640
EPS = 1e-6
LOG2E = math.log2(math.e)

bf16 = jnp.bfloat16
f32 = jnp.float32


def mm(a, b):
    return jnp.dot(a, b, preferred_element_type=f32)


def mm_nt(a, b):
    return lax.dot_general(a, b, (((1,), (1,)), ((), ())), preferred_element_type=f32)


def mm_tn(a, b):
    return lax.dot_general(a, b, (((0,), (0,)), ((), ())), preferred_element_type=f32)


def normed_of(x):
    mean = jnp.mean(x, axis=-1, keepdims=True)
    centred = x - mean
    var = jnp.mean(centred * centred, axis=-1, keepdims=True)
    inverse = lax.rsqrt(var + EPS)
    return centred * inverse, inverse


def norm_back(upstream, normed, inverse, gain):
    scaled = upstream * gain
    mean = jnp.mean(scaled, axis=-1, keepdims=True)
    along = jnp.mean(scaled * normed, axis=-1, keepdims=True)
    return inverse * (scaled - mean - normed * along)


def fold8(v):
    rows, cols = v.shape
    return jnp.sum(v.reshape(rows // 8, 8, cols), axis=0)


MESH = pl.DeviceIdType.MESH


def stages_of(clips):
    stages, stride = [("tm", 1, 2)], 1
    while clips > 1:
        size = 4 if clips % 4 == 0 else (2 if clips % 2 == 0 else clips)
        stages.append(("clips", stride, size))
        stride, clips = stride * size, clips // size
    return stages


def digit(stage):
    axis, stride, size = stage
    return lax.rem(lax.axis_index(axis) // stride, size)


def partner(stage, turn):
    axis, stride, size = stage
    mine = digit(stage)
    return {axis: lax.axis_index(axis) + (lax.rem(mine + turn, size) - mine) * stride}


def greet(stages):
    sem, count = pltpu.get_barrier_semaphore(), 0
    for stage in stages:
        for turn in range(1, stage[2]):
            pl.semaphore_signal(sem, inc=1, device_id=partner(stage, turn), device_id_type=MESH)
            count += 1
    pl.semaphore_wait(sem, count)


class Sum:
    def __init__(self, stages, pack, result, landing, sent, came):
        self.stages, self.pack, self.result, self.landing = stages, pack, result, landing
        self.sent, self.came = sent, came
        self.segments, start, length = [], 0, pack.shape[0]
        for stage in stages:
            self.segments.append((start, length))
            length = length // stage[2]
            start = start + digit(stage) * length
        self.segments.append((start, length))
        self.first = [sum(s[2] - 1 for s in stages[:i]) for i in range(len(stages) + 1)]

    def _scatter(self, i):
        stage, (start, length) = self.stages[i], self.segments[i]
        part = length // stage[2]
        for turn in range(1, stage[2]):
            slot = self.first[i] + turn - 1
            other = lax.rem(digit(stage) + turn, stage[2])
            yield pltpu.make_async_remote_copy(
                src_ref=self.pack.at[pl.ds(start + other * part, part)],
                dst_ref=self.landing[i].at[turn - 1],
                send_sem=self.sent.at[slot],
                recv_sem=self.came.at[slot],
                device_id=partner(stage, turn),
                device_id_type=MESH,
            )

    def _gather(self, i):
        stage, (start, length) = self.stages[i], self.segments[i + 1]
        for turn in range(1, stage[2]):
            slot = self.first[-1] + self.first[i] + turn - 1
            here = self.result.at[pl.ds(start, length)]
            yield pltpu.make_async_remote_copy(
                src_ref=here,
                dst_ref=here,
                send_sem=self.sent.at[slot],
                recv_sem=self.came.at[slot],
                device_id=partner(stage, turn),
                device_id_type=MESH,
            )

    def send(self, i):
        for copy in self._scatter(i):
            copy.start()

    def take(self, i):
        for copy in self._scatter(i):
            copy.wait()
        start, length = self.segments[i + 1]
        into = self.result if i == len(self.stages) - 1 else self.pack
        block = next(b for b in (28, 24, 21, 16, 14, 12, 8, 7, 6, 4, 3, 2, 1) if length % b == 0)

        def add(j, carry):
            total = self.pack[pl.ds(start + j * block, block)].astype(f32)
            for turn in range(1, self.stages[i][2]):
                total = total + self.landing[i][turn - 1, pl.ds(j * block, block)].astype(f32)
            into[pl.ds(start + j * block, block)] = total.astype(bf16)
            return carry

        lax.fori_loop(0, length // block, add, 0)

    def spread(self, i):
        for copy in self._gather(i):
            copy.start()

    def settle(self, i):
        for copy in self._gather(i):
            copy.wait()


def sum_scratch(stages, units):
    shapes, left = [], units
    for stage in stages:
        left //= stage[2]
        shapes.append(pltpu.VMEM((stage[2] - 1, left, 16, 128), bf16))
    copies = 2 * sum(s[2] - 1 for s in stages)
    return shapes + [pltpu.SemaphoreType.DMA((copies,)), pltpu.SemaphoreType.DMA((copies,))]


def pack_matrix(pack, first, value):
    rows, cols = value.shape
    tiles = rows // 16
    for c in range(cols // 128):
        pack[first + c * tiles : first + (c + 1) * tiles] = (
            value[:, 128 * c : 128 * (c + 1)].astype(bf16).reshape(tiles, 16, 128)
        )
    return first + cols // 128 * tiles


def pack_rows(pack, first, vectors):
    rows = [v[:, c : c + 128] for v in vectors for c in range(0, v.shape[1], 128)]
    rows += [jnp.zeros((1, 128), f32)] * (-len(rows) % 16)
    for r in range(0, len(rows), 16):
        pack[first + r // 16] = jnp.concatenate(rows[r : r + 16], axis=0).astype(bf16)
    last = first + len(rows) // 16
    if last < pack.shape[0]:
        pack[last:] = jnp.zeros((pack.shape[0] - last, 16, 128), bf16)


def unpack_matrix(res, first, rows, cols):
    tiles = rows // 16
    part = res[first : first + cols // 128 * tiles].reshape(cols // 128, tiles, 16, 128)
    return part.transpose(1, 2, 0, 3).reshape(rows, cols).astype(f32)


def units_for(needed, devices):
    return -(-needed // devices) * devices


def colsum(v):
    return jnp.sum(v, axis=0, keepdims=True)


def widen(ref, group, which):
    start = which * FRAME // 16 * 16
    shift = which * FRAME - start
    v = ref[pl.ds(pl.multiple_of(group * 4 * FRAME + start, 16), ROWS), :].astype(f32)
    if shift:
        v = pltpu.roll(v, ROWS - shift, 0)
    row = lax.broadcasted_iota(jnp.int32, (16, v.shape[1]), 0)
    return v, jnp.where(row < 16 - (ROWS - FRAME), v[ROWS - 16 :], 0.0)


def narrow_into(ref, start, v):
    edge = FRAME // 8 * 8
    over = FRAME - edge
    second = pltpu.roll(v[ROWS:], over, 0)
    row = lax.broadcasted_iota(jnp.int32, (8, v.shape[1]), 0)
    ref[pl.ds(pl.multiple_of(start, 8), edge), :] = v[:edge]
    ref[pl.ds(pl.multiple_of(start + edge, 8), 8), :] = jnp.where(row < over, v[edge : edge + 8], second[:8])
    rest = 2 * FRAME - edge - 8
    ref[pl.ds(pl.multiple_of(start + edge + 8, 8), rest), :] = second[8 : 8 + rest]


def forward_kernel(
    clip_ref,
    tok_ref,
    ghost_ref,
    g1_ref,
    s1_ref,
    qv_ref,
    bo_ref,
    g2_ref,
    s2_ref,
    bf1_ref,
    bf2_ref,
    wqkv_ref,
    cot_hbm,
    wout_hbm,
    w1_hbm,
    w2_hbm,
    x_hbm,
    kv_hbm,
    prob_ref,
    out_ref,
    qs_ref,
    ga_ref,
    gs_ref,
    gres_ref,
    li_ref,
    row_ref,
    pack_ref,
    x_ref,
    kv_ref,
    cot_ref,
    wout_ref,
    w1_ref,
    w2_ref,
    q_ref,
    cp_ref,
    flag_ref,
    s_ref,
    o_ref,
    flat_ref,
    gw1_ref,
    gw2_ref,
    gwo_ref,
    sb1_ref,
    s384_ref,
    sems,
):
    step = pl.program_id(0)
    steps = pl.num_programs(0)
    frames = x_ref.shape[0]
    width = x_ref.shape[-1]
    hidden = w1_ref.shape[-1]
    tm = lax.axis_index("tm")
    copies = [
        pltpu.make_async_copy(src, dst, sems.at[i])
        for i, (src, dst) in enumerate(
            ((cot_hbm, cot_ref), (wout_hbm, wout_ref), (w1_hbm, w1_ref), (w2_hbm, w2_ref), (x_ref, x_hbm), (kv_ref, kv_hbm))
        )
    ]

    @pl.when(step == 0)
    def _():
        for copy in copies[:4]:
            copy.start()
        vectors = [g1_ref[...], s1_ref[...], None, None, None, bo_ref[...], g2_ref[...], s2_ref[...], bf2_ref[...]]
        for i, v in enumerate(vectors):
            if v is not None:
                row_ref[:, i * width : (i + 1) * width] = v.astype(f32)[None, :]
        row_ref[:, 2 * width : 3 * width] = qv_ref[0:1, :].astype(f32)
        row_ref[:, 3 * width : 4 * width] = jnp.zeros((1, width), f32)
        row_ref[:, 4 * width : 5 * width] = qv_ref[1:2, :].astype(f32)
        row_ref[:, 9 * width :] = bf1_ref[...].astype(f32)[None, :]

    vec = lambda i, n=width: row_ref[:, i * width : i * width + n]
    gain1, shift1, bias3, biaso, gain2, shift2, bias2, bias1 = (
        vec(0), vec(1), vec(2, 3 * width), vec(5), vec(6), vec(7), vec(8), vec(9, hidden))

    @pl.when(step == 0)
    def _():
        gw1_ref[...] = jnp.zeros_like(gw1_ref)
        gw2_ref[...] = jnp.zeros_like(gw2_ref)
        gwo_ref[...] = jnp.zeros_like(gwo_ref)
        sb1_ref[...] = jnp.zeros_like(sb1_ref)
        s384_ref[...] = jnp.zeros_like(s384_ref)
        at = lax.broadcasted_iota(jnp.int32, flag_ref.shape, 0)
        lane = lax.broadcasted_iota(jnp.int32, flag_ref.shape, 1) % 64
        slot = at // ROWS
        flag_ref[...] = jnp.where(
            lane == 0,
            jnp.where(at - slot * ROWS < FRAME, 0.0, -1e30),
            jnp.where(lane == 1 + slot % 4, 1.0, 0.0),
        ).astype(bf16)
        zero_slot = jnp.where(tm == 0, 0, frames + 1)
        ghost_slot = frames + 1 - zero_slot
        kv_ref[pl.ds(pl.multiple_of(zero_slot * ROWS, 16), ROWS), :] = jnp.zeros((ROWS, 2 * width), bf16)
        kv_ref[(frames + 2) * ROWS :, :] = jnp.zeros((WIN - 3 * ROWS, 2 * width), bf16)

        x = ghost_ref[...].astype(f32)
        x = jnp.where(tm == 0, x, pltpu.roll(x, FRAME, 0))
        n, _ = normed_of(x)
        kv = mm((n * gain1 + shift1).astype(bf16), wqkv_ref[:, width:]) + bias3[:, width:]
        kv_ref[pl.ds(pl.multiple_of(ghost_slot * ROWS, 16), ROWS), :] = kv.astype(bf16)

        def pad(i, src, dst):
            for which in range(4):
                v, end = widen(src, i, which)
                dst[4 * i + which, : ROWS - 16] = v[: ROWS - 16].astype(bf16)
                dst[4 * i + which, ROWS - 16 :] = end.astype(bf16)

        def ready(i):
            x = x_ref[4 * i : 4 * i + 4].reshape(4 * ROWS, width).astype(f32)
            n, _ = normed_of(x)
            return (n * gain1 + shift1).astype(bf16)

        def project(i, normed):
            qkv = (mm(normed, wqkv_ref[...]) + bias3).astype(bf16)
            q_ref[4 * i : 4 * i + 4] = qkv[:, :width].reshape(4, ROWS, width)
            kv_ref[(4 * i + 1) * ROWS : (4 * i + 5) * ROWS, :] = qkv[:, width:]

        for i in range(frames // 4):
            pad(i, tok_ref, x_ref)
        normed = ready(0)
        for i in range(frames // 4):
            following = ready(i + 1) if i + 1 < frames // 4 else None
            project(i, normed)
            normed = following
        for copy in copies[4:]:
            copy.start()
        for copy in copies[:4]:
            copy.wait()
        for i in range(frames // 4):
            pad(i, cot_ref, cp_ref)

    low = lax.broadcasted_iota(jnp.int32, (ROWS, 128), 1) < 64
    wide_low = lax.broadcasted_iota(jnp.int32, (WIN, 128), 1) < 64
    lane = lax.broadcasted_iota(jnp.int32, (1, 128), 1) % 64
    ones = jnp.ones((WIN, 128), bf16)
    scale = LOG2E / math.sqrt(width // HEADS)
    flags, windows = [], []
    for sub in range(2):
        frame = 2 * step + sub
        here = tm * frames + frame
        own = clip_ref[here]
        before = jnp.where(here > 0, clip_ref[jnp.maximum(here - 1, 0)], -1)
        after = jnp.where(here < 2 * frames - 1, clip_ref[jnp.minimum(here + 1, 2 * frames - 1)], -1)
        none = jnp.float32(-1e30)
        row = jnp.where(lane == 0, 1.0, 0.0)
        row = jnp.where(lane == 1 + frame % 4, jnp.where(before == own, 0.0, none), row)
        row = jnp.where(lane == 1 + (frame + 2) % 4, jnp.where(after == own, 0.0, none), row)
        row = jnp.where(lane == 1 + (frame + 3) % 4, none, row)
        flags.append(jnp.broadcast_to(row.astype(bf16), (ROWS, 128)))
        windows.append(pl.ds(pl.multiple_of(frame * ROWS, 16), WIN))

    def score(t):
        sub, h = divmod(t, HEADS)
        cols = slice(h // 2 * 128, h // 2 * 128 + 128)
        mine, wide = (low, wide_low) if h % 2 == 0 else (~low, ~wide_low)
        q = jnp.where(mine, q_ref[2 * step + sub, :, cols], flags[sub])
        k = jnp.where(wide, kv_ref[windows[sub], cols], flag_ref[windows[sub], :])
        s_ref[t % 3] = mm_nt(q, k)

    def soften(t):
        sub, h = divmod(t, HEADS)
        s = s_ref[t % 3]
        top = jnp.max(s, axis=-1, keepdims=True)
        prob_ref[sub, h] = jnp.exp2((s - top) * scale).astype(bf16)

    parts = {}

    def attend(t):
        sub, h = divmod(t, HEADS)
        at = h // 2 * 128
        wide = wide_low if h % 2 == 0 else ~wide_low
        v = jnp.where(wide, kv_ref[windows[sub], width + at : width + at + 128], ones)
        parts[t] = mm(prob_ref[sub, h], v)
        if h % 2:
            even, odd = parts.pop(t - 1), parts.pop(t)
            total = pltpu.roll(jnp.where(low, odd, even), 64, 1)
            inverse = 1.0 / total
            rows = slice(sub * ROWS, (sub + 1) * ROWS)
            o_ref[rows, at : at + 128] = jnp.where(low, even, odd) * inverse
            li_ref[sub, :, at : at + 128] = inverse

    score(0)
    for t in range(2 * HEADS + 1):
        if t + 1 < 2 * HEADS:
            score(t + 1)
        if t >= 1:
            attend(t - 1)
        if t < 2 * HEADS:
            soften(t)

    att = o_ref[...].astype(bf16)
    both = pl.ds(2 * step, 2)
    x = x_ref[both].reshape(2 * ROWS, width).astype(f32)
    resid = x + mm(att, wout_ref[...]) + biaso
    n2, inv2 = normed_of(resid)
    mlp_in = (n2 * gain2 + shift2).astype(bf16)
    cot = cp_ref[both].reshape(2 * ROWS, width)
    chunk = 512
    chunks = [slice(c, c + chunk) for c in range(0, hidden, chunk)]
    held = {}

    def start(c):
        held[c] = mm(mlp_in, w1_ref[:, chunks[c]]), mm_nt(cot, w2_ref[chunks[c], :])

    def middle(c):
        pre, ghid = held[c]
        pre = pre + bias1[:, chunks[c]]
        cdf = 0.5 + 0.5 * lax.erf(pre * (1.0 / math.sqrt(2.0)))
        dens = jnp.exp2(pre * pre * (-0.5 * LOG2E)) * (1.0 / math.sqrt(2.0 * math.pi))
        gpre = (ghid * (cdf + pre * dens)).astype(bf16)
        sb1_ref[:, chunks[c]] += fold8(gpre.astype(f32))
        held[c] = (pre * cdf).astype(bf16), gpre

    def weights(c):
        gw2_ref[:, chunks[c]] += mm_tn(cot, held[c][0])
        gw1_ref[:, chunks[c]] += mm_tn(mlp_in, held[c][1])

    start(0)
    for c in range(len(chunks)):
        if c + 1 < len(chunks):
            start(c + 1)
        middle(c)
    hid = jnp.concatenate([held[c][0] for c in range(len(chunks))], axis=1)
    gpre = jnp.concatenate([held[c][1] for c in range(len(chunks))], axis=1)
    up = mm_nt(gpre, w1_ref[...])
    cot32 = cot.astype(f32)
    gres = cot32 + norm_back(up, n2, inv2, gain2)
    gres_ref[...] = gres.reshape(2, ROWS, width)
    branch = gres.astype(bf16)
    weights(0)
    g = mm_nt(branch, wout_ref[...]).astype(bf16)
    for c in range(1, len(chunks) - 1):
        weights(c)
    g32 = g.astype(f32)
    inverse = li_ref[...].reshape(2 * ROWS, width)
    gs_ref[...] = (g32 * inverse).astype(bf16).reshape(2, ROWS, width)
    qs_ref[...] = (q_ref[both].reshape(2 * ROWS, width).astype(f32) * inverse).astype(bf16).reshape(2, ROWS, width)
    dots = g32 * o_ref[...]
    low2 = lax.broadcasted_iota(jnp.int32, (2 * ROWS, 128), 1) < 64
    for pair in range(HEADS // 2):
        cols = slice(128 * pair, 128 * pair + 128)
        d = dots[:, cols]
        even = jnp.sum(jnp.where(low2, d, 0.0), axis=-1, keepdims=True)
        odd = jnp.sum(jnp.where(low2, 0.0, d), axis=-1, keepdims=True)
        less = -jnp.where(low2, odd, even)
        one = less.astype(bf16)
        two = (less - one.astype(f32)).astype(bf16)
        three = (less - one.astype(f32) - two.astype(f32)).astype(bf16)
        zero = jnp.zeros_like(one)
        lanes = jnp.broadcast_to(lane, (2 * ROWS, 128))
        tail = jnp.where(lanes == 0, one, jnp.where(lanes == 1, two, jnp.where(lanes == 2, three, zero)))
        gp = g[:, cols]
        ga_ref[:, :, 256 * pair : 256 * pair + 128] = jnp.where(low2, gp, tail).reshape(2, ROWS, 128)
        ga_ref[:, :, 256 * pair + 128 : 256 * pair + 256] = jnp.where(low2, tail, gp).reshape(2, ROWS, 128)
    s384_ref[0] += fold8(up * n2)
    s384_ref[1] += fold8(up)
    s384_ref[2] += fold8(branch.astype(f32))
    s384_ref[3] += fold8(cot32)
    weights(len(chunks) - 1)
    gwo_ref[...] += mm_tn(att, branch)
    out = resid + bias2 + mm(hid, w2_ref[...])
    narrow_into(flat_ref, step % 2 * 2 * FRAME, out)

    @pl.when(step % 2 == 1)
    def _():
        out_ref[...] = flat_ref[...].astype(bf16)

    @pl.when(step == steps - 1)
    def _():
        at = pack_matrix(pack_ref, 0, gw1_ref[...])
        at = pack_matrix(pack_ref, at, gw2_ref[...])
        at = pack_matrix(pack_ref, at, gwo_ref[...])
        pack_rows(pack_ref, at, [colsum(s384_ref[i]) for i in range(4)] + [colsum(sb1_ref[...])])
        for copy in copies[4:]:
            copy.wait()


class Rows:
    def __init__(self, stages, boards, sent, came):
        self.stages, self.boards, self.sent, self.came = stages, boards, sent, came
        self.first = [sum(s[2] - 1 for s in stages[:i]) for i in range(len(stages) + 1)]

    def _copies(self, i):
        stage = self.stages[i]
        here = self.boards[i].at[digit(stage)]
        for turn in range(1, stage[2]):
            slot = self.first[i] + turn - 1
            yield pltpu.make_async_remote_copy(
                src_ref=here,
                dst_ref=here,
                send_sem=self.sent.at[slot],
                recv_sem=self.came.at[slot],
                device_id=partner(stage, turn),
                device_id_type=MESH,
            )

    def spread(self, i, tile):
        self.boards[i][digit(self.stages[i])] = tile
        for copy in self._copies(i):
            copy.start()

    def settle(self, i):
        for copy in self._copies(i):
            copy.wait()
        total = self.boards[i][0]
        for j in range(1, self.stages[i][2]):
            total = total + self.boards[i][j]
        return total


def rows_scratch(stages):
    copies = sum(s[2] - 1 for s in stages)
    return [pltpu.VMEM((s[2], 16, 128), f32) for s in stages] + [pltpu.SemaphoreType.DMA((copies,))] * 2


def halves(units, devices):
    first = -(-units // (2 * devices)) * devices
    return first, units - first


def back_kernel(stages, prob_ref, kv_hbm, ga_ref, gs_ref, qs_ref, li_ref, x_hbm, gres_ref, row_ref,
                wqkv_hbm, pack_hbm, in_ref, res_ref, res2_ref, rows_ref,
                acc_ref, d_ref, ds_ref, dq_ref, gw_ref, sq_ref, s384_ref, own_ref, sum_ref, own2_ref, sum2_ref,
                ghost_ref, got_ref, kv_ref, x_ref, wqkv_ref, ghost_sems, load_sems, *rest):
    step = pl.program_id(0)
    width = gs_ref.shape[-1]
    frames = x_hbm.shape[0]
    steps = frames + 1 + frames // 2
    tm = lax.axis_index("tm")
    inv_scale = 1.0 / math.sqrt(width // HEADS)
    count = len(stages)
    last = count - 1
    devices = 2
    for stage in stages[1:]:
        devices *= stage[2]
    cut, _ = halves(own_ref.shape[0], devices)
    sums = []
    for n, (own, res) in enumerate(
        ((own_ref.at[:cut], sum_ref.at[:cut]), (own_ref.at[cut:], sum_ref.at[cut:]), (own2_ref, sum2_ref))
    ):
        mine = rest[n * (count + 2) : (n + 1) * (count + 2)]
        sums.append(Sum(stages, own, res, mine[:count], *mine[count:]))
    one, two, tail = sums
    extra = rest[3 * (count + 2) :]
    rows = Rows(stages, extra[:count], *extra[count:])
    near = 6 * ROWS
    loads = [
        pltpu.make_async_copy(src, dst, load_sems.at[i])
        for i, (src, dst) in enumerate(
            (
                (pack_hbm, own_ref),
                (kv_hbm.at[:near], kv_ref.at[:near]),
                (kv_hbm.at[near:], kv_ref.at[near:]),
                (x_hbm, x_ref),
                (wqkv_hbm, wqkv_ref),
            )
        )
    ]
    swap = pltpu.make_async_remote_copy(
        src_ref=ghost_ref,
        dst_ref=got_ref,
        send_sem=ghost_sems.at[0],
        recv_sem=ghost_sems.at[1],
        device_id=partner(stages[0], 1),
        device_id_type=MESH,
    )

    @pl.when(step == 0)
    def _():
        for load in loads:
            load.start()
        greet(stages)
        loads[0].wait()
        one.send(0)
        two.send(0)
        acc_ref[...] = jnp.zeros_like(acc_ref)
        gw_ref[...] = jnp.zeros_like(gw_ref)
        sq_ref[...] = jnp.zeros_like(sq_ref)
        s384_ref[...] = jnp.zeros_like(s384_ref)
        loads[1].wait()

    @pl.when(step == 1)
    def _():
        loads[2].wait()

    def at(when, *todo):
        @pl.when(step == when)
        def _():
            for act, i in todo:
                act(i)

    at(1, (one.take, 0), (two.take, 0), (one.send, 1))
    if count == 3:
        at(5, (one.take, 1), (one.send, 2), (two.send, 1))
        at(8, (one.take, 2), (one.spread, 2))
        at(9, (two.take, 1), (two.send, 2))
        at(11, (one.settle, 2), (one.spread, 1))
        at(13, (two.take, 2), (two.spread, 2))
        at(frames, (one.settle, 1), (two.settle, 2), (one.spread, 0), (two.spread, 1))
    else:
        at(5, *[t for i in range(1, last) for t in ((one.take, i), (one.send, i + 1))], (two.send, 1))
        at(8, (one.take, last), (one.spread, last))
        at(9, *[t for i in range(1, last) for t in ((two.take, i), (two.send, i + 1))])
        at(11, *[t for i in range(last, 1, -1) for t in ((one.settle, i), (one.spread, i - 1))])
        at(13, (two.take, last), (two.spread, last))
        at(frames, (one.settle, 1), *[t for i in range(last, 1, -1) for t in ((two.settle, i), (two.spread, i - 1))],
           (one.spread, 0))

    low = lax.broadcasted_iota(jnp.int32, (ROWS, 128), 1) < 64
    wide_low = lax.broadcasted_iota(jnp.int32, (WIN, 128), 1) < 64
    ones = jnp.ones((WIN, 128), bf16)
    edge_rows = pl.ds(pl.multiple_of(jnp.where(tm == 0, frames, 1) * ROWS, 16), ROWS)
    ghost_rows = pl.ds(pl.multiple_of(jnp.where(tm == 0, frames + 1, 0) * ROWS, 16), ROWS)

    @pl.when(step < frames)
    def _():
        window = pl.ds(pl.multiple_of(step * ROWS, 16), WIN)

        def differ(h):
            at = width + h // 2 * 128
            wide = wide_low if h % 2 == 0 else ~wide_low
            v = jnp.where(wide, kv_ref[window, at : at + 128], ones)
            d_ref[h % 3] = mm_nt(ga_ref[0, :, 128 * h : 128 * h + 128], v)

        def weigh(h):
            ds_ref[h % 3] = (prob_ref[0, h].astype(f32) * d_ref[h % 3]).astype(bf16)

        held = {}

        def spend(h):
            cols = slice(h // 2 * 128, h // 2 * 128 + 128)
            vcols = slice(width + h // 2 * 128, width + h // 2 * 128 + 128)
            mine = slice(h % 2 * 64, h % 2 * 64 + 64)
            ds = ds_ref[h % 3]
            if h % 2 == 0:
                held["qt"], held["gt"] = qs_ref[0, :, cols].T, gs_ref[0, :, cols].T
            held[h] = mm(ds, kv_ref[window, cols]), mm(held["qt"][mine], ds), mm(held["gt"][mine], prob_ref[0, h])
            if h % 2:
                even, odd = held.pop(h - 1), held.pop(h)
                dq = jnp.where(low, even[0], odd[0]) * (li_ref[0, :, cols] * inv_scale)
                dq_ref[pl.ds(pl.multiple_of(step * ROWS, 16), ROWS), cols] = dq.astype(bf16)
                acc_ref[window, cols] += jnp.concatenate([even[1], odd[1]], axis=0).T
                acc_ref[window, vcols] += jnp.concatenate([even[2], odd[2]], axis=0).T

        differ(0)
        for h in range(HEADS + 1):
            if h + 1 < HEADS:
                differ(h + 1)
            if h >= 1:
                spend(h - 1)
            if h < HEADS:
                weigh(h)

    @pl.when(step == frames - 1)
    def _():
        ghost_ref[:, :width] = (acc_ref[ghost_rows, :width] * inv_scale).astype(bf16)
        ghost_ref[:, width:] = acc_ref[ghost_rows, width:].astype(bf16)
        swap.start()

    block = 2 * ROWS

    def block_of(i):
        x = x_ref[pl.ds(2 * i, 2)].reshape(block, width).astype(f32)
        n, inverse = normed_of(x)
        dq = dq_ref[pl.ds(pl.multiple_of(i * block, 16), block), :]
        here = pl.ds(pl.multiple_of(ROWS + i * block, 16), block)
        dk = (acc_ref[here, :width] * inv_scale).astype(bf16)
        dv = acc_ref[here, width:].astype(bf16)
        return n, inverse, jnp.concatenate([dq, dk, dv], axis=1)

    @pl.when(step == frames)
    def _():
        loads[3].wait()
        loads[4].wait()
        swap.wait()
        got = got_ref[...].astype(f32)
        acc_ref[edge_rows, :width] += got[:, :width] * (1.0 / inv_scale)
        acc_ref[edge_rows, width:] += got[:, width:]

        def weights(i, carry):
            n, _, grads = block_of(i)
            attn_in = (n * row_ref[:, :width] + row_ref[:, width : 2 * width]).astype(bf16)
            gw_ref[...] += mm_tn(attn_in, grads)
            sq_ref[...] += fold8(grads.astype(f32))
            return carry

        lax.fori_loop(0, frames // 2, weights, 0)
        end = pack_matrix(own2_ref, 0, gw_ref[...])
        own2_ref[end:] = jnp.zeros((own2_ref.shape[0] - end, 16, 128), bf16)
        tail.send(0)

    at(frames + 3, (tail.take, 0), (tail.send, 1))

    @pl.when(step > frames)
    def _():
        n, inverse, grads = block_of(step - frames - 1)
        up = mm_nt(grads, wqkv_ref[...])
        gres = gres_ref[...].reshape(block, width)
        narrow_into(in_ref, 0, gres + norm_back(up, n, inverse, row_ref[:, :width]))
        s384_ref[0] += fold8(up * n)
        s384_ref[1] += fold8(up)

    @pl.when(step == steps - 1)
    def _():
        sq = colsum(sq_ref[...])
        parts = [colsum(s384_ref[0]), colsum(s384_ref[1]), sq[:, :width], sq[:, 2 * width :]]
        lines = [v[:, c : c + 128] for v in parts for c in range(0, width, 128)]
        lines += [jnp.zeros((1, 128), f32)] * (16 - len(lines))
        tile = jnp.concatenate(lines, axis=0)
        for i in range(1, count):
            tail.take(i)
            if i < last:
                tail.send(i + 1)
        for i in range(last, -1, -1):
            tail.spread(i)
            rows.spread(i, tile)
            if i == 1:
                two.settle(1)
                two.spread(0)
            if i == 0:
                one.settle(0)
                two.settle(0)
            tail.settle(i)
            tile = rows.settle(i)
        res_ref[...] = sum_ref[...]
        res2_ref[...] = sum2_ref[...]
        rows_ref[...] = tile


def unpack_kernel(in_hbm, res_hbm, res2_ref, rows_ref, out_hbm, gg1, gb1, gqkv_hbm, gqv, gwo_hbm, gbo, gg2, gb2, gw1_hbm,
                  gbf1, gw2_hbm, gbf2, gqkv, gwo, gw1, gw2, res_ref, mid_ref, sems):
    width, hidden = gw1.shape
    tiles = width // 16
    across = hidden // 128 * tiles
    pieces = 4
    piece = in_hbm.shape[0] // pieces
    come, go = [], []
    for i in range(pieces):
        rows = slice(i * piece, (i + 1) * piece)
        come.append(pltpu.make_async_copy(in_hbm.at[rows], mid_ref.at[rows], sems.at[7 + i]))
        go.append(pltpu.make_async_copy(mid_ref.at[rows], out_hbm.at[rows], sems.at[7 + pieces + i]))
    parts = (0, across, 2 * across, res_hbm.shape[0])
    loads = [
        pltpu.make_async_copy(res_hbm.at[lo:hi], res_ref.at[lo:hi], sems.at[i])
        for i, (lo, hi) in enumerate(zip(parts, parts[1:]))
    ]
    stores = [
        pltpu.make_async_copy(src, dst, sems.at[3 + i])
        for i, (src, dst) in enumerate(((gqkv, gqkv_hbm), (gwo, gwo_hbm), (gw1, gw1_hbm), (gw2, gw2_hbm)))
    ]
    for copy in loads + come:
        copy.start()
    at = 0
    for c in range(3 * width // 128):
        gqkv[:, 128 * c : 128 * c + 128] = res2_ref[at : at + tiles].reshape(width, 128).astype(f32)
        at += tiles
    stores[0].start()
    loads[0].wait()
    at = 0
    for c in range(hidden // 128):
        gw1[:, 128 * c : 128 * c + 128] = res_ref[at : at + tiles].reshape(width, 128).astype(f32)
        at += tiles
    stores[2].start()
    for i in range(pieces):
        come[i].wait()
        go[i].start()
    loads[1].wait()
    for c in range(hidden // 128):
        gw2[128 * c : 128 * c + 128, :] = res_ref[at : at + tiles].reshape(width, 128).astype(f32).T
        at += tiles
    stores[3].start()
    loads[2].wait()
    for c in range(width // 128):
        gwo[:, 128 * c : 128 * c + 128] = res_ref[at : at + tiles].reshape(width, 128).astype(f32)
        at += tiles
    stores[1].start()
    row = 0
    for out in (gg2, gb2, gbo, gbf2, gbf1):
        for c in range(out.shape[0] // 128):
            out[128 * c : 128 * c + 128] = res_ref[at + row // 16].astype(f32)[row % 16]
            row += 1
    rows = rows_ref[...]
    each = width // 128
    for i, out in enumerate((gg1, gb1)):
        for c in range(each):
            out[128 * c : 128 * c + 128] = rows[i * each + c]
    for i in range(2):
        for c in range(each):
            gqv[i : i + 1, 128 * c : 128 * c + 128] = rows[(i + 2) * each + c : (i + 2) * each + c + 1]
    for copy in stores + go:
        copy.wait()


def whole(shape):
    return pl.BlockSpec(shape, lambda i: (0,) * len(shape), pipeline_mode=pl.Buffered(1))


def pairs(shape):
    return pl.BlockSpec((2,) + shape, lambda i: (i,) + (0,) * len(shape))


def single(shape):
    return pl.BlockSpec((1,) + shape, lambda i: (i,) + (0,) * len(shape))


def params(collective=None):
    if collective is None:
        return pltpu.CompilerParams(vmem_limit_bytes=60 * 2**20)
    return pltpu.CompilerParams(vmem_limit_bytes=60 * 2**20, collective_id=collective, has_side_effects=True)


def per_device(tokens, frame_clip, ln1_gain, ln1_bias, w_qkv, qv_bias, w_out, b_out, ln2_gain, ln2_bias,
               w_fc1, b_fc1, w_fc2, b_fc2, cotangent):
    count, width = tokens.shape
    hidden = w_fc1.shape[1]
    frames = count // FRAME
    steps = frames // 2
    tm = lax.axis_index("tm")
    edge = jnp.where(tm == 0, tokens[count - ROWS :], tokens[:ROWS])
    ghost = lax.ppermute(edge, "tm", [(0, 1), (1, 0)])
    in_vmem = pl.BlockSpec(memory_space=pltpu.VMEM)
    in_hbm = pl.BlockSpec(memory_space=pl.ANY)
    kv_rows = (frames + 2) * ROWS + WIN - 3 * ROWS
    shape = jax.ShapeDtypeStruct
    stages = stages_of(lax.axis_size("clips"))
    devices = 2 * lax.axis_size("clips")
    tiles = width // 16
    units = units_for((2 * hidden + width) // 128 * tiles + 2, devices)
    units2 = units_for(3 * width // 128 * tiles + 1, devices)
    x_pad, kv, prob, block_out, qs, ga, gs, gres, li, row, pack = pl.pallas_call(
        forward_kernel,
        grid=(steps,),
        in_specs=[
            pl.BlockSpec(memory_space=pltpu.SMEM),
            whole((count, width)),
            whole((ROWS, width)),
            whole((width,)),
            whole((width,)),
            whole((2, width)),
            whole((width,)),
            whole((width,)),
            whole((width,)),
            whole((hidden,)),
            whole((width,)),
            whole((width, 3 * width)),
            in_hbm,
            in_hbm,
            in_hbm,
            in_hbm,
        ],
        out_specs=[
            in_hbm,
            in_hbm,
            pairs((HEADS, ROWS, WIN)),
            pl.BlockSpec((4 * FRAME, width), lambda i: (i // 2, 0)),
            pairs((ROWS, width)),
            pairs((ROWS, 2 * width)),
            pairs((ROWS, width)),
            pairs((ROWS, width)),
            pairs((ROWS, width)),
            whole((1, 9 * width + hidden)),
            whole((units, 16, 128)),
        ],
        out_shape=[
            shape((frames, ROWS, width), bf16),
            shape((kv_rows, 2 * width), bf16),
            shape((frames, HEADS, ROWS, WIN), bf16),
            shape((count, width), bf16),
            shape((frames, ROWS, width), bf16),
            shape((frames, ROWS, 2 * width), bf16),
            shape((frames, ROWS, width), bf16),
            shape((frames, ROWS, width), f32),
            shape((frames, ROWS, width), f32),
            shape((1, 9 * width + hidden), f32),
            shape((units, 16, 128), bf16),
        ],
        scratch_shapes=[
            pltpu.VMEM((frames, ROWS, width), bf16),
            pltpu.VMEM((kv_rows, 2 * width), bf16),
            pltpu.VMEM((count, width), bf16),
            pltpu.VMEM((width, width), bf16),
            pltpu.VMEM((width, hidden), bf16),
            pltpu.VMEM((hidden, width), bf16),
            pltpu.VMEM((frames, ROWS, width), bf16),
            pltpu.VMEM((frames, ROWS, width), bf16),
            pltpu.VMEM((kv_rows, 128), bf16),
            pltpu.VMEM((3, ROWS, WIN), f32),
            pltpu.VMEM((2 * ROWS, width), f32),
            pltpu.VMEM((4 * FRAME, width), f32),
            pltpu.VMEM((width, hidden), f32),
            pltpu.VMEM((width, hidden), f32),
            pltpu.VMEM((width, width), f32),
            pltpu.VMEM((8, hidden), f32),
            pltpu.VMEM((4, 8, width), f32),
            pltpu.SemaphoreType.DMA((6,)),
        ],
        compiler_params=params(),
    )(frame_clip, tokens, ghost, ln1_gain, ln1_bias, qv_bias, b_out, ln2_gain, ln2_bias, b_fc1, b_fc2, w_qkv, cotangent,
      w_out, w_fc1, w_fc2)

    first, second = halves(units, devices)
    early = lambda sh: pl.BlockSpec((1,) + sh, lambda i: (jnp.minimum(i, frames - 1),) + (0,) * len(sh))
    late = lambda i: jnp.maximum(i - frames - 1, 0)
    input_grad, res, res2, sums = pl.pallas_call(
        functools.partial(back_kernel, stages),
        grid=(frames + 1 + steps,),
        in_specs=[
            early((HEADS, ROWS, WIN)),
            in_hbm,
            early((ROWS, 2 * width)),
            early((ROWS, width)),
            early((ROWS, width)),
            early((ROWS, width)),
            in_hbm,
            pl.BlockSpec((2, ROWS, width), lambda i: (late(i), 0, 0)),
            whole(row.shape),
            in_hbm,
            in_hbm,
        ],
        out_specs=[
            pl.BlockSpec((2 * FRAME, width), lambda i: (late(i), 0)),
            whole((units, 16, 128)),
            whole((units2, 16, 128)),
            whole((16, 128)),
        ],
        out_shape=[
            shape((count, width), f32),
            shape((units, 16, 128), bf16),
            shape((units2, 16, 128), bf16),
            shape((16, 128), f32),
        ],
        scratch_shapes=[
            pltpu.VMEM((kv_rows, 2 * width), f32),
            pltpu.VMEM((3, ROWS, WIN), f32),
            pltpu.VMEM((3, ROWS, WIN), bf16),
            pltpu.VMEM((frames * ROWS, width), bf16),
            pltpu.VMEM((width, 3 * width), f32),
            pltpu.VMEM((8, 3 * width), f32),
            pltpu.VMEM((2, 8, width), f32),
            pltpu.VMEM((units, 16, 128), bf16),
            pltpu.VMEM((units, 16, 128), bf16),
            pltpu.VMEM((units2, 16, 128), bf16),
            pltpu.VMEM((units2, 16, 128), bf16),
            pltpu.VMEM((ROWS, 2 * width), bf16),
            pltpu.VMEM((ROWS, 2 * width), bf16),
            pltpu.VMEM((kv_rows, 2 * width), bf16),
            pltpu.VMEM((frames, ROWS, width), bf16),
            pltpu.VMEM((width, 3 * width), bf16),
            pltpu.SemaphoreType.DMA((2,)),
            pltpu.SemaphoreType.DMA((5,)),
        ]
        + sum_scratch(stages, first)
        + sum_scratch(stages, second)
        + sum_scratch(stages, units2)
        + rows_scratch(stages),
        compiler_params=params(0),
    )(prob, kv, ga, gs, qs, li, x_pad, gres, row, w_qkv, pack)

    sizes = [(width,), (width,), (width, 3 * width), (2, width), (width, width), (width,), (width,), (width,),
             (width, hidden), (hidden,), (hidden, width), (width,)]
    big = [len(z) == 2 and z[0] > 2 for z in sizes]
    outs = pl.pallas_call(
        unpack_kernel,
        in_specs=[in_hbm, in_hbm, in_vmem, in_vmem],
        out_specs=[in_hbm] + [in_hbm if far else in_vmem for far in big],
        out_shape=[shape((count, width), f32)] + [shape(z, f32) for z in sizes],
        scratch_shapes=[
            pltpu.VMEM((width, 3 * width), f32),
            pltpu.VMEM((width, width), f32),
            pltpu.VMEM((width, hidden), f32),
            pltpu.VMEM((hidden, width), f32),
            pltpu.VMEM((units, 16, 128), bf16),
            pltpu.VMEM((count, width), f32),
            pltpu.SemaphoreType.DMA((15,)),
        ],
        compiler_params=params(),
    )(input_grad, res, res2, sums)
    return (block_out,) + tuple(outs)


def solution(mesh):
    rows = P(("clips", "tm"), None)
    rep = P()
    return jax.shard_map(
        per_device,
        mesh=mesh,
        in_specs=(rows, P("clips")) + (rep,) * 12 + (rows,),
        out_specs=(rows, rows) + (rep,) * 12,
        check_vma=False,
    )
```

```python
import functools
import math

import jax
import jax.numpy as jnp
from jax import lax
from jax.experimental import pallas as pl
from jax.experimental.pallas import tpu as pltpu
from jax.sharding import PartitionSpec as P

HEADS = 6
FRAME = 196
ROWS = 208
WIN = 640
EPS = 1e-6
LOG2E = math.log2(math.e)

bf16 = jnp.bfloat16
f32 = jnp.float32


def mm(a, b):
    return jnp.dot(a, b, preferred_element_type=f32)


def mm_nt(a, b):
    return lax.dot_general(a, b, (((1,), (1,)), ((), ())), preferred_element_type=f32)


def mm_tn(a, b):
    return lax.dot_general(a, b, (((0,), (0,)), ((), ())), preferred_element_type=f32)


def normed_of(x):
    mean = jnp.mean(x, axis=-1, keepdims=True)
    centred = x - mean
    var = jnp.mean(centred * centred, axis=-1, keepdims=True)
    inverse = lax.rsqrt(var + EPS)
    return centred * inverse, inverse


def norm_back(upstream, normed, inverse, gain):
    scaled = upstream * gain
    mean = jnp.mean(scaled, axis=-1, keepdims=True)
    along = jnp.mean(scaled * normed, axis=-1, keepdims=True)
    return inverse * (scaled - mean - normed * along)


def fold8(v):
    rows, cols = v.shape
    return jnp.sum(v.reshape(rows // 8, 8, cols), axis=0)


MESH = pl.DeviceIdType.MESH


def stages_of(clips):
    stages, stride = [("tm", 1, 2)], 1
    while clips > 1:
        size = 4 if clips % 4 == 0 else (2 if clips % 2 == 0 else clips)
        stages.append(("clips", stride, size))
        stride, clips = stride * size, clips // size
    return stages


def digit(stage):
    axis, stride, size = stage
    return lax.rem(lax.axis_index(axis) // stride, size)


def partner(stage, turn):
    axis, stride, size = stage
    mine = digit(stage)
    return {axis: lax.axis_index(axis) + (lax.rem(mine + turn, size) - mine) * stride}


def greet(stages):
    sem, count = pltpu.get_barrier_semaphore(), 0
    for stage in stages:
        for turn in range(1, stage[2]):
            pl.semaphore_signal(sem, inc=1, device_id=partner(stage, turn), device_id_type=MESH)
            count += 1
    pl.semaphore_wait(sem, count)


class Sum:
    def __init__(self, stages, pack, result, landing, sent, came):
        self.stages, self.pack, self.result, self.landing = stages, pack, result, landing
        self.sent, self.came = sent, came
        self.segments, start, length = [], 0, pack.shape[0]
        for stage in stages:
            self.segments.append((start, length))
            length = length // stage[2]
            start = start + digit(stage) * length
        self.segments.append((start, length))
        self.first = [sum(s[2] - 1 for s in stages[:i]) for i in range(len(stages) + 1)]

    def _scatter(self, i):
        stage, (start, length) = self.stages[i], self.segments[i]
        part = length // stage[2]
        for turn in range(1, stage[2]):
            slot = self.first[i] + turn - 1
            other = lax.rem(digit(stage) + turn, stage[2])
            yield pltpu.make_async_remote_copy(
                src_ref=self.pack.at[pl.ds(start + other * part, part)],
                dst_ref=self.landing[i].at[turn - 1],
                send_sem=self.sent.at[slot],
                recv_sem=self.came.at[slot],
                device_id=partner(stage, turn),
                device_id_type=MESH,
            )

    def _gather(self, i):
        stage, (start, length) = self.stages[i], self.segments[i + 1]
        for turn in range(1, stage[2]):
            slot = self.first[-1] + self.first[i] + turn - 1
            here = self.result.at[pl.ds(start, length)]
            yield pltpu.make_async_remote_copy(
                src_ref=here,
                dst_ref=here,
                send_sem=self.sent.at[slot],
                recv_sem=self.came.at[slot],
                device_id=partner(stage, turn),
                device_id_type=MESH,
            )

    def send(self, i):
        for copy in self._scatter(i):
            copy.start()

    def take(self, i):
        for copy in self._scatter(i):
            copy.wait()
        start, length = self.segments[i + 1]
        into = self.result if i == len(self.stages) - 1 else self.pack
        block = next(b for b in (28, 24, 21, 16, 14, 12, 8, 7, 6, 4, 3, 2, 1) if length % b == 0)

        def add(j, carry):
            total = self.pack[pl.ds(start + j * block, block)].astype(f32)
            for turn in range(1, self.stages[i][2]):
                total = total + self.landing[i][turn - 1, pl.ds(j * block, block)].astype(f32)
            into[pl.ds(start + j * block, block)] = total.astype(bf16)
            return carry

        lax.fori_loop(0, length // block, add, 0)

    def spread(self, i):
        for copy in self._gather(i):
            copy.start()

    def settle(self, i):
        for copy in self._gather(i):
            copy.wait()


def sum_scratch(stages, units):
    shapes, left = [], units
    for stage in stages:
        left //= stage[2]
        shapes.append(pltpu.VMEM((stage[2] - 1, left, 16, 128), bf16))
    copies = 2 * sum(s[2] - 1 for s in stages)
    return shapes + [pltpu.SemaphoreType.DMA((copies,)), pltpu.SemaphoreType.DMA((copies,))]


def pack_matrix(pack, first, value):
    rows, cols = value.shape
    tiles = rows // 16
    for c in range(cols // 128):
        pack[first + c * tiles : first + (c + 1) * tiles] = (
            value[:, 128 * c : 128 * (c + 1)].astype(bf16).reshape(tiles, 16, 128)
        )
    return first + cols // 128 * tiles


def pack_rows(pack, first, vectors):
    rows = [v[:, c : c + 128] for v in vectors for c in range(0, v.shape[1], 128)]
    rows += [jnp.zeros((1, 128), f32)] * (-len(rows) % 16)
    for r in range(0, len(rows), 16):
        pack[first + r // 16] = jnp.concatenate(rows[r : r + 16], axis=0).astype(bf16)
    last = first + len(rows) // 16
    if last < pack.shape[0]:
        pack[last:] = jnp.zeros((pack.shape[0] - last, 16, 128), bf16)


def unpack_matrix(res, first, rows, cols):
    tiles = rows // 16
    part = res[first : first + cols // 128 * tiles].reshape(cols // 128, tiles, 16, 128)
    return part.transpose(1, 2, 0, 3).reshape(rows, cols).astype(f32)


def units_for(needed, devices):
    return -(-needed // devices) * devices


def colsum(v):
    return jnp.sum(v, axis=0, keepdims=True)


def widen(ref, group, which):
    start = which * FRAME // 16 * 16
    shift = which * FRAME - start
    v = ref[pl.ds(pl.multiple_of(group * 4 * FRAME + start, 16), ROWS), :].astype(f32)
    if shift:
        v = pltpu.roll(v, ROWS - shift, 0)
    row = lax.broadcasted_iota(jnp.int32, (16, v.shape[1]), 0)
    return v, jnp.where(row < 16 - (ROWS - FRAME), v[ROWS - 16 :], 0.0)


def narrow_into(ref, start, v):
    edge = FRAME // 8 * 8
    over = FRAME - edge
    second = pltpu.roll(v[ROWS:], over, 0)
    row = lax.broadcasted_iota(jnp.int32, (8, v.shape[1]), 0)
    ref[pl.ds(pl.multiple_of(start, 8), edge), :] = v[:edge]
    ref[pl.ds(pl.multiple_of(start + edge, 8), 8), :] = jnp.where(row < over, v[edge : edge + 8], second[:8])
    rest = 2 * FRAME - edge - 8
    ref[pl.ds(pl.multiple_of(start + edge + 8, 8), rest), :] = second[8 : 8 + rest]


def forward_kernel(
    clip_ref,
    tok_ref,
    ghost_ref,
    g1_ref,
    s1_ref,
    qv_ref,
    bo_ref,
    g2_ref,
    s2_ref,
    bf1_ref,
    bf2_ref,
    wqkv_ref,
    cot_hbm,
    wout_hbm,
    w1_hbm,
    w2_hbm,
    x_hbm,
    ain_hbm,
    kv_hbm,
    prob_ref,
    out_ref,
    qs_ref,
    ga_ref,
    gs_ref,
    gres_ref,
    li_ref,
    row_ref,
    pack_ref,
    x_ref,
    ain_ref,
    kv_ref,
    cot_ref,
    wout_ref,
    w1_ref,
    w2_ref,
    q_ref,
    cp_ref,
    flag_ref,
    s_ref,
    o_ref,
    flat_ref,
    gw1_ref,
    gw2_ref,
    gwo_ref,
    sb1_ref,
    s384_ref,
    sems,
):
    step = pl.program_id(0)
    steps = pl.num_programs(0)
    frames = x_ref.shape[0]
    width = x_ref.shape[-1]
    hidden = w1_ref.shape[-1]
    tm = lax.axis_index("tm")
    copies = [
        pltpu.make_async_copy(src, dst, sems.at[i])
        for i, (src, dst) in enumerate(
            ((cot_hbm, cot_ref), (wout_hbm, wout_ref), (w1_hbm, w1_ref), (w2_hbm, w2_ref), (x_ref, x_hbm), (kv_ref, kv_hbm),
             (ain_ref, ain_hbm))
        )
    ]

    @pl.when(step == 0)
    def _():
        for copy in copies[:4]:
            copy.start()
        vectors = [g1_ref[...], s1_ref[...], None, None, None, bo_ref[...], g2_ref[...], s2_ref[...], bf2_ref[...]]
        for i, v in enumerate(vectors):
            if v is not None:
                row_ref[:, i * width : (i + 1) * width] = v.astype(f32)[None, :]
        row_ref[:, 2 * width : 3 * width] = qv_ref[0:1, :].astype(f32)
        row_ref[:, 3 * width : 4 * width] = jnp.zeros((1, width), f32)
        row_ref[:, 4 * width : 5 * width] = qv_ref[1:2, :].astype(f32)
        row_ref[:, 9 * width :] = bf1_ref[...].astype(f32)[None, :]

    vec = lambda i, n=width: row_ref[:, i * width : i * width + n]
    gain1, shift1, bias3, biaso, gain2, shift2, bias2, bias1 = (
        vec(0), vec(1), vec(2, 3 * width), vec(5), vec(6), vec(7), vec(8), vec(9, hidden))

    @pl.when(step == 0)
    def _():
        gw1_ref[...] = jnp.zeros_like(gw1_ref)
        gw2_ref[...] = jnp.zeros_like(gw2_ref)
        gwo_ref[...] = jnp.zeros_like(gwo_ref)
        sb1_ref[...] = jnp.zeros_like(sb1_ref)
        s384_ref[...] = jnp.zeros_like(s384_ref)
        at = lax.broadcasted_iota(jnp.int32, flag_ref.shape, 0)
        lane = lax.broadcasted_iota(jnp.int32, flag_ref.shape, 1) % 64
        slot = at // ROWS
        flag_ref[...] = jnp.where(
            lane == 0,
            jnp.where(at - slot * ROWS < FRAME, 0.0, -1e30),
            jnp.where(lane == 1 + slot % 4, 1.0, 0.0),
        ).astype(bf16)
        zero_slot = jnp.where(tm == 0, 0, frames + 1)
        ghost_slot = frames + 1 - zero_slot
        kv_ref[pl.ds(pl.multiple_of(zero_slot * ROWS, 16), ROWS), :] = jnp.zeros((ROWS, 2 * width), bf16)
        kv_ref[(frames + 2) * ROWS :, :] = jnp.zeros((WIN - 3 * ROWS, 2 * width), bf16)

        x = ghost_ref[...].astype(f32)
        x = jnp.where(tm == 0, x, pltpu.roll(x, FRAME, 0))
        n, _ = normed_of(x)
        kv = mm((n * gain1 + shift1).astype(bf16), wqkv_ref[:, width:]) + bias3[:, width:]
        kv_ref[pl.ds(pl.multiple_of(ghost_slot * ROWS, 16), ROWS), :] = kv.astype(bf16)

        def pad(i, src, dst):
            for which in range(4):
                v, end = widen(src, i, which)
                dst[4 * i + which, : ROWS - 16] = v[: ROWS - 16].astype(bf16)
                dst[4 * i + which, ROWS - 16 :] = end.astype(bf16)

        def ready(i):
            x = x_ref[4 * i : 4 * i + 4].reshape(4 * ROWS, width).astype(f32)
            n, _ = normed_of(x)
            normed = (n * gain1 + shift1).astype(bf16)
            ain_ref[4 * i : 4 * i + 4] = normed.reshape(4, ROWS, width)
            return normed

        def project(i, normed):
            qkv = (mm(normed, wqkv_ref[...]) + bias3).astype(bf16)
            q_ref[4 * i : 4 * i + 4] = qkv[:, :width].reshape(4, ROWS, width)
            kv_ref[(4 * i + 1) * ROWS : (4 * i + 5) * ROWS, :] = qkv[:, width:]

        for i in range(frames // 4):
            pad(i, tok_ref, x_ref)
        normed = ready(0)
        for i in range(frames // 4):
            following = ready(i + 1) if i + 1 < frames // 4 else None
            project(i, normed)
            normed = following
        for copy in copies[4:]:
            copy.start()
        for copy in copies[:4]:
            copy.wait()
        for i in range(frames // 4):
            pad(i, cot_ref, cp_ref)

    low = lax.broadcasted_iota(jnp.int32, (ROWS, 128), 1) < 64
    wide_low = lax.broadcasted_iota(jnp.int32, (WIN, 128), 1) < 64
    lane = lax.broadcasted_iota(jnp.int32, (1, 128), 1) % 64
    ones = jnp.ones((WIN, 128), bf16)
    scale = LOG2E / math.sqrt(width // HEADS)
    flags, windows = [], []
    for sub in range(2):
        frame = 2 * step + sub
        here = tm * frames + frame
        own = clip_ref[here]
        before = jnp.where(here > 0, clip_ref[jnp.maximum(here - 1, 0)], -1)
        after = jnp.where(here < 2 * frames - 1, clip_ref[jnp.minimum(here + 1, 2 * frames - 1)], -1)
        none = jnp.float32(-1e30)
        row = jnp.where(lane == 0, 1.0, 0.0)
        row = jnp.where(lane == 1 + frame % 4, jnp.where(before == own, 0.0, none), row)
        row = jnp.where(lane == 1 + (frame + 2) % 4, jnp.where(after == own, 0.0, none), row)
        row = jnp.where(lane == 1 + (frame + 3) % 4, none, row)
        flags.append(jnp.broadcast_to(row.astype(bf16), (ROWS, 128)))
        windows.append(pl.ds(pl.multiple_of(frame * ROWS, 16), WIN))

    def score(t):
        sub, h = divmod(t, HEADS)
        cols = slice(h // 2 * 128, h // 2 * 128 + 128)
        mine, wide = (low, wide_low) if h % 2 == 0 else (~low, ~wide_low)
        q = jnp.where(mine, q_ref[2 * step + sub, :, cols], flags[sub])
        k = jnp.where(wide, kv_ref[windows[sub], cols], flag_ref[windows[sub], :])
        s_ref[t % 3] = mm_nt(q, k)

    def soften(t):
        sub, h = divmod(t, HEADS)
        s = s_ref[t % 3]
        top = jnp.max(s, axis=-1, keepdims=True)
        prob_ref[sub, h] = jnp.exp2((s - top) * scale).astype(bf16)

    parts = {}

    def attend(t):
        sub, h = divmod(t, HEADS)
        at = h // 2 * 128
        wide = wide_low if h % 2 == 0 else ~wide_low
        v = jnp.where(wide, kv_ref[windows[sub], width + at : width + at + 128], ones)
        parts[t] = mm(prob_ref[sub, h], v)
        if h % 2:
            even, odd = parts.pop(t - 1), parts.pop(t)
            total = pltpu.roll(jnp.where(low, odd, even), 64, 1)
            inverse = 1.0 / total
            rows = slice(sub * ROWS, (sub + 1) * ROWS)
            o_ref[rows, at : at + 128] = jnp.where(low, even, odd) * inverse
            li_ref[sub, :, at : at + 128] = inverse

    score(0)
    for t in range(2 * HEADS + 1):
        if t + 1 < 2 * HEADS:
            score(t + 1)
        if t >= 1:
            attend(t - 1)
        if t < 2 * HEADS:
            soften(t)

    att = o_ref[...].astype(bf16)
    both = pl.ds(2 * step, 2)
    x = x_ref[both].reshape(2 * ROWS, width).astype(f32)
    resid = x + mm(att, wout_ref[...]) + biaso
    n2, inv2 = normed_of(resid)
    mlp_in = (n2 * gain2 + shift2).astype(bf16)
    cot = cp_ref[both].reshape(2 * ROWS, width)
    chunk = 512
    chunks = [slice(c, c + chunk) for c in range(0, hidden, chunk)]
    held = {}

    def start(c):
        held[c] = mm(mlp_in, w1_ref[:, chunks[c]]), mm_nt(cot, w2_ref[chunks[c], :])

    def middle(c):
        pre, ghid = held[c]
        pre = pre + bias1[:, chunks[c]]
        cdf = 0.5 + 0.5 * lax.erf(pre * (1.0 / math.sqrt(2.0)))
        dens = jnp.exp2(pre * pre * (-0.5 * LOG2E)) * (1.0 / math.sqrt(2.0 * math.pi))
        gpre = (ghid * (cdf + pre * dens)).astype(bf16)
        sb1_ref[:, chunks[c]] += fold8(gpre.astype(f32))
        held[c] = (pre * cdf).astype(bf16), gpre

    def weights(c):
        gw2_ref[:, chunks[c]] += mm_tn(cot, held[c][0])
        gw1_ref[:, chunks[c]] += mm_tn(mlp_in, held[c][1])

    start(0)
    for c in range(len(chunks)):
        if c + 1 < len(chunks):
            start(c + 1)
        middle(c)
    hid = jnp.concatenate([held[c][0] for c in range(len(chunks))], axis=1)
    gpre = jnp.concatenate([held[c][1] for c in range(len(chunks))], axis=1)
    up = mm_nt(gpre, w1_ref[...])
    cot32 = cot.astype(f32)
    gres = cot32 + norm_back(up, n2, inv2, gain2)
    gres_ref[...] = gres.reshape(2, ROWS, width)
    branch = gres.astype(bf16)
    weights(0)
    g = mm_nt(branch, wout_ref[...]).astype(bf16)
    for c in range(1, len(chunks) - 1):
        weights(c)
    g32 = g.astype(f32)
    inverse = li_ref[...].reshape(2 * ROWS, width)
    gs_ref[...] = (g32 * inverse).astype(bf16).reshape(2, ROWS, width)
    qs_ref[...] = (q_ref[both].reshape(2 * ROWS, width).astype(f32) * inverse).astype(bf16).reshape(2, ROWS, width)
    dots = g32 * o_ref[...]
    low2 = lax.broadcasted_iota(jnp.int32, (2 * ROWS, 128), 1) < 64
    for pair in range(HEADS // 2):
        cols = slice(128 * pair, 128 * pair + 128)
        d = dots[:, cols]
        even = jnp.sum(jnp.where(low2, d, 0.0), axis=-1, keepdims=True)
        odd = jnp.sum(jnp.where(low2, 0.0, d), axis=-1, keepdims=True)
        less = -jnp.where(low2, odd, even)
        one = less.astype(bf16)
        two = (less - one.astype(f32)).astype(bf16)
        three = (less - one.astype(f32) - two.astype(f32)).astype(bf16)
        zero = jnp.zeros_like(one)
        lanes = jnp.broadcast_to(lane, (2 * ROWS, 128))
        tail = jnp.where(lanes == 0, one, jnp.where(lanes == 1, two, jnp.where(lanes == 2, three, zero)))
        gp = g[:, cols]
        ga_ref[:, :, 256 * pair : 256 * pair + 128] = jnp.where(low2, gp, tail).reshape(2, ROWS, 128)
        ga_ref[:, :, 256 * pair + 128 : 256 * pair + 256] = jnp.where(low2, tail, gp).reshape(2, ROWS, 128)
    s384_ref[0] += fold8(up * n2)
    s384_ref[1] += fold8(up)
    s384_ref[2] += fold8(branch.astype(f32))
    s384_ref[3] += fold8(cot32)
    weights(len(chunks) - 1)
    gwo_ref[...] += mm_tn(att, branch)
    out = resid + bias2 + mm(hid, w2_ref[...])
    narrow_into(flat_ref, step % 2 * 2 * FRAME, out)

    @pl.when(step % 2 == 1)
    def _():
        out_ref[...] = flat_ref[...].astype(bf16)

    @pl.when(step == steps - 1)
    def _():
        at = pack_matrix(pack_ref, 0, gw1_ref[...])
        at = pack_matrix(pack_ref, at, gw2_ref[...])
        at = pack_matrix(pack_ref, at, gwo_ref[...])
        pack_rows(pack_ref, at, [colsum(s384_ref[i]) for i in range(4)] + [colsum(sb1_ref[...])])
        for copy in copies[4:]:
            copy.wait()


class Rows:
    def __init__(self, stages, boards, sent, came):
        self.stages, self.boards, self.sent, self.came = stages, boards, sent, came
        self.first = [sum(s[2] - 1 for s in stages[:i]) for i in range(len(stages) + 1)]

    def _copies(self, i):
        stage = self.stages[i]
        here = self.boards[i].at[digit(stage)]
        for turn in range(1, stage[2]):
            slot = self.first[i] + turn - 1
            yield pltpu.make_async_remote_copy(
                src_ref=here,
                dst_ref=here,
                send_sem=self.sent.at[slot],
                recv_sem=self.came.at[slot],
                device_id=partner(stage, turn),
                device_id_type=MESH,
            )

    def spread(self, i, tile):
        self.boards[i][digit(self.stages[i])] = tile
        for copy in self._copies(i):
            copy.start()

    def settle(self, i):
        for copy in self._copies(i):
            copy.wait()
        total = self.boards[i][0]
        for j in range(1, self.stages[i][2]):
            total = total + self.boards[i][j]
        return total


def rows_scratch(stages):
    copies = sum(s[2] - 1 for s in stages)
    return [pltpu.VMEM((s[2], 16, 128), f32) for s in stages] + [pltpu.SemaphoreType.DMA((copies,))] * 2


def halves(units, devices):
    first = -(-units // (2 * devices)) * devices
    return first, units - first


def back_kernel(stages, prob_ref, kv_hbm, ga_ref, gs_ref, qs_ref, li_ref, x_hbm, ain_hbm, gres_ref, row_ref,
                wqkv_hbm, pack_hbm, in_ref, res_hbm, res2_ref, rows_ref,
                acc_ref, d_ref, ds_ref, dq_ref, sq_ref, s384_ref, own_ref, sum_ref, own2_ref, sum2_ref,
                ghost_ref, got_ref, kv_ref, x_ref, ain_ref, wqkv_ref, ghost_sems, load_sems, *rest):
    step = pl.program_id(0)
    width = gs_ref.shape[-1]
    frames = x_hbm.shape[0]
    steps = frames + 1 + frames // 2
    tm = lax.axis_index("tm")
    inv_scale = 1.0 / math.sqrt(width // HEADS)
    count = len(stages)
    last = count - 1
    devices = 2
    for stage in stages[1:]:
        devices *= stage[2]
    cut, _ = halves(own_ref.shape[0], devices)
    tiles = width // 16
    early_cols = 3 * width // 128 // 2 * 128
    cut2 = units_for(early_cols // 128 * tiles, devices)
    sums = []
    for n, (own, res) in enumerate(
        (
            (own_ref.at[:cut], sum_ref.at[:cut]),
            (own_ref.at[cut:], sum_ref.at[cut:]),
            (own2_ref.at[:cut2], sum2_ref.at[:cut2]),
            (own2_ref.at[cut2:], sum2_ref.at[cut2:]),
        )
    ):
        mine = rest[n * (count + 2) : (n + 1) * (count + 2)]
        sums.append(Sum(stages, own, res, mine[:count], *mine[count:]))
    one, two, three, four = sums
    extra = rest[4 * (count + 2) :]
    rows = Rows(stages, extra[:count], *extra[count:])
    near = 6 * ROWS
    loads = [
        pltpu.make_async_copy(src, dst, load_sems.at[i])
        for i, (src, dst) in enumerate(
            (
                (pack_hbm, own_ref),
                (kv_hbm.at[:near], kv_ref.at[:near]),
                (kv_hbm.at[near:], kv_ref.at[near:]),
                (x_hbm, x_ref),
                (ain_hbm, ain_ref),
                (wqkv_hbm, wqkv_ref),
            )
        )
    ]
    keep = pltpu.make_async_copy(sum_ref, res_hbm, load_sems.at[6])
    swap = pltpu.make_async_remote_copy(
        src_ref=ghost_ref,
        dst_ref=got_ref,
        send_sem=ghost_sems.at[0],
        recv_sem=ghost_sems.at[1],
        device_id=partner(stages[0], 1),
        device_id_type=MESH,
    )

    @pl.when(step == 0)
    def _():
        for load in loads:
            load.start()
        greet(stages)
        acc_ref[: 2 * ROWS] = jnp.zeros((2 * ROWS, 2 * width), f32)
        sq_ref[...] = jnp.zeros_like(sq_ref)
        s384_ref[...] = jnp.zeros_like(s384_ref)
        loads[0].wait()
        one.send(0)
        two.send(0)
        loads[1].wait()

    @pl.when(step == 1)
    def _():
        loads[2].wait()

    def at(when, *todo):
        @pl.when(step == when)
        def _():
            for act, i in todo:
                act(i)

    def scatter(total):
        return [t for i in range(1, last) for t in ((total.take, i), (total.send, i + 1))]

    def gather(total):
        return [t for i in range(last, 1, -1) for t in ((total.settle, i), (total.spread, i - 1))]

    norm_step = frames + 1
    at(1, (one.take, 0), (two.take, 0), (one.send, 1))
    at(5, *scatter(one), (two.send, 1))
    at(8, (one.take, last), (one.spread, last))
    at(9, *scatter(two))
    at(11, *gather(one))
    at(12, (two.take, last), (two.spread, last))
    at(15, *gather(two), (one.settle, 1), (one.spread, 0))

    low = lax.broadcasted_iota(jnp.int32, (ROWS, 128), 1) < 64
    wide_low = lax.broadcasted_iota(jnp.int32, (WIN, 128), 1) < 64
    ones = jnp.ones((WIN, 128), bf16)
    edge_rows = pl.ds(pl.multiple_of(jnp.where(tm == 0, frames, 1) * ROWS, 16), ROWS)
    ghost_rows = pl.ds(pl.multiple_of(jnp.where(tm == 0, frames + 1, 0) * ROWS, 16), ROWS)

    @pl.when(step < frames)
    def _():
        window = pl.ds(pl.multiple_of(step * ROWS, 16), WIN)
        seen = pl.ds(pl.multiple_of(step * ROWS, 16), 2 * ROWS)
        fresh = pl.ds(pl.multiple_of((step + 2) * ROWS, 16), ROWS)

        def differ(h):
            at = width + h // 2 * 128
            wide = wide_low if h % 2 == 0 else ~wide_low
            v = jnp.where(wide, kv_ref[window, at : at + 128], ones)
            d_ref[h % 3] = mm_nt(ga_ref[0, :, 128 * h : 128 * h + 128], v)

        def weigh(h):
            ds_ref[h % 3] = (prob_ref[0, h].astype(f32) * d_ref[h % 3]).astype(bf16)

        held = {}

        def spend(h):
            cols = slice(h // 2 * 128, h // 2 * 128 + 128)
            vcols = slice(width + h // 2 * 128, width + h // 2 * 128 + 128)
            mine = slice(h % 2 * 64, h % 2 * 64 + 64)
            ds = ds_ref[h % 3]
            if h % 2 == 0:
                held["qt"], held["gt"] = qs_ref[0, :, cols].T, gs_ref[0, :, cols].T
            held[h] = mm(ds, kv_ref[window, cols]), mm(held["qt"][mine], ds), mm(held["gt"][mine], prob_ref[0, h])
            if h % 2:
                even, odd = held.pop(h - 1), held.pop(h)
                dq = jnp.where(low, even[0], odd[0]) * (li_ref[0, :, cols] * inv_scale)
                dq_ref[pl.ds(pl.multiple_of(step * ROWS, 16), ROWS), cols] = dq.astype(bf16)
                for i, into in ((1, cols), (2, vcols)):
                    grad = jnp.concatenate([even[i], odd[i]], axis=0).T
                    acc_ref[seen, into] += grad[: 2 * ROWS]
                    acc_ref[fresh, into] = grad[2 * ROWS : 3 * ROWS]

        differ(0)
        for h in range(HEADS + 1):
            if h + 1 < HEADS:
                differ(h + 1)
            if h >= 1:
                spend(h - 1)
            if h < HEADS:
                weigh(h)

    @pl.when(step == frames - 1)
    def _():
        ghost_ref[:, :width] = (acc_ref[ghost_rows, :width] * inv_scale).astype(bf16)
        ghost_ref[:, width:] = acc_ref[ghost_rows, width:].astype(bf16)
        swap.start()
        for load in loads[3:]:
            load.wait()

    def grads_of(start, size, lo, hi):
        here = pl.ds(pl.multiple_of(start, 16), size)
        below = pl.ds(pl.multiple_of(start + ROWS, 16), size)
        parts = []
        if lo < width:
            parts.append(dq_ref[here, lo : min(hi, width)])
        if lo < 2 * width and hi > width:
            parts.append((acc_ref[below, max(lo - width, 0) : min(hi, 2 * width) - width] * inv_scale).astype(bf16))
        if hi > 2 * width:
            parts.append(acc_ref[below, max(lo, 2 * width) - width : hi - width].astype(bf16))
        return jnp.concatenate(parts, axis=1)

    @pl.when(step == frames)
    def _():
        swap.wait()
        got = got_ref[...].astype(f32)
        acc_ref[edge_rows, :width] += got[:, :width] * (1.0 / inv_scale)
        acc_ref[edge_rows, width:] += got[:, width:]

        def weights(lo, hi):
            total = 0.0
            for i in range(frames // 4):
                grads = grads_of(4 * i * ROWS, 4 * ROWS, lo, hi)
                total = total + mm_tn(ain_ref[4 * i : 4 * i + 4].reshape(4 * ROWS, width), grads)
                sq_ref[:, lo:hi] += fold8(grads.astype(f32))
            return total

        def pad(end, stop):
            if end < stop:
                own2_ref[end:stop] = jnp.zeros((stop - end, 16, 128), bf16)

        pad(pack_matrix(own2_ref, 0, weights(0, early_cols)), cut2)
        three.send(0)
        late = weights(early_cols, 3 * width)
        three.take(0)
        three.send(1)
        pad(pack_matrix(own2_ref, cut2, late), own2_ref.shape[0])
        four.send(0)

    at(norm_step + 1, (four.take, 0), (four.send, 1))
    at(norm_step + 3, (one.settle, 0), (two.settle, 1), (two.spread, 0))
    at(norm_step + 4, (three.take, 1), (three.send, 2))

    @pl.when(step == norm_step + 5)
    def _():
        two.settle(0)
        keep.start()

    at(norm_step + 7, (four.take, 1), (four.send, 2))

    @pl.when(step > frames)
    def _():
        i = step - norm_step
        block = 2 * ROWS
        x = x_ref[pl.ds(2 * i, 2)].reshape(block, width).astype(f32)
        n, inverse = normed_of(x)
        up = mm_nt(grads_of(i * block, block, 0, 3 * width), wqkv_ref[...])
        gres = gres_ref[...].reshape(block, width)
        narrow_into(in_ref, 0, gres + norm_back(up, n, inverse, row_ref[:, :width]))
        s384_ref[0] += fold8(up * n)
        s384_ref[1] += fold8(up)

    @pl.when(step == steps - 1)
    def _():
        sq = colsum(sq_ref[...])
        parts = [colsum(s384_ref[0]), colsum(s384_ref[1]), sq[:, :width], sq[:, 2 * width :]]
        lines = [v[:, c : c + 128] for v in parts for c in range(0, width, 128)]
        lines += [jnp.zeros((1, 128), f32)] * (16 - len(lines))
        rows.spread(last, jnp.concatenate(lines, axis=0))
        for i in range(2, count):
            for total in (three, four):
                total.take(i)
                if i < last:
                    total.send(i + 1)
                else:
                    total.spread(last)
        for i in range(last, 0, -1):
            tile = rows.settle(i)
            rows.spread(i - 1, tile)
            for total in (three, four):
                total.settle(i)
                total.spread(i - 1)
        rows_ref[...] = rows.settle(0)
        three.settle(0)
        four.settle(0)
        res2_ref[...] = sum2_ref[...]
        keep.wait()


def unpack_kernel(cut2, in_hbm, res_hbm, res2_ref, rows_ref, out_hbm, gg1, gb1, gqkv_hbm, gqv, gwo_hbm, gbo, gg2, gb2, gw1_hbm,
                  gbf1, gw2_hbm, gbf2, gqkv, gwo, gw1, gw2, res_ref, mid_ref, sems):
    width, hidden = gw1.shape
    tiles = width // 16
    across = hidden // 128 * tiles
    pieces = 4
    piece = in_hbm.shape[0] // pieces
    come, go = [], []
    for i in range(pieces):
        rows = slice(i * piece, (i + 1) * piece)
        come.append(pltpu.make_async_copy(in_hbm.at[rows], mid_ref.at[rows], sems.at[7 + i]))
        go.append(pltpu.make_async_copy(mid_ref.at[rows], out_hbm.at[rows], sems.at[7 + pieces + i]))
    parts = (0, across, 2 * across, res_hbm.shape[0])
    loads = [
        pltpu.make_async_copy(res_hbm.at[lo:hi], res_ref.at[lo:hi], sems.at[i])
        for i, (lo, hi) in enumerate(zip(parts, parts[1:]))
    ]
    stores = [
        pltpu.make_async_copy(src, dst, sems.at[3 + i])
        for i, (src, dst) in enumerate(((gqkv, gqkv_hbm), (gwo, gwo_hbm), (gw1, gw1_hbm), (gw2, gw2_hbm)))
    ]
    for copy in loads + come:
        copy.start()
    early = 3 * width // 128 // 2
    for c in range(3 * width // 128):
        at = c * tiles if c < early else cut2 + (c - early) * tiles
        gqkv[:, 128 * c : 128 * c + 128] = res2_ref[at : at + tiles].reshape(width, 128).astype(f32)
    stores[0].start()
    loads[0].wait()
    at = 0
    for c in range(hidden // 128):
        gw1[:, 128 * c : 128 * c + 128] = res_ref[at : at + tiles].reshape(width, 128).astype(f32)
        at += tiles
    stores[2].start()
    for i in range(pieces):
        come[i].wait()
        go[i].start()
    loads[1].wait()
    for c in range(hidden // 128):
        gw2[128 * c : 128 * c + 128, :] = res_ref[at : at + tiles].reshape(width, 128).astype(f32).T
        at += tiles
    stores[3].start()
    loads[2].wait()
    for c in range(width // 128):
        gwo[:, 128 * c : 128 * c + 128] = res_ref[at : at + tiles].reshape(width, 128).astype(f32)
        at += tiles
    stores[1].start()
    row = 0
    for out in (gg2, gb2, gbo, gbf2, gbf1):
        for c in range(out.shape[0] // 128):
            out[128 * c : 128 * c + 128] = res_ref[at + row // 16].astype(f32)[row % 16]
            row += 1
    rows = rows_ref[...]
    each = width // 128
    for i, out in enumerate((gg1, gb1)):
        for c in range(each):
            out[128 * c : 128 * c + 128] = rows[i * each + c]
    for i in range(2):
        for c in range(each):
            gqv[i : i + 1, 128 * c : 128 * c + 128] = rows[(i + 2) * each + c : (i + 2) * each + c + 1]
    for copy in stores + go:
        copy.wait()


def whole(shape):
    return pl.BlockSpec(shape, lambda i: (0,) * len(shape), pipeline_mode=pl.Buffered(1))


def pairs(shape):
    return pl.BlockSpec((2,) + shape, lambda i: (i,) + (0,) * len(shape))


def single(shape):
    return pl.BlockSpec((1,) + shape, lambda i: (i,) + (0,) * len(shape))


def params(collective=None):
    if collective is None:
        return pltpu.CompilerParams(vmem_limit_bytes=60 * 2**20)
    return pltpu.CompilerParams(vmem_limit_bytes=60 * 2**20, collective_id=collective, has_side_effects=True)


def per_device(tokens, frame_clip, ln1_gain, ln1_bias, w_qkv, qv_bias, w_out, b_out, ln2_gain, ln2_bias,
               w_fc1, b_fc1, w_fc2, b_fc2, cotangent):
    count, width = tokens.shape
    hidden = w_fc1.shape[1]
    frames = count // FRAME
    steps = frames // 2
    tm = lax.axis_index("tm")
    edge = jnp.where(tm == 0, tokens[count - ROWS :], tokens[:ROWS])
    ghost = lax.ppermute(edge, "tm", [(0, 1), (1, 0)])
    in_vmem = pl.BlockSpec(memory_space=pltpu.VMEM)
    in_hbm = pl.BlockSpec(memory_space=pl.ANY)
    kv_rows = (frames + 2) * ROWS + WIN - 3 * ROWS
    shape = jax.ShapeDtypeStruct
    stages = stages_of(lax.axis_size("clips"))
    devices = 2 * lax.axis_size("clips")
    tiles = width // 16
    units = units_for((2 * hidden + width) // 128 * tiles + 2, devices)
    across2 = 3 * width // 128
    first2 = units_for(across2 // 2 * tiles, devices)
    second2 = units_for((across2 - across2 // 2) * tiles, devices)
    units2 = first2 + second2
    x_pad, ain, kv, prob, block_out, qs, ga, gs, gres, li, row, pack = pl.pallas_call(
        forward_kernel,
        grid=(steps,),
        in_specs=[
            pl.BlockSpec(memory_space=pltpu.SMEM),
            whole((count, width)),
            whole((ROWS, width)),
            whole((width,)),
            whole((width,)),
            whole((2, width)),
            whole((width,)),
            whole((width,)),
            whole((width,)),
            whole((hidden,)),
            whole((width,)),
            whole((width, 3 * width)),
            in_hbm,
            in_hbm,
            in_hbm,
            in_hbm,
        ],
        out_specs=[
            in_hbm,
            in_hbm,
            in_hbm,
            pairs((HEADS, ROWS, WIN)),
            pl.BlockSpec((4 * FRAME, width), lambda i: (i // 2, 0)),
            pairs((ROWS, width)),
            pairs((ROWS, 2 * width)),
            pairs((ROWS, width)),
            pairs((ROWS, width)),
            pairs((ROWS, width)),
            whole((1, 9 * width + hidden)),
            whole((units, 16, 128)),
        ],
        out_shape=[
            shape((frames, ROWS, width), bf16),
            shape((frames, ROWS, width), bf16),
            shape((kv_rows, 2 * width), bf16),
            shape((frames, HEADS, ROWS, WIN), bf16),
            shape((count, width), bf16),
            shape((frames, ROWS, width), bf16),
            shape((frames, ROWS, 2 * width), bf16),
            shape((frames, ROWS, width), bf16),
            shape((frames, ROWS, width), f32),
            shape((frames, ROWS, width), f32),
            shape((1, 9 * width + hidden), f32),
            shape((units, 16, 128), bf16),
        ],
        scratch_shapes=[
            pltpu.VMEM((frames, ROWS, width), bf16),
            pltpu.VMEM((frames, ROWS, width), bf16),
            pltpu.VMEM((kv_rows, 2 * width), bf16),
            pltpu.VMEM((count, width), bf16),
            pltpu.VMEM((width, width), bf16),
            pltpu.VMEM((width, hidden), bf16),
            pltpu.VMEM((hidden, width), bf16),
            pltpu.VMEM((frames, ROWS, width), bf16),
            pltpu.VMEM((frames, ROWS, width), bf16),
            pltpu.VMEM((kv_rows, 128), bf16),
            pltpu.VMEM((3, ROWS, WIN), f32),
            pltpu.VMEM((2 * ROWS, width), f32),
            pltpu.VMEM((4 * FRAME, width), f32),
            pltpu.VMEM((width, hidden), f32),
            pltpu.VMEM((width, hidden), f32),
            pltpu.VMEM((width, width), f32),
            pltpu.VMEM((8, hidden), f32),
            pltpu.VMEM((4, 8, width), f32),
            pltpu.SemaphoreType.DMA((7,)),
        ],
        compiler_params=params(),
    )(frame_clip, tokens, ghost, ln1_gain, ln1_bias, qv_bias, b_out, ln2_gain, ln2_bias, b_fc1, b_fc2, w_qkv, cotangent,
      w_out, w_fc1, w_fc2)

    first, second = halves(units, devices)
    early = lambda sh: pl.BlockSpec((1,) + sh, lambda i: (jnp.minimum(i, frames - 1),) + (0,) * len(sh))
    late = lambda i: jnp.maximum(i - frames - 1, 0)
    input_grad, res, res2, sums = pl.pallas_call(
        functools.partial(back_kernel, stages),
        grid=(frames + 1 + steps,),
        in_specs=[
            early((HEADS, ROWS, WIN)),
            in_hbm,
            early((ROWS, 2 * width)),
            early((ROWS, width)),
            early((ROWS, width)),
            early((ROWS, width)),
            in_hbm,
            in_hbm,
            pl.BlockSpec((2, ROWS, width), lambda i: (late(i), 0, 0)),
            whole(row.shape),
            in_hbm,
            in_hbm,
        ],
        out_specs=[
            pl.BlockSpec((2 * FRAME, width), lambda i: (late(i), 0)),
            in_hbm,
            whole((units2, 16, 128)),
            whole((16, 128)),
        ],
        out_shape=[
            shape((count, width), f32),
            shape((units, 16, 128), bf16),
            shape((units2, 16, 128), bf16),
            shape((16, 128), f32),
        ],
        scratch_shapes=[
            pltpu.VMEM((kv_rows, 2 * width), f32),
            pltpu.VMEM((3, ROWS, WIN), f32),
            pltpu.VMEM((3, ROWS, WIN), bf16),
            pltpu.VMEM((frames * ROWS, width), bf16),
            pltpu.VMEM((8, 3 * width), f32),
            pltpu.VMEM((2, 8, width), f32),
            pltpu.VMEM((units, 16, 128), bf16),
            pltpu.VMEM((units, 16, 128), bf16),
            pltpu.VMEM((units2, 16, 128), bf16),
            pltpu.VMEM((units2, 16, 128), bf16),
            pltpu.VMEM((ROWS, 2 * width), bf16),
            pltpu.VMEM((ROWS, 2 * width), bf16),
            pltpu.VMEM((kv_rows, 2 * width), bf16),
            pltpu.VMEM((frames, ROWS, width), bf16),
            pltpu.VMEM((frames, ROWS, width), bf16),
            pltpu.VMEM((width, 3 * width), bf16),
            pltpu.SemaphoreType.DMA((2,)),
            pltpu.SemaphoreType.DMA((7,)),
        ]
        + sum_scratch(stages, first)
        + sum_scratch(stages, second)
        + sum_scratch(stages, first2)
        + sum_scratch(stages, second2)
        + rows_scratch(stages),
        compiler_params=params(0),
    )(prob, kv, ga, gs, qs, li, x_pad, ain, gres, row, w_qkv, pack)

    sizes = [(width,), (width,), (width, 3 * width), (2, width), (width, width), (width,), (width,), (width,),
             (width, hidden), (hidden,), (hidden, width), (width,)]
    big = [len(z) == 2 and z[0] > 2 for z in sizes]
    outs = pl.pallas_call(
        functools.partial(unpack_kernel, first2),
        in_specs=[in_hbm, in_hbm, in_vmem, in_vmem],
        out_specs=[in_hbm] + [in_hbm if far else in_vmem for far in big],
        out_shape=[shape((count, width), f32)] + [shape(z, f32) for z in sizes],
        scratch_shapes=[
            pltpu.VMEM((width, 3 * width), f32),
            pltpu.VMEM((width, width), f32),
            pltpu.VMEM((width, hidden), f32),
            pltpu.VMEM((hidden, width), f32),
            pltpu.VMEM((units, 16, 128), bf16),
            pltpu.VMEM((count, width), f32),
            pltpu.SemaphoreType.DMA((15,)),
        ],
        compiler_params=params(),
    )(input_grad, res, res2, sums)
    return (block_out,) + tuple(outs)


def solution(mesh):
    rows = P(("clips", "tm"), None)
    rep = P()
    return jax.shard_map(
        per_device,
        mesh=mesh,
        in_specs=(rows, P("clips")) + (rep,) * 12 + (rows,),
        out_specs=(rows, rows) + (rep,) * 12,
        check_vma=False,
    )
```

```python
import functools
import math

import jax
import jax.numpy as jnp
from jax import lax
from jax.experimental import pallas as pl
from jax.experimental.pallas import tpu as pltpu
from jax.sharding import PartitionSpec as P

HEADS = 6
FRAME = 196
ROWS = 208
WIN = 640
EXTRA = 16
EPS = 1e-6
LOG2E = math.log2(math.e)

bf16 = jnp.bfloat16
f32 = jnp.float32


def mm(a, b):
    return jnp.dot(a, b, preferred_element_type=f32)


def mm_nt(a, b):
    return lax.dot_general(a, b, (((1,), (1,)), ((), ())), preferred_element_type=f32)


def mm_tn(a, b):
    return lax.dot_general(a, b, (((0,), (0,)), ((), ())), preferred_element_type=f32)


def normed_of(x):
    mean = jnp.mean(x, axis=-1, keepdims=True)
    centred = x - mean
    var = jnp.mean(centred * centred, axis=-1, keepdims=True)
    inverse = lax.rsqrt(var + EPS)
    return centred * inverse, inverse


def norm_back(upstream, normed, inverse, gain):
    scaled = upstream * gain
    mean = jnp.mean(scaled, axis=-1, keepdims=True)
    along = jnp.mean(scaled * normed, axis=-1, keepdims=True)
    return inverse * (scaled - mean - normed * along)


def fold8(v):
    rows, cols = v.shape
    return jnp.sum(v.reshape(rows // 8, 8, cols), axis=0)


MESH = pl.DeviceIdType.MESH


def stages_of(clips):
    stages, stride = [("tm", 1, 2)], 1
    while clips > 1:
        size = 4 if clips % 4 == 0 else (2 if clips % 2 == 0 else clips)
        stages.append(("clips", stride, size))
        stride, clips = stride * size, clips // size
    return stages


def digit(stage):
    axis, stride, size = stage
    return lax.rem(lax.axis_index(axis) // stride, size)


def partner(stage, turn):
    axis, stride, size = stage
    mine = digit(stage)
    return {axis: lax.axis_index(axis) + (lax.rem(mine + turn, size) - mine) * stride}


def greet(stages):
    sem, count = pltpu.get_barrier_semaphore(), 0
    for stage in stages:
        for turn in range(1, stage[2]):
            pl.semaphore_signal(sem, inc=1, device_id=partner(stage, turn), device_id_type=MESH)
            count += 1
    pl.semaphore_wait(sem, count)


class Sum:
    def __init__(self, stages, pack, result, landing, sent, came):
        self.stages, self.pack, self.result, self.landing = stages, pack, result, landing
        self.sent, self.came = sent, came
        self.segments, start, length = [], 0, pack.shape[0]
        for stage in stages:
            self.segments.append((start, length))
            length = length // stage[2]
            start = start + digit(stage) * length
        self.segments.append((start, length))
        self.first = [sum(s[2] - 1 for s in stages[:i]) for i in range(len(stages) + 1)]

    def _scatter(self, i):
        stage, (start, length) = self.stages[i], self.segments[i]
        part = length // stage[2]
        for turn in range(1, stage[2]):
            slot = self.first[i] + turn - 1
            other = lax.rem(digit(stage) + turn, stage[2])
            yield pltpu.make_async_remote_copy(
                src_ref=self.pack.at[pl.ds(start + other * part, part)],
                dst_ref=self.landing[i].at[turn - 1],
                send_sem=self.sent.at[slot],
                recv_sem=self.came.at[slot],
                device_id=partner(stage, turn),
                device_id_type=MESH,
            )

    def _gather(self, i):
        stage, (start, length) = self.stages[i], self.segments[i + 1]
        for turn in range(1, stage[2]):
            slot = self.first[-1] + self.first[i] + turn - 1
            here = self.result.at[pl.ds(start, length)]
            yield pltpu.make_async_remote_copy(
                src_ref=here,
                dst_ref=here,
                send_sem=self.sent.at[slot],
                recv_sem=self.came.at[slot],
                device_id=partner(stage, turn),
                device_id_type=MESH,
            )

    def send(self, i):
        for copy in self._scatter(i):
            copy.start()

    def take(self, i):
        for copy in self._scatter(i):
            copy.wait()
        start, length = self.segments[i + 1]
        into = self.result if i == len(self.stages) - 1 else self.pack
        block = next(b for b in (28, 24, 21, 16, 14, 12, 8, 7, 6, 4, 3, 2, 1) if length % b == 0)

        def add(j, carry):
            total = self.pack[pl.ds(start + j * block, block)].astype(f32)
            for turn in range(1, self.stages[i][2]):
                total = total + self.landing[i][turn - 1, pl.ds(j * block, block)].astype(f32)
            into[pl.ds(start + j * block, block)] = total.astype(bf16)
            return carry

        lax.fori_loop(0, length // block, add, 0)

    def spread(self, i):
        for copy in self._gather(i):
            copy.start()

    def settle(self, i):
        for copy in self._gather(i):
            copy.wait()


def sum_scratch(stages, units):
    shapes, left = [], units
    for stage in stages:
        left //= stage[2]
        shapes.append(pltpu.VMEM((stage[2] - 1, left, 16, 128), bf16))
    copies = 2 * sum(s[2] - 1 for s in stages)
    return shapes + [pltpu.SemaphoreType.DMA((copies,)), pltpu.SemaphoreType.DMA((copies,))]


def pack_matrix(pack, first, value):
    rows, cols = value.shape
    tiles = rows // 16
    for c in range(cols // 128):
        pack[first + c * tiles : first + (c + 1) * tiles] = (
            value[:, 128 * c : 128 * (c + 1)].astype(bf16).reshape(tiles, 16, 128)
        )
    return first + cols // 128 * tiles


def pack_rows(pack, first, vectors):
    rows = [v[:, c : c + 128] for v in vectors for c in range(0, v.shape[1], 128)]
    rows += [jnp.zeros((1, 128), f32)] * (-len(rows) % 16)
    for r in range(0, len(rows), 16):
        pack[first + r // 16] = jnp.concatenate(rows[r : r + 16], axis=0).astype(bf16)
    last = first + len(rows) // 16
    if last < pack.shape[0]:
        pack[last:] = jnp.zeros((pack.shape[0] - last, 16, 128), bf16)


def unpack_matrix(res, first, rows, cols):
    tiles = rows // 16
    part = res[first : first + cols // 128 * tiles].reshape(cols // 128, tiles, 16, 128)
    return part.transpose(1, 2, 0, 3).reshape(rows, cols).astype(f32)


def units_for(needed, devices):
    return -(-needed // devices) * devices


def colsum(v):
    return jnp.sum(v, axis=0, keepdims=True)


def widen(ref, group, which):
    start = which * FRAME // 16 * 16
    shift = which * FRAME - start
    v = ref[pl.ds(pl.multiple_of(group * 4 * FRAME + start, 16), ROWS), :].astype(f32)
    if shift:
        v = pltpu.roll(v, ROWS - shift, 0)
    row = lax.broadcasted_iota(jnp.int32, (16, v.shape[1]), 0)
    return v, jnp.where(row < 16 - (ROWS - FRAME), v[ROWS - 16 :], 0.0)


def narrow_into(ref, start, v):
    edge = FRAME // 8 * 8
    over = FRAME - edge
    second = pltpu.roll(v[ROWS:], over, 0)
    row = lax.broadcasted_iota(jnp.int32, (8, v.shape[1]), 0)
    ref[pl.ds(pl.multiple_of(start, 8), edge), :] = v[:edge]
    ref[pl.ds(pl.multiple_of(start + edge, 8), 8), :] = jnp.where(row < over, v[edge : edge + 8], second[:8])
    rest = 2 * FRAME - edge - 8
    ref[pl.ds(pl.multiple_of(start + edge + 8, 8), rest), :] = second[8 : 8 + rest]


def forward_kernel(
    clip_ref,
    tok_hbm,
    ghost_ref,
    g1_ref,
    s1_ref,
    qv_ref,
    bo_ref,
    g2_ref,
    s2_ref,
    bf1_ref,
    bf2_ref,
    wqkv_ref,
    cot_hbm,
    wout_hbm,
    w1_hbm,
    w2_hbm,
    x_hbm,
    ain_hbm,
    kv_hbm,
    prob_ref,
    out_ref,
    qs_ref,
    ga_ref,
    gs_ref,
    gres_ref,
    li_ref,
    row_ref,
    pack_ref,
    x_ref,
    ain_ref,
    kv_ref,
    raw_ref,
    wout_ref,
    w1_ref,
    w2_ref,
    q_ref,
    cp_ref,
    flag_ref,
    s_ref,
    o_ref,
    flat_ref,
    gw1_ref,
    gw2_ref,
    gwo_ref,
    sb1_ref,
    s384_ref,
    sems,
):
    step = pl.program_id(0)
    steps = pl.num_programs(0)
    frames = x_ref.shape[0]
    width = x_ref.shape[-1]
    hidden = w1_ref.shape[-1]
    tm = lax.axis_index("tm")
    copies = [
        pltpu.make_async_copy(src, dst, sems.at[i])
        for i, (src, dst) in enumerate(
            ((cot_hbm, raw_ref), (wout_hbm, wout_ref), (w1_hbm, w1_ref), (w2_hbm, w2_ref), (x_ref, x_hbm), (kv_ref, kv_hbm),
             (ain_ref, ain_hbm), (tok_hbm, raw_ref))
        )
    ]

    @pl.when(step == 0)
    def _():
        copies[7].start()
        for copy in copies[1:4]:
            copy.start()
        vectors = [g1_ref[...], s1_ref[...], None, None, None, bo_ref[...], g2_ref[...], s2_ref[...], bf2_ref[...]]
        for i, v in enumerate(vectors):
            if v is not None:
                row_ref[:, i * width : (i + 1) * width] = v.astype(f32)[None, :]
        row_ref[:, 2 * width : 3 * width] = qv_ref[0:1, :].astype(f32)
        row_ref[:, 3 * width : 4 * width] = jnp.zeros((1, width), f32)
        row_ref[:, 4 * width : 5 * width] = qv_ref[1:2, :].astype(f32)
        row_ref[:, 9 * width :] = bf1_ref[...].astype(f32)[None, :]

    vec = lambda i, n=width: row_ref[:, i * width : i * width + n]
    gain1, shift1, bias3, biaso, gain2, shift2, bias2, bias1 = (
        vec(0), vec(1), vec(2, 3 * width), vec(5), vec(6), vec(7), vec(8), vec(9, hidden))

    @pl.when(step == 0)
    def _():
        gw1_ref[...] = jnp.zeros_like(gw1_ref)
        gw2_ref[...] = jnp.zeros_like(gw2_ref)
        gwo_ref[...] = jnp.zeros_like(gwo_ref)
        sb1_ref[...] = jnp.zeros_like(sb1_ref)
        s384_ref[...] = jnp.zeros_like(s384_ref)
        at = lax.broadcasted_iota(jnp.int32, flag_ref.shape, 0)
        lane = lax.broadcasted_iota(jnp.int32, flag_ref.shape, 1)
        slot = at // ROWS
        flag_ref[...] = jnp.where(
            lane == 0,
            jnp.where(at - slot * ROWS < FRAME, 0.0, -1e30),
            jnp.where(lane == 1 + slot % 4, 1.0, 0.0),
        ).astype(bf16)
        zero_slot = jnp.where(tm == 0, 0, frames + 1)
        ghost_slot = frames + 1 - zero_slot
        kv_ref[pl.ds(pl.multiple_of(zero_slot * ROWS, 16), ROWS), :] = jnp.zeros((ROWS, 2 * width), bf16)
        kv_ref[(frames + 2) * ROWS :, :] = jnp.zeros((WIN - 3 * ROWS, 2 * width), bf16)

        x = ghost_ref[...].astype(f32)
        x = jnp.where(tm == 0, x, pltpu.roll(x, FRAME, 0))
        n, _ = normed_of(x)
        kv = mm((n * gain1 + shift1).astype(bf16), wqkv_ref[:, width:]) + bias3[:, width:]
        kv_ref[pl.ds(pl.multiple_of(ghost_slot * ROWS, 16), ROWS), :] = kv.astype(bf16)

        def pad(i, src, dst):
            for which in range(4):
                v, end = widen(src, i, which)
                dst[4 * i + which, : ROWS - 16] = v[: ROWS - 16].astype(bf16)
                dst[4 * i + which, ROWS - 16 :] = end.astype(bf16)

        def ready(i):
            x = x_ref[4 * i : 4 * i + 4].reshape(4 * ROWS, width).astype(f32)
            n, _ = normed_of(x)
            normed = (n * gain1 + shift1).astype(bf16)
            ain_ref[4 * i : 4 * i + 4] = normed.reshape(4, ROWS, width)
            return normed

        def project(i, normed):
            qkv = (mm(normed, wqkv_ref[...]) + bias3).astype(bf16)
            q_ref[4 * i : 4 * i + 4] = qkv[:, :width].reshape(4, ROWS, width)
            kv_ref[(4 * i + 1) * ROWS : (4 * i + 5) * ROWS, :] = qkv[:, width:]

        copies[7].wait()
        for i in range(frames // 4):
            pad(i, raw_ref, x_ref)
        copies[0].start()
        normed = ready(0)
        for i in range(frames // 4):
            following = ready(i + 1) if i + 1 < frames // 4 else None
            project(i, normed)
            normed = following
        for copy in copies[4:7]:
            copy.start()
        for copy in copies[:4]:
            copy.wait()
        for i in range(frames // 4):
            pad(i, raw_ref, cp_ref)

    low = lax.broadcasted_iota(jnp.int32, (ROWS, 128), 1) < 64
    lane = lax.broadcasted_iota(jnp.int32, (1, 128), 1)
    scale = LOG2E / math.sqrt(width // HEADS)
    twins = HEADS // 2
    flags, windows = [], []
    for sub in range(2):
        frame = 2 * step + sub
        here = tm * frames + frame
        own = clip_ref[here]
        before = jnp.where(here > 0, clip_ref[jnp.maximum(here - 1, 0)], -1)
        after = jnp.where(here < 2 * frames - 1, clip_ref[jnp.minimum(here + 1, 2 * frames - 1)], -1)
        none = jnp.float32(-1e30)
        row = jnp.where(lane == 0, 1.0, 0.0)
        row = jnp.where(lane == 1 + frame % 4, jnp.where(before == own, 0.0, none), row)
        row = jnp.where(lane == 1 + (frame + 2) % 4, jnp.where(after == own, 0.0, none), row)
        row = jnp.where(lane == 1 + (frame + 3) % 4, none, row)
        flags.append(jnp.broadcast_to(row.astype(bf16), (2 * ROWS, 128))[:, :EXTRA])
        windows.append(pl.ds(pl.multiple_of(frame * ROWS, 16), WIN))

    def score(t):
        sub, pair = divmod(t, twins)
        cols = slice(pair * 128, pair * 128 + 128)
        q = q_ref[2 * step + sub, :, cols]
        zero = jnp.zeros_like(q)
        both = jnp.concatenate([jnp.where(low, q, zero), jnp.where(low, zero, q)], axis=0)
        k = jnp.concatenate([kv_ref[windows[sub], cols], flag_ref[windows[sub], :EXTRA]], axis=1)
        s_ref[t % 3] = mm_nt(jnp.concatenate([both, flags[sub]], axis=1), k)

    inverses = {}

    def soften(t):
        sub, pair = divmod(t, twins)
        s = s_ref[t % 3]
        top = jnp.max(s, axis=-1, keepdims=True)
        e = jnp.exp2((s - top) * scale)
        inverses[t] = 1.0 / jnp.sum(e, axis=-1, keepdims=True)
        prob_ref[sub, pair] = e.astype(bf16)

    def attend(t):
        sub, pair = divmod(t, twins)
        at = pair * 128
        o = mm(prob_ref[sub, pair], kv_ref[windows[sub], width + at : width + at + 128])
        inverse = jnp.where(low, inverses[t][:ROWS], inverses[t][ROWS:])
        rows = slice(sub * ROWS, (sub + 1) * ROWS)
        o_ref[rows, at : at + 128] = jnp.where(low, o[:ROWS], o[ROWS:]) * inverse
        li_ref[sub, :, at : at + 128] = inverse

    score(0)
    for t in range(2 * twins + 1):
        if t + 1 < 2 * twins:
            score(t + 1)
        if t >= 1:
            attend(t - 1)
        if t < 2 * twins:
            soften(t)

    att = o_ref[...].astype(bf16)
    both = pl.ds(2 * step, 2)
    x = x_ref[both].reshape(2 * ROWS, width).astype(f32)
    resid = x + mm(att, wout_ref[...]) + biaso
    n2, inv2 = normed_of(resid)
    mlp_in = (n2 * gain2 + shift2).astype(bf16)
    cot = cp_ref[both].reshape(2 * ROWS, width)
    chunk = 512
    chunks = [slice(c, c + chunk) for c in range(0, hidden, chunk)]
    held = {}

    def start(c):
        held[c] = mm(mlp_in, w1_ref[:, chunks[c]]), mm_nt(cot, w2_ref[chunks[c], :])

    def middle(c):
        pre, ghid = held[c]
        pre = pre + bias1[:, chunks[c]]
        cdf = 0.5 + 0.5 * lax.erf(pre * (1.0 / math.sqrt(2.0)))
        dens = jnp.exp2(pre * pre * (-0.5 * LOG2E)) * (1.0 / math.sqrt(2.0 * math.pi))
        gpre = (ghid * (cdf + pre * dens)).astype(bf16)
        sb1_ref[:, chunks[c]] += fold8(gpre.astype(f32))
        held[c] = (pre * cdf).astype(bf16), gpre

    def weights(c):
        gw2_ref[:, chunks[c]] += mm_tn(cot, held[c][0])
        gw1_ref[:, chunks[c]] += mm_tn(mlp_in, held[c][1])

    start(0)
    for c in range(len(chunks)):
        if c + 1 < len(chunks):
            start(c + 1)
        middle(c)
    hid = jnp.concatenate([held[c][0] for c in range(len(chunks))], axis=1)
    gpre = jnp.concatenate([held[c][1] for c in range(len(chunks))], axis=1)
    up = mm_nt(gpre, w1_ref[...])
    cot32 = cot.astype(f32)
    gres = cot32 + norm_back(up, n2, inv2, gain2)
    gres_ref[...] = gres.reshape(2, ROWS, width)
    branch = gres.astype(bf16)
    weights(0)
    g = mm_nt(branch, wout_ref[...]).astype(bf16)
    for c in range(1, len(chunks) - 1):
        weights(c)
    g32 = g.astype(f32)
    inverse = li_ref[...].reshape(2 * ROWS, width)
    gs_ref[...] = (g32 * inverse).astype(bf16).reshape(2, ROWS, width)
    qs_ref[...] = (q_ref[both].reshape(2 * ROWS, width).astype(f32) * inverse).astype(bf16).reshape(2, ROWS, width)
    dots = g32 * o_ref[...]
    some = lax.broadcasted_iota(jnp.int32, (2 * ROWS, EXTRA), 1)
    for sub in range(2):
        for pair in range(twins):
            rows, cols = slice(sub * ROWS, (sub + 1) * ROWS), slice(128 * pair, 128 * pair + 128)
            d = dots[rows, cols]
            even = jnp.sum(jnp.where(low, d, 0.0), axis=-1, keepdims=True)
            odd = jnp.sum(jnp.where(low, 0.0, d), axis=-1, keepdims=True)
            less = jnp.broadcast_to(-jnp.concatenate([even, odd], axis=0), (2 * ROWS, EXTRA))
            one = less.astype(bf16).astype(f32)
            two = (less - one).astype(bf16).astype(f32)
            three = less - one - two
            ga_ref[sub, pair, :, 128 : 128 + EXTRA] = jnp.where(
                some == 0, one, jnp.where(some == 1, two, jnp.where(some == 2, three, 0.0))
            ).astype(bf16)
            gp = g[rows, cols]
            zero = jnp.zeros_like(gp)
            ga_ref[sub, pair, :ROWS, :128] = jnp.where(low, gp, zero)
            ga_ref[sub, pair, ROWS:, :128] = jnp.where(low, zero, gp)
    s384_ref[0] += fold8(up * n2)
    s384_ref[1] += fold8(up)
    s384_ref[2] += fold8(branch.astype(f32))
    s384_ref[3] += fold8(cot32)
    weights(len(chunks) - 1)
    gwo_ref[...] += mm_tn(att, branch)
    out = resid + bias2 + mm(hid, w2_ref[...])
    narrow_into(flat_ref, step % 2 * 2 * FRAME, out)

    @pl.when(step % 2 == 1)
    def _():
        out_ref[...] = flat_ref[...].astype(bf16)

    @pl.when(step == steps - 1)
    def _():
        at = pack_matrix(pack_ref, 0, gw1_ref[...])
        at = pack_matrix(pack_ref, at, gw2_ref[...])
        at = pack_matrix(pack_ref, at, gwo_ref[...])
        pack_rows(pack_ref, at, [colsum(s384_ref[i]) for i in range(4)] + [colsum(sb1_ref[...])])
        for copy in copies[4:7]:
            copy.wait()


class Rows:
    def __init__(self, stages, boards, sent, came):
        self.stages, self.boards, self.sent, self.came = stages, boards, sent, came
        self.first = [sum(s[2] - 1 for s in stages[:i]) for i in range(len(stages) + 1)]

    def _copies(self, i):
        stage = self.stages[i]
        here = self.boards[i].at[digit(stage)]
        for turn in range(1, stage[2]):
            slot = self.first[i] + turn - 1
            yield pltpu.make_async_remote_copy(
                src_ref=here,
                dst_ref=here,
                send_sem=self.sent.at[slot],
                recv_sem=self.came.at[slot],
                device_id=partner(stage, turn),
                device_id_type=MESH,
            )

    def spread(self, i, tile):
        self.boards[i][digit(self.stages[i])] = tile
        for copy in self._copies(i):
            copy.start()

    def settle(self, i):
        for copy in self._copies(i):
            copy.wait()
        total = self.boards[i][0]
        for j in range(1, self.stages[i][2]):
            total = total + self.boards[i][j]
        return total


def rows_scratch(stages):
    copies = sum(s[2] - 1 for s in stages)
    return [pltpu.VMEM((s[2], 16, 128), f32) for s in stages] + [pltpu.SemaphoreType.DMA((copies,))] * 2


def shares(units, devices):
    blocks = units // devices
    side = max(1, round(blocks / 7))
    first = -(-(blocks - side) // 2)
    return first * devices, (blocks - side - first) * devices, side * devices


def turned(stages):
    return stages[:1] + stages[:0:-1]


def back_kernel(stages, prob_ref, kv_hbm, ga_ref, gs_ref, qs_ref, li_ref, x_hbm, ain_hbm, gres_ref, row_ref,
                wqkv_hbm, pack_hbm, in_ref, res_hbm, res2_ref, rows_ref,
                acc_ref, d_ref, ds_ref, dq_ref, sq_ref, s384_ref, own_ref, sum_ref, own2_ref, sum2_ref,
                ghost_ref, got_ref, kv_ref, x_ref, ain_ref, wqkv_ref, ghost_sems, load_sems, *rest):
    step = pl.program_id(0)
    width = gs_ref.shape[-1]
    frames = x_hbm.shape[0]
    steps = frames + 1 + frames // 2
    tm = lax.axis_index("tm")
    inv_scale = 1.0 / math.sqrt(width // HEADS)
    count = len(stages)
    last = count - 1
    devices = 2
    for stage in stages[1:]:
        devices *= stage[2]
    first, second, _ = shares(own_ref.shape[0], devices)
    both = first + second
    tiles = width // 16
    early_cols = 3 * width // 128 // 2 * 128
    cut2 = units_for(early_cols // 128 * tiles, devices)
    sums = []
    for n, (route, own, res) in enumerate(
        (
            (stages, own_ref.at[:first], sum_ref.at[:first]),
            (stages, own_ref.at[first:both], sum_ref.at[first:both]),
            (turned(stages), own_ref.at[both:], sum_ref.at[both:]),
            (stages, own2_ref.at[:cut2], sum2_ref.at[:cut2]),
            (stages, own2_ref.at[cut2:], sum2_ref.at[cut2:]),
        )
    ):
        mine = rest[n * (count + 2) : (n + 1) * (count + 2)]
        sums.append(Sum(route, own, res, mine[:count], *mine[count:]))
    one, two, side, three, four = sums
    extra = rest[5 * (count + 2) :]
    rows = Rows(stages, extra[:count], *extra[count:])
    near = 6 * ROWS
    loads = [
        pltpu.make_async_copy(src, dst, load_sems.at[i])
        for i, (src, dst) in enumerate(
            (
                (pack_hbm, own_ref),
                (kv_hbm.at[:near], kv_ref.at[:near]),
                (kv_hbm.at[near:], kv_ref.at[near:]),
                (x_hbm, x_ref),
                (ain_hbm, ain_ref),
                (wqkv_hbm, wqkv_ref),
            )
        )
    ]
    keep = pltpu.make_async_copy(sum_ref, res_hbm, load_sems.at[6])
    swap = pltpu.make_async_remote_copy(
        src_ref=ghost_ref,
        dst_ref=got_ref,
        send_sem=ghost_sems.at[0],
        recv_sem=ghost_sems.at[1],
        device_id=partner(stages[0], 1),
        device_id_type=MESH,
    )

    @pl.when(step == 0)
    def _():
        for load in loads:
            load.start()
        greet(stages)
        acc_ref[: 2 * ROWS] = jnp.zeros((2 * ROWS, 2 * width), f32)
        sq_ref[...] = jnp.zeros_like(sq_ref)
        s384_ref[...] = jnp.zeros_like(s384_ref)
        loads[0].wait()
        one.send(0)
        side.send(0)
        two.send(0)
        loads[1].wait()

    @pl.when(step == 1)
    def _():
        loads[2].wait()

    def at(when, *todo):
        @pl.when(step == when)
        def _():
            for act, i in todo:
                act(i)

    def scatter(total):
        return [t for i in range(1, last) for t in ((total.take, i), (total.send, i + 1))]

    def gather(total):
        return [t for i in range(last, 1, -1) for t in ((total.settle, i), (total.spread, i - 1))]

    norm_step = frames + 1
    at(1, (one.take, 0), (one.send, 1), (side.take, 0), (side.send, 1), (two.take, 0))
    at(4, (two.send, 1), *scatter(side))
    at(6, *scatter(one))
    at(8, *scatter(two), (side.take, last), (side.spread, last))
    at(9, (one.take, last), (one.spread, last))
    at(10, *gather(side))
    at(11, (two.take, last), (two.spread, last))
    at(13, *gather(one))
    at(15, *gather(two), (side.settle, 1), (side.spread, 0))

    low = lax.broadcasted_iota(jnp.int32, (ROWS, 128), 1) < 64
    ones = jnp.ones((WIN, EXTRA), bf16)
    edge_rows = pl.ds(pl.multiple_of(jnp.where(tm == 0, frames, 1) * ROWS, 16), ROWS)
    ghost_rows = pl.ds(pl.multiple_of(jnp.where(tm == 0, frames + 1, 0) * ROWS, 16), ROWS)

    @pl.when(step < frames)
    def _():
        window = pl.ds(pl.multiple_of(step * ROWS, 16), WIN)
        seen = pl.ds(pl.multiple_of(step * ROWS, 16), 2 * ROWS)
        fresh = pl.ds(pl.multiple_of((step + 2) * ROWS, 16), ROWS)

        def differ(t):
            at = width + t * 128
            v = jnp.concatenate([kv_ref[window, at : at + 128], ones], axis=1)
            d_ref[t % 3] = mm_nt(ga_ref[0, t], v)

        def weigh(t):
            ds_ref[t % 3] = (prob_ref[0, t].astype(f32) * d_ref[t % 3]).astype(bf16)

        def spend(t):
            cols = slice(t * 128, t * 128 + 128)
            vcols = slice(width + t * 128, width + t * 128 + 128)
            ds = ds_ref[t % 3]
            dq = mm(ds, kv_ref[window, cols])
            dq = jnp.where(low, dq[:ROWS], dq[ROWS:]) * (li_ref[0, :, cols] * inv_scale)
            dq_ref[pl.ds(pl.multiple_of(step * ROWS, 16), ROWS), cols] = dq.astype(bf16)
            prob = prob_ref[0, t]
            for left, right, into in ((qs_ref, ds, cols), (gs_ref, prob, vcols)):
                turned = left[0, :, cols].T
                grad = jnp.concatenate([mm(turned[:64], right[:ROWS]), mm(turned[64:], right[ROWS:])], axis=0).T
                acc_ref[seen, into] += grad[: 2 * ROWS]
                acc_ref[fresh, into] = grad[2 * ROWS : 3 * ROWS]

        twins = HEADS // 2
        differ(0)
        for t in range(twins + 1):
            if t + 1 < twins:
                differ(t + 1)
            if t >= 1:
                spend(t - 1)
            if t < twins:
                weigh(t)

    @pl.when(step == frames - 1)
    def _():
        ghost_ref[:, :width] = (acc_ref[ghost_rows, :width] * inv_scale).astype(bf16)
        ghost_ref[:, width:] = acc_ref[ghost_rows, width:].astype(bf16)
        swap.start()
        for load in loads[3:]:
            load.wait()

    def grads_of(start, size, lo, hi):
        here = pl.ds(pl.multiple_of(start, 16), size)
        below = pl.ds(pl.multiple_of(start + ROWS, 16), size)
        parts = []
        if lo < width:
            parts.append(dq_ref[here, lo : min(hi, width)])
        if lo < 2 * width and hi > width:
            parts.append((acc_ref[below, max(lo - width, 0) : min(hi, 2 * width) - width] * inv_scale).astype(bf16))
        if hi > 2 * width:
            parts.append(acc_ref[below, max(lo, 2 * width) - width : hi - width].astype(bf16))
        return jnp.concatenate(parts, axis=1)

    @pl.when(step == frames)
    def _():
        swap.wait()
        got = got_ref[...].astype(f32)
        acc_ref[edge_rows, :width] += got[:, :width] * (1.0 / inv_scale)
        acc_ref[edge_rows, width:] += got[:, width:]

        def weights(lo, hi):
            total = 0.0
            for i in range(frames // 4):
                grads = grads_of(4 * i * ROWS, 4 * ROWS, lo, hi)
                total = total + mm_tn(ain_ref[4 * i : 4 * i + 4].reshape(4 * ROWS, width), grads)
                sq_ref[:, lo:hi] += fold8(grads.astype(f32))
            return total

        def pad(end, stop):
            if end < stop:
                own2_ref[end:stop] = jnp.zeros((stop - end, 16, 128), bf16)

        pad(pack_matrix(own2_ref, 0, weights(0, early_cols)), cut2)
        three.send(0)
        late = weights(early_cols, 3 * width)
        three.take(0)
        three.send(1)
        pad(pack_matrix(own2_ref, cut2, late), own2_ref.shape[0])
        four.send(0)

    at(norm_step + 1, (four.take, 0), (four.send, 1), (one.settle, 1), (one.spread, 0))
    at(norm_step + 4, (three.take, 1), (three.send, 2), (two.settle, 1), (two.spread, 0))

    @pl.when(step == norm_step + 6)
    def _():
        for total in (one, two, side):
            total.settle(0)
        keep.start()

    at(norm_step + 7, (four.take, 1), (four.send, 2))

    @pl.when(step > frames)
    def _():
        i = step - norm_step
        block = 2 * ROWS
        x = x_ref[pl.ds(2 * i, 2)].reshape(block, width).astype(f32)
        n, inverse = normed_of(x)
        up = mm_nt(grads_of(i * block, block, 0, 3 * width), wqkv_ref[...])
        gres = gres_ref[...].reshape(block, width)
        narrow_into(in_ref, 0, gres + norm_back(up, n, inverse, row_ref[:, :width]))
        s384_ref[0] += fold8(up * n)
        s384_ref[1] += fold8(up)

    @pl.when(step == steps - 1)
    def _():
        sq = colsum(sq_ref[...])
        parts = [colsum(s384_ref[0]), colsum(s384_ref[1]), sq[:, :width], sq[:, 2 * width :]]
        lines = [v[:, c : c + 128] for v in parts for c in range(0, width, 128)]
        lines += [jnp.zeros((1, 128), f32)] * (16 - len(lines))
        rows.spread(last, jnp.concatenate(lines, axis=0))
        for i in range(2, count):
            for total in (three, four):
                total.take(i)
                if i < last:
                    total.send(i + 1)
                else:
                    total.spread(last)
        for i in range(last, 0, -1):
            tile = rows.settle(i)
            rows.spread(i - 1, tile)
            for total in (three, four):
                total.settle(i)
                total.spread(i - 1)
        rows_ref[...] = rows.settle(0)
        three.settle(0)
        four.settle(0)
        res2_ref[...] = sum2_ref[...]
        keep.wait()


def unpack_kernel(cut2, in_hbm, res_hbm, res2_ref, rows_ref, out_hbm, gg1, gb1, gqkv_hbm, gqv, gwo_hbm, gbo, gg2, gb2, gw1_hbm,
                  gbf1, gw2_hbm, gbf2, gqkv, gwo, gw1, gw2, res_ref, mid_ref, sems):
    width, hidden = gw1.shape
    tiles = width // 16
    across = hidden // 128 * tiles
    pieces = 4
    piece = in_hbm.shape[0] // pieces
    come, go = [], []
    for i in range(pieces):
        rows = slice(i * piece, (i + 1) * piece)
        come.append(pltpu.make_async_copy(in_hbm.at[rows], mid_ref.at[rows], sems.at[7 + i]))
        go.append(pltpu.make_async_copy(mid_ref.at[rows], out_hbm.at[rows], sems.at[7 + pieces + i]))
    parts = (0, across, 2 * across, res_hbm.shape[0])
    loads = [
        pltpu.make_async_copy(res_hbm.at[lo:hi], res_ref.at[lo:hi], sems.at[i])
        for i, (lo, hi) in enumerate(zip(parts, parts[1:]))
    ]
    stores = [
        pltpu.make_async_copy(src, dst, sems.at[3 + i])
        for i, (src, dst) in enumerate(((gqkv, gqkv_hbm), (gwo, gwo_hbm), (gw1, gw1_hbm), (gw2, gw2_hbm)))
    ]
    for copy in loads + come:
        copy.start()
    early = 3 * width // 128 // 2
    for c in range(3 * width // 128):
        at = c * tiles if c < early else cut2 + (c - early) * tiles
        gqkv[:, 128 * c : 128 * c + 128] = res2_ref[at : at + tiles].reshape(width, 128).astype(f32)
    stores[0].start()
    loads[0].wait()
    at = 0
    for c in range(hidden // 128):
        gw1[:, 128 * c : 128 * c + 128] = res_ref[at : at + tiles].reshape(width, 128).astype(f32)
        at += tiles
    stores[2].start()
    for i in range(pieces):
        come[i].wait()
        go[i].start()
    loads[1].wait()
    for c in range(hidden // 128):
        gw2[128 * c : 128 * c + 128, :] = res_ref[at : at + tiles].reshape(width, 128).astype(f32).T
        at += tiles
    stores[3].start()
    loads[2].wait()
    for c in range(width // 128):
        gwo[:, 128 * c : 128 * c + 128] = res_ref[at : at + tiles].reshape(width, 128).astype(f32)
        at += tiles
    stores[1].start()
    row = 0
    for out in (gg2, gb2, gbo, gbf2, gbf1):
        for c in range(out.shape[0] // 128):
            out[128 * c : 128 * c + 128] = res_ref[at + row // 16].astype(f32)[row % 16]
            row += 1
    rows = rows_ref[...]
    each = width // 128
    for i, out in enumerate((gg1, gb1)):
        for c in range(each):
            out[128 * c : 128 * c + 128] = rows[i * each + c]
    for i in range(2):
        for c in range(each):
            gqv[i : i + 1, 128 * c : 128 * c + 128] = rows[(i + 2) * each + c : (i + 2) * each + c + 1]
    for copy in stores + go:
        copy.wait()


def whole(shape):
    return pl.BlockSpec(shape, lambda i: (0,) * len(shape), pipeline_mode=pl.Buffered(1))


def pairs(shape):
    return pl.BlockSpec((2,) + shape, lambda i: (i,) + (0,) * len(shape))


def single(shape):
    return pl.BlockSpec((1,) + shape, lambda i: (i,) + (0,) * len(shape))


def params(collective=None):
    if collective is None:
        return pltpu.CompilerParams(vmem_limit_bytes=60 * 2**20)
    return pltpu.CompilerParams(vmem_limit_bytes=60 * 2**20, collective_id=collective, has_side_effects=True)


def per_device(tokens, frame_clip, ln1_gain, ln1_bias, w_qkv, qv_bias, w_out, b_out, ln2_gain, ln2_bias,
               w_fc1, b_fc1, w_fc2, b_fc2, cotangent):
    count, width = tokens.shape
    hidden = w_fc1.shape[1]
    frames = count // FRAME
    steps = frames // 2
    tm = lax.axis_index("tm")
    edge = jnp.where(tm == 0, tokens[count - ROWS :], tokens[:ROWS])
    ghost = lax.ppermute(edge, "tm", [(0, 1), (1, 0)])
    in_vmem = pl.BlockSpec(memory_space=pltpu.VMEM)
    in_hbm = pl.BlockSpec(memory_space=pl.ANY)
    kv_rows = (frames + 2) * ROWS + WIN - 3 * ROWS
    shape = jax.ShapeDtypeStruct
    stages = stages_of(lax.axis_size("clips"))
    devices = 2 * lax.axis_size("clips")
    tiles = width // 16
    units = units_for((2 * hidden + width) // 128 * tiles + 2, devices)
    across2 = 3 * width // 128
    first2 = units_for(across2 // 2 * tiles, devices)
    second2 = units_for((across2 - across2 // 2) * tiles, devices)
    units2 = first2 + second2
    x_pad, ain, kv, prob, block_out, qs, ga, gs, gres, li, row, pack = pl.pallas_call(
        forward_kernel,
        grid=(steps,),
        in_specs=[
            pl.BlockSpec(memory_space=pltpu.SMEM),
            in_hbm,
            whole((ROWS, width)),
            whole((width,)),
            whole((width,)),
            whole((2, width)),
            whole((width,)),
            whole((width,)),
            whole((width,)),
            whole((hidden,)),
            whole((width,)),
            whole((width, 3 * width)),
            in_hbm,
            in_hbm,
            in_hbm,
            in_hbm,
        ],
        out_specs=[
            in_hbm,
            in_hbm,
            in_hbm,
            pairs((HEADS // 2, 2 * ROWS, WIN)),
            pl.BlockSpec((4 * FRAME, width), lambda i: (i // 2, 0)),
            pairs((ROWS, width)),
            pairs((HEADS // 2, 2 * ROWS, 128 + EXTRA)),
            pairs((ROWS, width)),
            pairs((ROWS, width)),
            pairs((ROWS, width)),
            whole((1, 9 * width + hidden)),
            whole((units, 16, 128)),
        ],
        out_shape=[
            shape((frames, ROWS, width), bf16),
            shape((frames, ROWS, width), bf16),
            shape((kv_rows, 2 * width), bf16),
            shape((frames, HEADS // 2, 2 * ROWS, WIN), bf16),
            shape((count, width), bf16),
            shape((frames, ROWS, width), bf16),
            shape((frames, HEADS // 2, 2 * ROWS, 128 + EXTRA), bf16),
            shape((frames, ROWS, width), bf16),
            shape((frames, ROWS, width), f32),
            shape((frames, ROWS, width), f32),
            shape((1, 9 * width + hidden), f32),
            shape((units, 16, 128), bf16),
        ],
        scratch_shapes=[
            pltpu.VMEM((frames, ROWS, width), bf16),
            pltpu.VMEM((frames, ROWS, width), bf16),
            pltpu.VMEM((kv_rows, 2 * width), bf16),
            pltpu.VMEM((count, width), bf16),
            pltpu.VMEM((width, width), bf16),
            pltpu.VMEM((width, hidden), bf16),
            pltpu.VMEM((hidden, width), bf16),
            pltpu.VMEM((frames, ROWS, width), bf16),
            pltpu.VMEM((frames, ROWS, width), bf16),
            pltpu.VMEM((kv_rows, 128), bf16),
            pltpu.VMEM((3, 2 * ROWS, WIN), f32),
            pltpu.VMEM((2 * ROWS, width), f32),
            pltpu.VMEM((4 * FRAME, width), f32),
            pltpu.VMEM((width, hidden), f32),
            pltpu.VMEM((width, hidden), f32),
            pltpu.VMEM((width, width), f32),
            pltpu.VMEM((8, hidden), f32),
            pltpu.VMEM((4, 8, width), f32),
            pltpu.SemaphoreType.DMA((8,)),
        ],
        compiler_params=params(),
    )(frame_clip, tokens, ghost, ln1_gain, ln1_bias, qv_bias, b_out, ln2_gain, ln2_bias, b_fc1, b_fc2, w_qkv, cotangent,
      w_out, w_fc1, w_fc2)

    first, second, side = shares(units, devices)
    early = lambda sh: pl.BlockSpec((1,) + sh, lambda i: (jnp.minimum(i, frames - 1),) + (0,) * len(sh))
    late = lambda i: jnp.maximum(i - frames - 1, 0)
    input_grad, res, res2, sums = pl.pallas_call(
        functools.partial(back_kernel, stages),
        grid=(frames + 1 + steps,),
        in_specs=[
            early((HEADS // 2, 2 * ROWS, WIN)),
            in_hbm,
            early((HEADS // 2, 2 * ROWS, 128 + EXTRA)),
            early((ROWS, width)),
            early((ROWS, width)),
            early((ROWS, width)),
            in_hbm,
            in_hbm,
            pl.BlockSpec((2, ROWS, width), lambda i: (late(i), 0, 0)),
            whole(row.shape),
            in_hbm,
            in_hbm,
        ],
        out_specs=[
            pl.BlockSpec((2 * FRAME, width), lambda i: (late(i), 0)),
            in_hbm,
            whole((units2, 16, 128)),
            whole((16, 128)),
        ],
        out_shape=[
            shape((count, width), f32),
            shape((units, 16, 128), bf16),
            shape((units2, 16, 128), bf16),
            shape((16, 128), f32),
        ],
        scratch_shapes=[
            pltpu.VMEM((kv_rows, 2 * width), f32),
            pltpu.VMEM((3, 2 * ROWS, WIN), f32),
            pltpu.VMEM((3, 2 * ROWS, WIN), bf16),
            pltpu.VMEM((frames * ROWS, width), bf16),
            pltpu.VMEM((8, 3 * width), f32),
            pltpu.VMEM((2, 8, width), f32),
            pltpu.VMEM((units, 16, 128), bf16),
            pltpu.VMEM((units, 16, 128), bf16),
            pltpu.VMEM((units2, 16, 128), bf16),
            pltpu.VMEM((units2, 16, 128), bf16),
            pltpu.VMEM((ROWS, 2 * width), bf16),
            pltpu.VMEM((ROWS, 2 * width), bf16),
            pltpu.VMEM((kv_rows, 2 * width), bf16),
            pltpu.VMEM((frames, ROWS, width), bf16),
            pltpu.VMEM((frames, ROWS, width), bf16),
            pltpu.VMEM((width, 3 * width), bf16),
            pltpu.SemaphoreType.DMA((2,)),
            pltpu.SemaphoreType.DMA((7,)),
        ]
        + sum_scratch(stages, first)
        + sum_scratch(stages, second)
        + sum_scratch(turned(stages), side)
        + sum_scratch(stages, first2)
        + sum_scratch(stages, second2)
        + rows_scratch(stages),
        compiler_params=params(0),
    )(prob, kv, ga, gs, qs, li, x_pad, ain, gres, row, w_qkv, pack)

    sizes = [(width,), (width,), (width, 3 * width), (2, width), (width, width), (width,), (width,), (width,),
             (width, hidden), (hidden,), (hidden, width), (width,)]
    big = [len(z) == 2 and z[0] > 2 for z in sizes]
    outs = pl.pallas_call(
        functools.partial(unpack_kernel, first2),
        in_specs=[in_hbm, in_hbm, in_vmem, in_vmem],
        out_specs=[in_hbm] + [in_hbm if far else in_vmem for far in big],
        out_shape=[shape((count, width), f32)] + [shape(z, f32) for z in sizes],
        scratch_shapes=[
            pltpu.VMEM((width, 3 * width), f32),
            pltpu.VMEM((width, width), f32),
            pltpu.VMEM((width, hidden), f32),
            pltpu.VMEM((hidden, width), f32),
            pltpu.VMEM((units, 16, 128), bf16),
            pltpu.VMEM((count, width), f32),
            pltpu.SemaphoreType.DMA((15,)),
        ],
        compiler_params=params(),
    )(input_grad, res, res2, sums)
    return (block_out,) + tuple(outs)


def solution(mesh):
    rows = P(("clips", "tm"), None)
    rep = P()
    return jax.shard_map(
        per_device,
        mesh=mesh,
        in_specs=(rows, P("clips")) + (rep,) * 12 + (rows,),
        out_specs=(rows, rows) + (rep,) * 12,
        check_vma=False,
    )
```

```python
import functools
import math

import jax
import jax.numpy as jnp
from jax import lax
from jax.experimental import pallas as pl
from jax.experimental.pallas import tpu as pltpu
from jax.sharding import PartitionSpec as P

HEADS = 6
FRAME = 196
ROWS = 208
WIN = 640
EXTRA = 16
EPS = 1e-6
LOG2E = math.log2(math.e)

bf16 = jnp.bfloat16
f32 = jnp.float32


def mm(a, b):
    return jnp.dot(a, b, preferred_element_type=f32)


def mm_nt(a, b):
    return lax.dot_general(a, b, (((1,), (1,)), ((), ())), preferred_element_type=f32)


def mm_tn(a, b):
    return lax.dot_general(a, b, (((0,), (0,)), ((), ())), preferred_element_type=f32)


def normed_of(x):
    mean = jnp.mean(x, axis=-1, keepdims=True)
    centred = x - mean
    var = jnp.mean(centred * centred, axis=-1, keepdims=True)
    inverse = lax.rsqrt(var + EPS)
    return centred * inverse, inverse


def norm_back(upstream, normed, inverse, gain):
    scaled = upstream * gain
    mean = jnp.mean(scaled, axis=-1, keepdims=True)
    along = jnp.mean(scaled * normed, axis=-1, keepdims=True)
    return inverse * (scaled - mean - normed * along)


def fold8(v):
    rows, cols = v.shape
    return jnp.sum(v.reshape(rows // 8, 8, cols), axis=0)


MESH = pl.DeviceIdType.MESH


def stages_of(clips):
    stages, stride = [("tm", 1, 2)], 1
    while clips > 1:
        size = 4 if clips % 4 == 0 else (2 if clips % 2 == 0 else clips)
        stages.append(("clips", stride, size))
        stride, clips = stride * size, clips // size
    return stages


def digit(stage):
    axis, stride, size = stage
    return lax.rem(lax.axis_index(axis) // stride, size)


def partner(stage, turn):
    axis, stride, size = stage
    mine = digit(stage)
    return {axis: lax.axis_index(axis) + (lax.rem(mine + turn, size) - mine) * stride}


def greet(stages):
    sem, count = pltpu.get_barrier_semaphore(), 0
    for stage in stages:
        for turn in range(1, stage[2]):
            pl.semaphore_signal(sem, inc=1, device_id=partner(stage, turn), device_id_type=MESH)
            count += 1
    pl.semaphore_wait(sem, count)


class Sum:
    def __init__(self, stages, pack, result, landing, sent, came):
        self.stages, self.pack, self.result, self.landing = stages, pack, result, landing
        self.sent, self.came = sent, came
        self.segments, start, length = [], 0, pack.shape[0]
        for stage in stages:
            self.segments.append((start, length))
            length = length // stage[2]
            start = start + digit(stage) * length
        self.segments.append((start, length))
        self.first = [sum(s[2] - 1 for s in stages[:i]) for i in range(len(stages) + 1)]

    def _scatter(self, i):
        stage, (start, length) = self.stages[i], self.segments[i]
        part = length // stage[2]
        for turn in range(1, stage[2]):
            slot = self.first[i] + turn - 1
            other = lax.rem(digit(stage) + turn, stage[2])
            yield pltpu.make_async_remote_copy(
                src_ref=self.pack.at[pl.ds(start + other * part, part)],
                dst_ref=self.landing[i].at[turn - 1],
                send_sem=self.sent.at[slot],
                recv_sem=self.came.at[slot],
                device_id=partner(stage, turn),
                device_id_type=MESH,
            )

    def _gather(self, i):
        stage, (start, length) = self.stages[i], self.segments[i + 1]
        for turn in range(1, stage[2]):
            slot = self.first[-1] + self.first[i] + turn - 1
            here = self.result.at[pl.ds(start, length)]
            yield pltpu.make_async_remote_copy(
                src_ref=here,
                dst_ref=here,
                send_sem=self.sent.at[slot],
                recv_sem=self.came.at[slot],
                device_id=partner(stage, turn),
                device_id_type=MESH,
            )

    def send(self, i):
        for copy in self._scatter(i):
            copy.start()

    def take(self, i):
        for copy in self._scatter(i):
            copy.wait()
        start, length = self.segments[i + 1]
        into = self.result if i == len(self.stages) - 1 else self.pack
        block = next(b for b in (28, 24, 21, 16, 14, 12, 8, 7, 6, 4, 3, 2, 1) if length % b == 0)

        def add(j, carry):
            total = self.pack[pl.ds(start + j * block, block)].astype(f32)
            for turn in range(1, self.stages[i][2]):
                total = total + self.landing[i][turn - 1, pl.ds(j * block, block)].astype(f32)
            into[pl.ds(start + j * block, block)] = total.astype(bf16)
            return carry

        lax.fori_loop(0, length // block, add, 0)

    def spread(self, i):
        for copy in self._gather(i):
            copy.start()

    def settle(self, i):
        for copy in self._gather(i):
            copy.wait()


def sum_scratch(stages, units):
    shapes, left = [], units
    for stage in stages:
        left //= stage[2]
        shapes.append(pltpu.VMEM((stage[2] - 1, left, 16, 128), bf16))
    copies = 2 * sum(s[2] - 1 for s in stages)
    return shapes + [pltpu.SemaphoreType.DMA((copies,)), pltpu.SemaphoreType.DMA((copies,))]


def pack_matrix(pack, first, value):
    rows, cols = value.shape
    tiles = rows // 16
    for c in range(cols // 128):
        pack[first + c * tiles : first + (c + 1) * tiles] = (
            value[:, 128 * c : 128 * (c + 1)].astype(bf16).reshape(tiles, 16, 128)
        )
    return first + cols // 128 * tiles


def pack_rows(pack, first, vectors):
    rows = [v[:, c : c + 128] for v in vectors for c in range(0, v.shape[1], 128)]
    rows += [jnp.zeros((1, 128), f32)] * (-len(rows) % 16)
    for r in range(0, len(rows), 16):
        pack[first + r // 16] = jnp.concatenate(rows[r : r + 16], axis=0).astype(bf16)
    last = first + len(rows) // 16
    if last < pack.shape[0]:
        pack[last:] = jnp.zeros((pack.shape[0] - last, 16, 128), bf16)


def unpack_matrix(res, first, rows, cols):
    tiles = rows // 16
    part = res[first : first + cols // 128 * tiles].reshape(cols // 128, tiles, 16, 128)
    return part.transpose(1, 2, 0, 3).reshape(rows, cols).astype(f32)


def units_for(needed, devices):
    return -(-needed // devices) * devices


def colsum(v):
    return jnp.sum(v, axis=0, keepdims=True)


def widen(ref, group, which):
    start = which * FRAME // 16 * 16
    shift = which * FRAME - start
    v = ref[pl.ds(pl.multiple_of(group * 4 * FRAME + start, 16), ROWS), :].astype(f32)
    if shift:
        v = pltpu.roll(v, ROWS - shift, 0)
    row = lax.broadcasted_iota(jnp.int32, (16, v.shape[1]), 0)
    return v, jnp.where(row < 16 - (ROWS - FRAME), v[ROWS - 16 :], 0.0)


def narrow_into(ref, start, v):
    edge = FRAME // 8 * 8
    over = FRAME - edge
    second = pltpu.roll(v[ROWS:], over, 0)
    row = lax.broadcasted_iota(jnp.int32, (8, v.shape[1]), 0)
    ref[pl.ds(pl.multiple_of(start, 8), edge), :] = v[:edge]
    ref[pl.ds(pl.multiple_of(start + edge, 8), 8), :] = jnp.where(row < over, v[edge : edge + 8], second[:8])
    rest = 2 * FRAME - edge - 8
    ref[pl.ds(pl.multiple_of(start + edge + 8, 8), rest), :] = second[8 : 8 + rest]


def forward_kernel(
    clip_ref,
    tok_hbm,
    ghost_ref,
    g1_ref,
    s1_ref,
    qv_ref,
    bo_ref,
    g2_ref,
    s2_ref,
    bf1_ref,
    bf2_ref,
    wqkv_ref,
    cot_hbm,
    wout_hbm,
    w1_hbm,
    w2_hbm,
    x_hbm,
    ain_hbm,
    kv_hbm,
    prob_ref,
    out_ref,
    qs_ref,
    ga_ref,
    gs_ref,
    gres_ref,
    li_ref,
    row_ref,
    pack_ref,
    x_ref,
    ain_ref,
    kv_ref,
    raw_ref,
    wout_ref,
    w1_ref,
    w2_ref,
    q_ref,
    cp_ref,
    flag_ref,
    s_ref,
    o_ref,
    flat_ref,
    gw1_ref,
    gw2_ref,
    gwo_ref,
    sb1_ref,
    s384_ref,
    sems,
):
    step = pl.program_id(0)
    steps = pl.num_programs(0)
    frames = x_ref.shape[0]
    width = x_ref.shape[-1]
    hidden = w1_ref.shape[-1]
    tm = lax.axis_index("tm")
    copies = [
        pltpu.make_async_copy(src, dst, sems.at[i])
        for i, (src, dst) in enumerate(
            ((cot_hbm, raw_ref), (wout_hbm, wout_ref), (w1_hbm, w1_ref), (w2_hbm, w2_ref), (x_ref, x_hbm), (kv_ref, kv_hbm),
             (ain_ref, ain_hbm), (tok_hbm, raw_ref))
        )
    ]

    @pl.when(step == 0)
    def _():
        copies[7].start()
        for copy in copies[1:4]:
            copy.start()
        vectors = [g1_ref[...], s1_ref[...], None, None, None, bo_ref[...], g2_ref[...], s2_ref[...], bf2_ref[...]]
        for i, v in enumerate(vectors):
            if v is not None:
                row_ref[:, i * width : (i + 1) * width] = v.astype(f32)[None, :]
        row_ref[:, 2 * width : 3 * width] = qv_ref[0:1, :].astype(f32)
        row_ref[:, 3 * width : 4 * width] = jnp.zeros((1, width), f32)
        row_ref[:, 4 * width : 5 * width] = qv_ref[1:2, :].astype(f32)
        row_ref[:, 9 * width :] = bf1_ref[...].astype(f32)[None, :]

    vec = lambda i, n=width: row_ref[:, i * width : i * width + n]
    gain1, shift1, bias3, biaso, gain2, shift2, bias2, bias1 = (
        vec(0), vec(1), vec(2, 3 * width), vec(5), vec(6), vec(7), vec(8), vec(9, hidden))

    @pl.when(step == 0)
    def _():
        gw1_ref[...] = jnp.zeros_like(gw1_ref)
        gw2_ref[...] = jnp.zeros_like(gw2_ref)
        gwo_ref[...] = jnp.zeros_like(gwo_ref)
        sb1_ref[...] = jnp.zeros_like(sb1_ref)
        s384_ref[...] = jnp.zeros_like(s384_ref)
        at = lax.broadcasted_iota(jnp.int32, flag_ref.shape, 0)
        lane = lax.broadcasted_iota(jnp.int32, flag_ref.shape, 1)
        slot = at // ROWS
        flag_ref[...] = jnp.where(
            lane == 0,
            jnp.where(at - slot * ROWS < FRAME, 0.0, -1e30),
            jnp.where(lane == 1 + slot % 4, 1.0, 0.0),
        ).astype(bf16)
        zero_slot = jnp.where(tm == 0, 0, frames + 1)
        ghost_slot = frames + 1 - zero_slot
        kv_ref[pl.ds(pl.multiple_of(zero_slot * ROWS, 16), ROWS), :] = jnp.zeros((ROWS, 2 * width), bf16)
        kv_ref[(frames + 2) * ROWS :, :] = jnp.zeros((WIN - 3 * ROWS, 2 * width), bf16)

        x = ghost_ref[...].astype(f32)
        x = jnp.where(tm == 0, x, pltpu.roll(x, FRAME, 0))
        n, _ = normed_of(x)
        kv = mm((n * gain1 + shift1).astype(bf16), wqkv_ref[:, width:]) + bias3[:, width:]
        kv_ref[pl.ds(pl.multiple_of(ghost_slot * ROWS, 16), ROWS), :] = kv.astype(bf16)

        def pad(i, src, dst):
            for which in range(4):
                v, end = widen(src, i, which)
                dst[4 * i + which, : ROWS - 16] = v[: ROWS - 16].astype(bf16)
                dst[4 * i + which, ROWS - 16 :] = end.astype(bf16)

        def ready(i):
            x = x_ref[4 * i : 4 * i + 4].reshape(4 * ROWS, width).astype(f32)
            n, _ = normed_of(x)
            normed = (n * gain1 + shift1).astype(bf16)
            ain_ref[4 * i : 4 * i + 4] = normed.reshape(4, ROWS, width)
            return normed

        def project(i, normed):
            qkv = (mm(normed, wqkv_ref[...]) + bias3).astype(bf16)
            q_ref[4 * i : 4 * i + 4] = qkv[:, :width].reshape(4, ROWS, width)
            kv_ref[(4 * i + 1) * ROWS : (4 * i + 5) * ROWS, :] = qkv[:, width:]

        copies[7].wait()
        for i in range(frames // 4):
            pad(i, raw_ref, x_ref)
        copies[0].start()
        normed = ready(0)
        for i in range(frames // 4):
            following = ready(i + 1) if i + 1 < frames // 4 else None
            project(i, normed)
            normed = following
        for copy in copies[4:7]:
            copy.start()
        for copy in copies[:4]:
            copy.wait()
        for i in range(frames // 4):
            pad(i, raw_ref, cp_ref)

    low = lax.broadcasted_iota(jnp.int32, (ROWS, 128), 1) < 64
    lane = lax.broadcasted_iota(jnp.int32, (1, 128), 1)
    scale = LOG2E / math.sqrt(width // HEADS)
    twins = HEADS // 2
    flags, windows = [], []
    for sub in range(2):
        frame = 2 * step + sub
        here = tm * frames + frame
        own = clip_ref[here]
        before = jnp.where(here > 0, clip_ref[jnp.maximum(here - 1, 0)], -1)
        after = jnp.where(here < 2 * frames - 1, clip_ref[jnp.minimum(here + 1, 2 * frames - 1)], -1)
        none = jnp.float32(-1e30)
        row = jnp.where(lane == 0, 1.0, 0.0)
        row = jnp.where(lane == 1 + frame % 4, jnp.where(before == own, 0.0, none), row)
        row = jnp.where(lane == 1 + (frame + 2) % 4, jnp.where(after == own, 0.0, none), row)
        row = jnp.where(lane == 1 + (frame + 3) % 4, none, row)
        flags.append(jnp.broadcast_to(row.astype(bf16), (2 * ROWS, 128))[:, :EXTRA])
        windows.append(pl.ds(pl.multiple_of(frame * ROWS, 16), WIN))

    def score(t):
        sub, pair = divmod(t, twins)
        cols = slice(pair * 128, pair * 128 + 128)
        q = q_ref[2 * step + sub, :, cols]
        zero = jnp.zeros_like(q)
        both = jnp.concatenate([jnp.where(low, q, zero), jnp.where(low, zero, q)], axis=0)
        k = jnp.concatenate([kv_ref[windows[sub], cols], flag_ref[windows[sub], :EXTRA]], axis=1)
        s_ref[t % 3] = mm_nt(jnp.concatenate([both, flags[sub]], axis=1), k)

    inverses = {}

    def soften(t):
        sub, pair = divmod(t, twins)
        s = s_ref[t % 3]
        top = jnp.max(s, axis=-1, keepdims=True)
        e = jnp.exp2((s - top) * scale)
        inverses[t] = 1.0 / jnp.sum(e, axis=-1, keepdims=True)
        prob_ref[sub, pair] = e.astype(bf16)

    def attend(t):
        sub, pair = divmod(t, twins)
        at = pair * 128
        o = mm(prob_ref[sub, pair], kv_ref[windows[sub], width + at : width + at + 128])
        inverse = jnp.where(low, inverses[t][:ROWS], inverses[t][ROWS:])
        rows = slice(sub * ROWS, (sub + 1) * ROWS)
        o_ref[rows, at : at + 128] = jnp.where(low, o[:ROWS], o[ROWS:]) * inverse
        li_ref[sub, :, at : at + 128] = inverse

    score(0)
    for t in range(2 * twins + 1):
        if t + 1 < 2 * twins:
            score(t + 1)
        if t >= 1:
            attend(t - 1)
        if t < 2 * twins:
            soften(t)

    att = o_ref[...].astype(bf16)
    both = pl.ds(2 * step, 2)
    x = x_ref[both].reshape(2 * ROWS, width).astype(f32)
    resid = x + mm(att, wout_ref[...]) + biaso
    n2, inv2 = normed_of(resid)
    mlp_in = (n2 * gain2 + shift2).astype(bf16)
    cot = cp_ref[both].reshape(2 * ROWS, width)
    chunk = 512
    chunks = [slice(c, c + chunk) for c in range(0, hidden, chunk)]
    held = {}

    def start(c):
        held[c] = mm(mlp_in, w1_ref[:, chunks[c]]), mm_nt(cot, w2_ref[chunks[c], :])

    def middle(c):
        pre, ghid = held[c]
        pre = pre + bias1[:, chunks[c]]
        cdf = 0.5 + 0.5 * lax.erf(pre * (1.0 / math.sqrt(2.0)))
        dens = jnp.exp2(pre * pre * (-0.5 * LOG2E)) * (1.0 / math.sqrt(2.0 * math.pi))
        gpre = (ghid * (cdf + pre * dens)).astype(bf16)
        sb1_ref[:, chunks[c]] += fold8(gpre.astype(f32))
        held[c] = (pre * cdf).astype(bf16), gpre

    def weights(c):
        gw2_ref[:, chunks[c]] += mm_tn(cot, held[c][0])
        gw1_ref[:, chunks[c]] += mm_tn(mlp_in, held[c][1])

    start(0)
    for c in range(len(chunks)):
        if c + 1 < len(chunks):
            start(c + 1)
        middle(c)
    hid = jnp.concatenate([held[c][0] for c in range(len(chunks))], axis=1)
    gpre = jnp.concatenate([held[c][1] for c in range(len(chunks))], axis=1)
    up = mm_nt(gpre, w1_ref[...])
    cot32 = cot.astype(f32)
    gres = cot32 + norm_back(up, n2, inv2, gain2)
    gres_ref[...] = gres.reshape(2, ROWS, width)
    branch = gres.astype(bf16)
    weights(0)
    g = mm_nt(branch, wout_ref[...]).astype(bf16)
    for c in range(1, len(chunks) - 1):
        weights(c)
    g32 = g.astype(f32)
    inverse = li_ref[...].reshape(2 * ROWS, width)
    gs_ref[...] = (g32 * inverse).astype(bf16).reshape(2, ROWS, width)
    qs_ref[...] = (q_ref[both].reshape(2 * ROWS, width).astype(f32) * inverse).astype(bf16).reshape(2, ROWS, width)
    dots = g32 * o_ref[...]
    some = lax.broadcasted_iota(jnp.int32, (2 * ROWS, EXTRA), 1)
    for sub in range(2):
        for pair in range(twins):
            rows, cols = slice(sub * ROWS, (sub + 1) * ROWS), slice(128 * pair, 128 * pair + 128)
            d = dots[rows, cols]
            even = jnp.sum(jnp.where(low, d, 0.0), axis=-1, keepdims=True)
            odd = jnp.sum(jnp.where(low, 0.0, d), axis=-1, keepdims=True)
            less = jnp.broadcast_to(-jnp.concatenate([even, odd], axis=0), (2 * ROWS, EXTRA))
            one = less.astype(bf16).astype(f32)
            two = (less - one).astype(bf16).astype(f32)
            three = less - one - two
            ga_ref[sub, pair, :, 128 : 128 + EXTRA] = jnp.where(
                some == 0, one, jnp.where(some == 1, two, jnp.where(some == 2, three, 0.0))
            ).astype(bf16)
            gp = g[rows, cols]
            zero = jnp.zeros_like(gp)
            ga_ref[sub, pair, :ROWS, :128] = jnp.where(low, gp, zero)
            ga_ref[sub, pair, ROWS:, :128] = jnp.where(low, zero, gp)
    s384_ref[0] += fold8(up * n2)
    s384_ref[1] += fold8(up)
    s384_ref[2] += fold8(branch.astype(f32))
    s384_ref[3] += fold8(cot32)
    weights(len(chunks) - 1)
    gwo_ref[...] += mm_tn(att, branch)
    out = resid + bias2 + mm(hid, w2_ref[...])
    narrow_into(flat_ref, step % 2 * 2 * FRAME, out)

    @pl.when(step % 2 == 1)
    def _():
        out_ref[...] = flat_ref[...].astype(bf16)

    @pl.when(step == steps - 1)
    def _():
        at = pack_matrix(pack_ref, 0, gw1_ref[...])
        at = pack_matrix(pack_ref, at, gw2_ref[...])
        at = pack_matrix(pack_ref, at, gwo_ref[...])
        pack_rows(pack_ref, at, [colsum(s384_ref[i]) for i in range(4)] + [colsum(sb1_ref[...])])
        for copy in copies[4:7]:
            copy.wait()


class Rows:
    def __init__(self, stages, boards, sent, came):
        self.stages, self.boards, self.sent, self.came = stages, boards, sent, came
        self.first = [sum(s[2] - 1 for s in stages[:i]) for i in range(len(stages) + 1)]

    def _copies(self, i):
        stage = self.stages[i]
        here = self.boards[i].at[digit(stage)]
        for turn in range(1, stage[2]):
            slot = self.first[i] + turn - 1
            yield pltpu.make_async_remote_copy(
                src_ref=here,
                dst_ref=here,
                send_sem=self.sent.at[slot],
                recv_sem=self.came.at[slot],
                device_id=partner(stage, turn),
                device_id_type=MESH,
            )

    def spread(self, i, tile):
        self.boards[i][digit(self.stages[i])] = tile
        for copy in self._copies(i):
            copy.start()

    def settle(self, i):
        for copy in self._copies(i):
            copy.wait()
        total = self.boards[i][0]
        for j in range(1, self.stages[i][2]):
            total = total + self.boards[i][j]
        return total


def rows_scratch(stages):
    copies = sum(s[2] - 1 for s in stages)
    return [pltpu.VMEM((s[2], 16, 128), f32) for s in stages] + [pltpu.SemaphoreType.DMA((copies,))] * 2


def shares(units, devices):
    blocks = units // devices
    side = max(1, round(blocks / 7))
    first = -(-(blocks - side) // 2)
    return first * devices, (blocks - side - first) * devices, side * devices


def turned(stages):
    return stages[:1] + stages[:0:-1]


def back_kernel(stages, prob_ref, kv_hbm, ga_ref, gs_ref, qs_ref, li_ref, x_hbm, ain_hbm, gres_ref, row_ref,
                wqkv_hbm, pack_hbm, in_ref, res_hbm, res2_ref, rows_ref,
                acc_ref, d_ref, ds_ref, dq_ref, sq_ref, s384_ref, own_ref, sum_ref, own2_ref, sum2_ref,
                ghost_ref, got_ref, kv_ref, x_ref, ain_ref, wqkv_ref, ghost_sems, load_sems, *rest):
    step = pl.program_id(0)
    width = gs_ref.shape[-1]
    frames = x_hbm.shape[0]
    steps = frames + 1 + frames // 2
    tm = lax.axis_index("tm")
    inv_scale = 1.0 / math.sqrt(width // HEADS)
    count = len(stages)
    last = count - 1
    devices = 2
    for stage in stages[1:]:
        devices *= stage[2]
    first, second, _ = shares(own_ref.shape[0], devices)
    both = first + second
    tiles = width // 16
    early_cols = 3 * width // 128 // 2 * 128
    cut2 = units_for(early_cols // 128 * tiles, devices)
    sums = []
    for n, (route, own, res) in enumerate(
        (
            (stages, own_ref.at[:first], sum_ref.at[:first]),
            (stages, own_ref.at[first:both], sum_ref.at[first:both]),
            (turned(stages), own_ref.at[both:], sum_ref.at[both:]),
            (stages, own2_ref.at[:cut2], sum2_ref.at[:cut2]),
            (stages, own2_ref.at[cut2:], sum2_ref.at[cut2:]),
        )
    ):
        mine = rest[n * (count + 2) : (n + 1) * (count + 2)]
        sums.append(Sum(route, own, res, mine[:count], *mine[count:]))
    one, two, side, three, four = sums
    extra = rest[5 * (count + 2) :]
    rows = Rows(stages, extra[:count], *extra[count:])
    near = 6 * ROWS
    loads = [
        pltpu.make_async_copy(src, dst, load_sems.at[i])
        for i, (src, dst) in enumerate(
            (
                (pack_hbm, own_ref),
                (kv_hbm.at[:near], kv_ref.at[:near]),
                (kv_hbm.at[near:], kv_ref.at[near:]),
                (x_hbm, x_ref),
                (ain_hbm, ain_ref),
                (wqkv_hbm, wqkv_ref),
            )
        )
    ]
    keep = pltpu.make_async_copy(sum_ref, res_hbm, load_sems.at[6])
    swap = pltpu.make_async_remote_copy(
        src_ref=ghost_ref,
        dst_ref=got_ref,
        send_sem=ghost_sems.at[0],
        recv_sem=ghost_sems.at[1],
        device_id=partner(stages[0], 1),
        device_id_type=MESH,
    )

    @pl.when(step == 0)
    def _():
        for load in loads[:2]:
            load.start()
        greet(stages)
        loads[0].wait()
        one.send(0)
        side.send(0)
        two.send(0)
        for load in loads[2:]:
            load.start()
        acc_ref[: 2 * ROWS] = jnp.zeros((2 * ROWS, 2 * width), f32)
        sq_ref[...] = jnp.zeros_like(sq_ref)
        s384_ref[...] = jnp.zeros_like(s384_ref)
        loads[1].wait()

    @pl.when(step == 1)
    def _():
        loads[2].wait()

    def at(when, *todo):
        @pl.when(step == when)
        def _():
            for act, i in todo:
                act(i)

    def scatter(total):
        return [t for i in range(1, last) for t in ((total.take, i), (total.send, i + 1))]

    def gather(total):
        return [t for i in range(last, 1, -1) for t in ((total.settle, i), (total.spread, i - 1))]

    norm_step = frames + 1
    at(1, (one.take, 0), (one.send, 1), (side.take, 0), (side.send, 1), (two.take, 0))
    at(4, (two.send, 1), *scatter(side))
    at(6, *scatter(one))
    at(8, *scatter(two), (side.take, last), (side.spread, last))
    at(9, (one.take, last), (one.spread, last))
    at(10, *gather(side))
    at(11, (two.take, last), (two.spread, last))
    at(13, *gather(one))
    at(15, *gather(two), (side.settle, 1), (side.spread, 0))

    low = lax.broadcasted_iota(jnp.int32, (ROWS, 128), 1) < 64
    ones = jnp.ones((WIN, EXTRA), bf16)
    edge_rows = pl.ds(pl.multiple_of(jnp.where(tm == 0, frames, 1) * ROWS, 16), ROWS)
    ghost_rows = pl.ds(pl.multiple_of(jnp.where(tm == 0, frames + 1, 0) * ROWS, 16), ROWS)

    @pl.when(step < frames)
    def _():
        window = pl.ds(pl.multiple_of(step * ROWS, 16), WIN)
        seen = pl.ds(pl.multiple_of(step * ROWS, 16), 2 * ROWS)
        fresh = pl.ds(pl.multiple_of((step + 2) * ROWS, 16), ROWS)

        def differ(t):
            at = width + t * 128
            v = jnp.concatenate([kv_ref[window, at : at + 128], ones], axis=1)
            d_ref[t % 3] = mm_nt(ga_ref[0, t], v)

        def weigh(t):
            ds_ref[t % 3] = (prob_ref[0, t].astype(f32) * d_ref[t % 3]).astype(bf16)

        def spend(t):
            cols = slice(t * 128, t * 128 + 128)
            vcols = slice(width + t * 128, width + t * 128 + 128)
            ds = ds_ref[t % 3]
            dq = mm(ds, kv_ref[window, cols])
            dq = jnp.where(low, dq[:ROWS], dq[ROWS:]) * (li_ref[0, :, cols] * inv_scale)
            dq_ref[pl.ds(pl.multiple_of(step * ROWS, 16), ROWS), cols] = dq.astype(bf16)
            prob = prob_ref[0, t]
            for left, right, into in ((qs_ref, ds, cols), (gs_ref, prob, vcols)):
                turned = left[0, :, cols].T
                grad = jnp.concatenate([mm(turned[:64], right[:ROWS]), mm(turned[64:], right[ROWS:])], axis=0).T
                acc_ref[seen, into] += grad[: 2 * ROWS]
                acc_ref[fresh, into] = grad[2 * ROWS : 3 * ROWS]

        twins = HEADS // 2
        differ(0)
        for t in range(twins + 1):
            if t + 1 < twins:
                differ(t + 1)
            if t >= 1:
                spend(t - 1)
            if t < twins:
                weigh(t)

    @pl.when(step == frames - 1)
    def _():
        ghost_ref[:, :width] = (acc_ref[ghost_rows, :width] * inv_scale).astype(bf16)
        ghost_ref[:, width:] = acc_ref[ghost_rows, width:].astype(bf16)
        swap.start()
        for load in loads[3:]:
            load.wait()

    def grads_of(start, size, lo, hi):
        here = pl.ds(pl.multiple_of(start, 16), size)
        below = pl.ds(pl.multiple_of(start + ROWS, 16), size)
        parts = []
        if lo < width:
            parts.append(dq_ref[here, lo : min(hi, width)])
        if lo < 2 * width and hi > width:
            parts.append((acc_ref[below, max(lo - width, 0) : min(hi, 2 * width) - width] * inv_scale).astype(bf16))
        if hi > 2 * width:
            parts.append(acc_ref[below, max(lo, 2 * width) - width : hi - width].astype(bf16))
        return jnp.concatenate(parts, axis=1)

    @pl.when(step == frames)
    def _():
        swap.wait()
        got = got_ref[...].astype(f32)
        acc_ref[edge_rows, :width] += got[:, :width] * (1.0 / inv_scale)
        acc_ref[edge_rows, width:] += got[:, width:]

        def weights(lo, hi):
            total = 0.0
            for i in range(frames // 4):
                grads = grads_of(4 * i * ROWS, 4 * ROWS, lo, hi)
                total = total + mm_tn(ain_ref[4 * i : 4 * i + 4].reshape(4 * ROWS, width), grads)
                sq_ref[:, lo:hi] += fold8(grads.astype(f32))
            return total

        def pad(end, stop):
            if end < stop:
                own2_ref[end:stop] = jnp.zeros((stop - end, 16, 128), bf16)

        pad(pack_matrix(own2_ref, 0, weights(0, early_cols)), cut2)
        three.send(0)
        late = weights(early_cols, 3 * width)
        three.take(0)
        three.send(1)
        pad(pack_matrix(own2_ref, cut2, late), own2_ref.shape[0])
        four.send(0)

    at(norm_step + 1, (four.take, 0), (four.send, 1), (one.settle, 1), (one.spread, 0))
    at(norm_step + 4, (three.take, 1), (three.send, 2), (two.settle, 1), (two.spread, 0))

    @pl.when(step == norm_step + 6)
    def _():
        for total in (one, two, side):
            total.settle(0)
        keep.start()

    at(norm_step + 7, (four.take, 1), (four.send, 2))

    @pl.when(step > frames)
    def _():
        i = step - norm_step
        block = 2 * ROWS
        x = x_ref[pl.ds(2 * i, 2)].reshape(block, width).astype(f32)
        n, inverse = normed_of(x)
        up = mm_nt(grads_of(i * block, block, 0, 3 * width), wqkv_ref[...])
        gres = gres_ref[...].reshape(block, width)
        narrow_into(in_ref, 0, gres + norm_back(up, n, inverse, row_ref[:, :width]))
        s384_ref[0] += fold8(up * n)
        s384_ref[1] += fold8(up)

    @pl.when(step == steps - 1)
    def _():
        sq = colsum(sq_ref[...])
        parts = [colsum(s384_ref[0]), colsum(s384_ref[1]), sq[:, :width], sq[:, 2 * width :]]
        lines = [v[:, c : c + 128] for v in parts for c in range(0, width, 128)]
        lines += [jnp.zeros((1, 128), f32)] * (16 - len(lines))
        rows.spread(last, jnp.concatenate(lines, axis=0))
        for i in range(2, count):
            for total in (three, four):
                total.take(i)
                if i < last:
                    total.send(i + 1)
                else:
                    total.spread(last)
        for i in range(last, 0, -1):
            tile = rows.settle(i)
            rows.spread(i - 1, tile)
            for total in (three, four):
                total.settle(i)
                total.spread(i - 1)
        rows_ref[...] = rows.settle(0)
        three.settle(0)
        four.settle(0)
        res2_ref[...] = sum2_ref[...]
        keep.wait()


def unpack_kernel(cut2, in_hbm, res_hbm, res2_ref, rows_ref, out_hbm, gg1, gb1, gqkv_hbm, gqv, gwo_hbm, gbo, gg2, gb2, gw1_hbm,
                  gbf1, gw2_hbm, gbf2, gqkv, gwo, gw1, gw2, res_ref, mid_ref, sems):
    width, hidden = gw1.shape
    tiles = width // 16
    across = hidden // 128 * tiles
    pieces = 4
    piece = in_hbm.shape[0] // pieces
    come, go = [], []
    for i in range(pieces):
        rows = slice(i * piece, (i + 1) * piece)
        come.append(pltpu.make_async_copy(in_hbm.at[rows], mid_ref.at[rows], sems.at[7 + i]))
        go.append(pltpu.make_async_copy(mid_ref.at[rows], out_hbm.at[rows], sems.at[7 + pieces + i]))
    parts = (0, across, 2 * across, res_hbm.shape[0])
    loads = [
        pltpu.make_async_copy(res_hbm.at[lo:hi], res_ref.at[lo:hi], sems.at[i])
        for i, (lo, hi) in enumerate(zip(parts, parts[1:]))
    ]
    stores = [
        pltpu.make_async_copy(src, dst, sems.at[3 + i])
        for i, (src, dst) in enumerate(((gqkv, gqkv_hbm), (gwo, gwo_hbm), (gw1, gw1_hbm), (gw2, gw2_hbm)))
    ]
    for copy in come + loads:
        copy.start()
    for i in range(pieces):
        come[i].wait()
        go[i].start()
    early = 3 * width // 128 // 2
    for c in range(3 * width // 128):
        at = c * tiles if c < early else cut2 + (c - early) * tiles
        gqkv[:, 128 * c : 128 * c + 128] = res2_ref[at : at + tiles].reshape(width, 128).astype(f32)
    stores[0].start()
    loads[0].wait()
    at = 0
    for c in range(hidden // 128):
        gw1[:, 128 * c : 128 * c + 128] = res_ref[at : at + tiles].reshape(width, 128).astype(f32)
        at += tiles
    stores[2].start()
    loads[1].wait()
    for c in range(hidden // 128):
        gw2[128 * c : 128 * c + 128, :] = res_ref[at : at + tiles].reshape(width, 128).astype(f32).T
        at += tiles
    stores[3].start()
    loads[2].wait()
    for c in range(width // 128):
        gwo[:, 128 * c : 128 * c + 128] = res_ref[at : at + tiles].reshape(width, 128).astype(f32)
        at += tiles
    stores[1].start()
    row = 0
    for out in (gg2, gb2, gbo, gbf2, gbf1):
        for c in range(out.shape[0] // 128):
            out[128 * c : 128 * c + 128] = res_ref[at + row // 16].astype(f32)[row % 16]
            row += 1
    rows = rows_ref[...]
    each = width // 128
    for i, out in enumerate((gg1, gb1)):
        for c in range(each):
            out[128 * c : 128 * c + 128] = rows[i * each + c]
    for i in range(2):
        for c in range(each):
            gqv[i : i + 1, 128 * c : 128 * c + 128] = rows[(i + 2) * each + c : (i + 2) * each + c + 1]
    for copy in stores + go:
        copy.wait()


def whole(shape):
    return pl.BlockSpec(shape, lambda i: (0,) * len(shape), pipeline_mode=pl.Buffered(1))


def pairs(shape):
    return pl.BlockSpec((2,) + shape, lambda i: (i,) + (0,) * len(shape))


def single(shape):
    return pl.BlockSpec((1,) + shape, lambda i: (i,) + (0,) * len(shape))


def params(collective=None):
    if collective is None:
        return pltpu.CompilerParams(vmem_limit_bytes=60 * 2**20)
    return pltpu.CompilerParams(vmem_limit_bytes=60 * 2**20, collective_id=collective, has_side_effects=True)


def per_device(tokens, frame_clip, ln1_gain, ln1_bias, w_qkv, qv_bias, w_out, b_out, ln2_gain, ln2_bias,
               w_fc1, b_fc1, w_fc2, b_fc2, cotangent):
    count, width = tokens.shape
    hidden = w_fc1.shape[1]
    frames = count // FRAME
    steps = frames // 2
    tm = lax.axis_index("tm")
    edge = jnp.where(tm == 0, tokens[count - ROWS :], tokens[:ROWS])
    ghost = lax.ppermute(edge, "tm", [(0, 1), (1, 0)])
    in_vmem = pl.BlockSpec(memory_space=pltpu.VMEM)
    in_hbm = pl.BlockSpec(memory_space=pl.ANY)
    kv_rows = (frames + 2) * ROWS + WIN - 3 * ROWS
    shape = jax.ShapeDtypeStruct
    stages = stages_of(lax.axis_size("clips"))
    devices = 2 * lax.axis_size("clips")
    tiles = width // 16
    units = units_for((2 * hidden + width) // 128 * tiles + 2, devices)
    across2 = 3 * width // 128
    first2 = units_for(across2 // 2 * tiles, devices)
    second2 = units_for((across2 - across2 // 2) * tiles, devices)
    units2 = first2 + second2
    x_pad, ain, kv, prob, block_out, qs, ga, gs, gres, li, row, pack = pl.pallas_call(
        forward_kernel,
        grid=(steps,),
        in_specs=[
            pl.BlockSpec(memory_space=pltpu.SMEM),
            in_hbm,
            whole((ROWS, width)),
            whole((width,)),
            whole((width,)),
            whole((2, width)),
            whole((width,)),
            whole((width,)),
            whole((width,)),
            whole((hidden,)),
            whole((width,)),
            whole((width, 3 * width)),
            in_hbm,
            in_hbm,
            in_hbm,
            in_hbm,
        ],
        out_specs=[
            in_hbm,
            in_hbm,
            in_hbm,
            pairs((HEADS // 2, 2 * ROWS, WIN)),
            pl.BlockSpec((4 * FRAME, width), lambda i: (i // 2, 0)),
            pairs((ROWS, width)),
            pairs((HEADS // 2, 2 * ROWS, 128 + EXTRA)),
            pairs((ROWS, width)),
            pairs((ROWS, width)),
            pairs((ROWS, width)),
            whole((1, 9 * width + hidden)),
            whole((units, 16, 128)),
        ],
        out_shape=[
            shape((frames, ROWS, width), bf16),
            shape((frames, ROWS, width), bf16),
            shape((kv_rows, 2 * width), bf16),
            shape((frames, HEADS // 2, 2 * ROWS, WIN), bf16),
            shape((count, width), bf16),
            shape((frames, ROWS, width), bf16),
            shape((frames, HEADS // 2, 2 * ROWS, 128 + EXTRA), bf16),
            shape((frames, ROWS, width), bf16),
            shape((frames, ROWS, width), f32),
            shape((frames, ROWS, width), f32),
            shape((1, 9 * width + hidden), f32),
            shape((units, 16, 128), bf16),
        ],
        scratch_shapes=[
            pltpu.VMEM((frames, ROWS, width), bf16),
            pltpu.VMEM((frames, ROWS, width), bf16),
            pltpu.VMEM((kv_rows, 2 * width), bf16),
            pltpu.VMEM((count, width), bf16),
            pltpu.VMEM((width, width), bf16),
            pltpu.VMEM((width, hidden), bf16),
            pltpu.VMEM((hidden, width), bf16),
            pltpu.VMEM((frames, ROWS, width), bf16),
            pltpu.VMEM((frames, ROWS, width), bf16),
            pltpu.VMEM((kv_rows, 128), bf16),
            pltpu.VMEM((3, 2 * ROWS, WIN), f32),
            pltpu.VMEM((2 * ROWS, width), f32),
            pltpu.VMEM((4 * FRAME, width), f32),
            pltpu.VMEM((width, hidden), f32),
            pltpu.VMEM((width, hidden), f32),
            pltpu.VMEM((width, width), f32),
            pltpu.VMEM((8, hidden), f32),
            pltpu.VMEM((4, 8, width), f32),
            pltpu.SemaphoreType.DMA((8,)),
        ],
        compiler_params=params(),
    )(frame_clip, tokens, ghost, ln1_gain, ln1_bias, qv_bias, b_out, ln2_gain, ln2_bias, b_fc1, b_fc2, w_qkv, cotangent,
      w_out, w_fc1, w_fc2)

    first, second, side = shares(units, devices)
    early = lambda sh: pl.BlockSpec((1,) + sh, lambda i: (jnp.minimum(i, frames - 1),) + (0,) * len(sh))
    late = lambda i: jnp.maximum(i - frames - 1, 0)
    input_grad, res, res2, sums = pl.pallas_call(
        functools.partial(back_kernel, stages),
        grid=(frames + 1 + steps,),
        in_specs=[
            early((HEADS // 2, 2 * ROWS, WIN)),
            in_hbm,
            early((HEADS // 2, 2 * ROWS, 128 + EXTRA)),
            early((ROWS, width)),
            early((ROWS, width)),
            early((ROWS, width)),
            in_hbm,
            in_hbm,
            pl.BlockSpec((2, ROWS, width), lambda i: (late(i), 0, 0)),
            whole(row.shape),
            in_hbm,
            in_hbm,
        ],
        out_specs=[
            pl.BlockSpec((2 * FRAME, width), lambda i: (late(i), 0)),
            in_hbm,
            whole((units2, 16, 128)),
            whole((16, 128)),
        ],
        out_shape=[
            shape((count, width), f32),
            shape((units, 16, 128), bf16),
            shape((units2, 16, 128), bf16),
            shape((16, 128), f32),
        ],
        scratch_shapes=[
            pltpu.VMEM((kv_rows, 2 * width), f32),
            pltpu.VMEM((3, 2 * ROWS, WIN), f32),
            pltpu.VMEM((3, 2 * ROWS, WIN), bf16),
            pltpu.VMEM((frames * ROWS, width), bf16),
            pltpu.VMEM((8, 3 * width), f32),
            pltpu.VMEM((2, 8, width), f32),
            pltpu.VMEM((units, 16, 128), bf16),
            pltpu.VMEM((units, 16, 128), bf16),
            pltpu.VMEM((units2, 16, 128), bf16),
            pltpu.VMEM((units2, 16, 128), bf16),
            pltpu.VMEM((ROWS, 2 * width), bf16),
            pltpu.VMEM((ROWS, 2 * width), bf16),
            pltpu.VMEM((kv_rows, 2 * width), bf16),
            pltpu.VMEM((frames, ROWS, width), bf16),
            pltpu.VMEM((frames, ROWS, width), bf16),
            pltpu.VMEM((width, 3 * width), bf16),
            pltpu.SemaphoreType.DMA((2,)),
            pltpu.SemaphoreType.DMA((7,)),
        ]
        + sum_scratch(stages, first)
        + sum_scratch(stages, second)
        + sum_scratch(turned(stages), side)
        + sum_scratch(stages, first2)
        + sum_scratch(stages, second2)
        + rows_scratch(stages),
        compiler_params=params(0),
    )(prob, kv, ga, gs, qs, li, x_pad, ain, gres, row, w_qkv, pack)

    sizes = [(width,), (width,), (width, 3 * width), (2, width), (width, width), (width,), (width,), (width,),
             (width, hidden), (hidden,), (hidden, width), (width,)]
    big = [len(z) == 2 and z[0] > 2 for z in sizes]
    outs = pl.pallas_call(
        functools.partial(unpack_kernel, first2),
        in_specs=[in_hbm, in_hbm, in_vmem, in_vmem],
        out_specs=[in_hbm] + [in_hbm if far else in_vmem for far in big],
        out_shape=[shape((count, width), f32)] + [shape(z, f32) for z in sizes],
        scratch_shapes=[
            pltpu.VMEM((width, 3 * width), f32),
            pltpu.VMEM((width, width), f32),
            pltpu.VMEM((width, hidden), f32),
            pltpu.VMEM((hidden, width), f32),
            pltpu.VMEM((units, 16, 128), bf16),
            pltpu.VMEM((count, width), f32),
            pltpu.SemaphoreType.DMA((15,)),
        ],
        compiler_params=params(),
    )(input_grad, res, res2, sums)
    return (block_out,) + tuple(outs)


def solution(mesh):
    rows = P(("clips", "tm"), None)
    rep = P()
    return jax.shard_map(
        per_device,
        mesh=mesh,
        in_specs=(rows, P("clips")) + (rep,) * 12 + (rows,),
        out_specs=(rows, rows) + (rep,) * 12,
        check_vma=False,
    )
```

```python
import functools
import math

import jax
import jax.numpy as jnp
from jax import lax
from jax.experimental import pallas as pl
from jax.experimental.pallas import tpu as pltpu
from jax.sharding import PartitionSpec as P

HEADS = 6
FRAME = 196
ROWS = 208
WIN = 640
EXTRA = 16
EPS = 1e-6
LOG2E = math.log2(math.e)

bf16 = jnp.bfloat16
f32 = jnp.float32


def mm(a, b):
    return jnp.dot(a, b, preferred_element_type=f32)


def mm_nt(a, b):
    return lax.dot_general(a, b, (((1,), (1,)), ((), ())), preferred_element_type=f32)


def mm_tn(a, b):
    return lax.dot_general(a, b, (((0,), (0,)), ((), ())), preferred_element_type=f32)


def normed_of(x):
    mean = jnp.mean(x, axis=-1, keepdims=True)
    centred = x - mean
    var = jnp.mean(centred * centred, axis=-1, keepdims=True)
    inverse = lax.rsqrt(var + EPS)
    return centred * inverse, inverse


def norm_back(upstream, normed, inverse, gain):
    scaled = upstream * gain
    mean = jnp.mean(scaled, axis=-1, keepdims=True)
    along = jnp.mean(scaled * normed, axis=-1, keepdims=True)
    return inverse * (scaled - mean - normed * along)


def fold8(v):
    rows, cols = v.shape
    return jnp.sum(v.reshape(rows // 8, 8, cols), axis=0)


MESH = pl.DeviceIdType.MESH


def stages_of(clips):
    stages, stride = [("tm", 1, 2)], 1
    while clips > 1:
        size = 4 if clips % 4 == 0 else (2 if clips % 2 == 0 else clips)
        stages.append(("clips", stride, size))
        stride, clips = stride * size, clips // size
    return stages


def digit(stage):
    axis, stride, size = stage
    return lax.rem(lax.axis_index(axis) // stride, size)


def partner(stage, turn):
    axis, stride, size = stage
    mine = digit(stage)
    return {axis: lax.axis_index(axis) + (lax.rem(mine + turn, size) - mine) * stride}


def greet(stages):
    sem, count = pltpu.get_barrier_semaphore(), 0
    for stage in stages:
        for turn in range(1, stage[2]):
            pl.semaphore_signal(sem, inc=1, device_id=partner(stage, turn), device_id_type=MESH)
            count += 1
    pl.semaphore_wait(sem, count)


class Sum:
    def __init__(self, stages, pack, result, landing, sent, came):
        self.stages, self.pack, self.result, self.landing = stages, pack, result, landing
        self.sent, self.came = sent, came
        self.segments, start, length = [], 0, pack.shape[0]
        for stage in stages:
            self.segments.append((start, length))
            length = length // stage[2]
            start = start + digit(stage) * length
        self.segments.append((start, length))
        self.first = [sum(s[2] - 1 for s in stages[:i]) for i in range(len(stages) + 1)]

    def _scatter(self, i):
        stage, (start, length) = self.stages[i], self.segments[i]
        part = length // stage[2]
        for turn in range(1, stage[2]):
            slot = self.first[i] + turn - 1
            other = lax.rem(digit(stage) + turn, stage[2])
            yield pltpu.make_async_remote_copy(
                src_ref=self.pack.at[pl.ds(start + other * part, part)],
                dst_ref=self.landing[i].at[turn - 1],
                send_sem=self.sent.at[slot],
                recv_sem=self.came.at[slot],
                device_id=partner(stage, turn),
                device_id_type=MESH,
            )

    def _gather(self, i):
        stage, (start, length) = self.stages[i], self.segments[i + 1]
        for turn in range(1, stage[2]):
            slot = self.first[-1] + self.first[i] + turn - 1
            here = self.result.at[pl.ds(start, length)]
            yield pltpu.make_async_remote_copy(
                src_ref=here,
                dst_ref=here,
                send_sem=self.sent.at[slot],
                recv_sem=self.came.at[slot],
                device_id=partner(stage, turn),
                device_id_type=MESH,
            )

    def send(self, i):
        for copy in self._scatter(i):
            copy.start()

    def take(self, i):
        for copy in self._scatter(i):
            copy.wait()
        start, length = self.segments[i + 1]
        into = self.result if i == len(self.stages) - 1 else self.pack
        block = next(b for b in (28, 24, 21, 16, 14, 12, 8, 7, 6, 4, 3, 2, 1) if length % b == 0)

        def add(j, carry):
            total = self.pack[pl.ds(start + j * block, block)].astype(f32)
            for turn in range(1, self.stages[i][2]):
                total = total + self.landing[i][turn - 1, pl.ds(j * block, block)].astype(f32)
            into[pl.ds(start + j * block, block)] = total.astype(bf16)
            return carry

        lax.fori_loop(0, length // block, add, 0)

    def spread(self, i):
        for copy in self._gather(i):
            copy.start()

    def settle(self, i):
        for copy in self._gather(i):
            copy.wait()


def sum_scratch(stages, units):
    shapes, left = [], units
    for stage in stages:
        left //= stage[2]
        shapes.append(pltpu.VMEM((stage[2] - 1, left, 16, 128), bf16))
    copies = 2 * sum(s[2] - 1 for s in stages)
    return shapes + [pltpu.SemaphoreType.DMA((copies,)), pltpu.SemaphoreType.DMA((copies,))]


def pack_matrix(pack, first, value):
    rows, cols = value.shape
    tiles = rows // 16
    for c in range(cols // 128):
        pack[first + c * tiles : first + (c + 1) * tiles] = (
            value[:, 128 * c : 128 * (c + 1)].astype(bf16).reshape(tiles, 16, 128)
        )
    return first + cols // 128 * tiles


def pack_rows(pack, first, vectors):
    rows = [v[:, c : c + 128] for v in vectors for c in range(0, v.shape[1], 128)]
    rows += [jnp.zeros((1, 128), f32)] * (-len(rows) % 16)
    for r in range(0, len(rows), 16):
        pack[first + r // 16] = jnp.concatenate(rows[r : r + 16], axis=0).astype(bf16)
    last = first + len(rows) // 16
    if last < pack.shape[0]:
        pack[last:] = jnp.zeros((pack.shape[0] - last, 16, 128), bf16)


def unpack_matrix(res, first, rows, cols):
    tiles = rows // 16
    part = res[first : first + cols // 128 * tiles].reshape(cols // 128, tiles, 16, 128)
    return part.transpose(1, 2, 0, 3).reshape(rows, cols).astype(f32)


def units_for(needed, devices):
    return -(-needed // devices) * devices


def colsum(v):
    return jnp.sum(v, axis=0, keepdims=True)


def widen(ref, group, which):
    start = which * FRAME // 16 * 16
    shift = which * FRAME - start
    v = ref[pl.ds(pl.multiple_of(group * 4 * FRAME + start, 16), ROWS), :].astype(f32)
    if shift:
        v = pltpu.roll(v, ROWS - shift, 0)
    row = lax.broadcasted_iota(jnp.int32, (16, v.shape[1]), 0)
    return v, jnp.where(row < 16 - (ROWS - FRAME), v[ROWS - 16 :], 0.0)


def narrow_into(ref, start, v):
    edge = FRAME // 8 * 8
    over = FRAME - edge
    second = pltpu.roll(v[ROWS:], over, 0)
    row = lax.broadcasted_iota(jnp.int32, (8, v.shape[1]), 0)
    ref[pl.ds(pl.multiple_of(start, 8), edge), :] = v[:edge]
    ref[pl.ds(pl.multiple_of(start + edge, 8), 8), :] = jnp.where(row < over, v[edge : edge + 8], second[:8])
    rest = 2 * FRAME - edge - 8
    ref[pl.ds(pl.multiple_of(start + edge + 8, 8), rest), :] = second[8 : 8 + rest]


def forward_kernel(
    clip_ref,
    tok_hbm,
    ghost_ref,
    g1_ref,
    s1_ref,
    qv_ref,
    bo_ref,
    g2_ref,
    s2_ref,
    bf1_ref,
    bf2_ref,
    wqkv_ref,
    cot_hbm,
    wout_hbm,
    w1_hbm,
    w2_hbm,
    x_hbm,
    ain_hbm,
    kv_hbm,
    prob_ref,
    out_ref,
    qs_ref,
    ga_ref,
    gs_ref,
    gres_ref,
    li_ref,
    row_ref,
    pack_ref,
    x_ref,
    ain_ref,
    kv_ref,
    raw_ref,
    wout_ref,
    w1_ref,
    w2_ref,
    q_ref,
    cp_ref,
    flag_ref,
    s_ref,
    o_ref,
    flat_ref,
    gw1_ref,
    gw2_ref,
    gwo_ref,
    sb1_ref,
    s384_ref,
    sems,
):
    step = pl.program_id(0)
    steps = pl.num_programs(0)
    frames = x_ref.shape[0]
    width = x_ref.shape[-1]
    hidden = w1_ref.shape[-1]
    tm = lax.axis_index("tm")
    copies = [
        pltpu.make_async_copy(src, dst, sems.at[i])
        for i, (src, dst) in enumerate(
            ((cot_hbm, raw_ref), (wout_hbm, wout_ref), (w1_hbm, w1_ref), (w2_hbm, w2_ref), (x_ref, x_hbm), (kv_ref, kv_hbm),
             (ain_ref, ain_hbm), (tok_hbm, raw_ref))
        )
    ]

    @pl.when(step == 0)
    def _():
        copies[7].start()
        for copy in copies[1:4]:
            copy.start()
        vectors = [g1_ref[...], s1_ref[...], None, None, None, bo_ref[...], g2_ref[...], s2_ref[...], bf2_ref[...]]
        for i, v in enumerate(vectors):
            if v is not None:
                row_ref[:, i * width : (i + 1) * width] = v.astype(f32)[None, :]
        row_ref[:, 2 * width : 3 * width] = qv_ref[0:1, :].astype(f32)
        row_ref[:, 3 * width : 4 * width] = jnp.zeros((1, width), f32)
        row_ref[:, 4 * width : 5 * width] = qv_ref[1:2, :].astype(f32)
        row_ref[:, 9 * width :] = bf1_ref[...].astype(f32)[None, :]

    vec = lambda i, n=width: row_ref[:, i * width : i * width + n]
    gain1, shift1, bias3, biaso, gain2, shift2, bias2, bias1 = (
        vec(0), vec(1), vec(2, 3 * width), vec(5), vec(6), vec(7), vec(8), vec(9, hidden))

    @pl.when(step == 0)
    def _():
        gw1_ref[...] = jnp.zeros_like(gw1_ref)
        gw2_ref[...] = jnp.zeros_like(gw2_ref)
        gwo_ref[...] = jnp.zeros_like(gwo_ref)
        sb1_ref[...] = jnp.zeros_like(sb1_ref)
        s384_ref[...] = jnp.zeros_like(s384_ref)
        at = lax.broadcasted_iota(jnp.int32, flag_ref.shape, 0)
        lane = lax.broadcasted_iota(jnp.int32, flag_ref.shape, 1)
        slot = at // ROWS
        flag_ref[...] = jnp.where(
            lane == 0,
            jnp.where(at - slot * ROWS < FRAME, 0.0, -1e30),
            jnp.where(lane == 1 + slot % 4, 1.0, 0.0),
        ).astype(bf16)
        zero_slot = jnp.where(tm == 0, 0, frames + 1)
        ghost_slot = frames + 1 - zero_slot
        kv_ref[pl.ds(pl.multiple_of(zero_slot * ROWS, 16), ROWS), :] = jnp.zeros((ROWS, 2 * width), bf16)
        kv_ref[(frames + 2) * ROWS :, :] = jnp.zeros((WIN - 3 * ROWS, 2 * width), bf16)

        x = ghost_ref[...].astype(f32)
        x = jnp.where(tm == 0, x, pltpu.roll(x, FRAME, 0))
        n, _ = normed_of(x)
        kv = mm((n * gain1 + shift1).astype(bf16), wqkv_ref[:, width:]) + bias3[:, width:]
        kv_ref[pl.ds(pl.multiple_of(ghost_slot * ROWS, 16), ROWS), :] = kv.astype(bf16)

        def pad(i, src, dst):
            for which in range(4):
                v, end = widen(src, i, which)
                dst[4 * i + which, : ROWS - 16] = v[: ROWS - 16].astype(bf16)
                dst[4 * i + which, ROWS - 16 :] = end.astype(bf16)

        def ready(i):
            x = x_ref[4 * i : 4 * i + 4].reshape(4 * ROWS, width).astype(f32)
            n, _ = normed_of(x)
            normed = (n * gain1 + shift1).astype(bf16)
            ain_ref[4 * i : 4 * i + 4] = normed.reshape(4, ROWS, width)
            return normed

        def project(i, normed):
            qkv = (mm(normed, wqkv_ref[...]) + bias3).astype(bf16)
            q_ref[4 * i : 4 * i + 4] = qkv[:, :width].reshape(4, ROWS, width)
            kv_ref[(4 * i + 1) * ROWS : (4 * i + 5) * ROWS, :] = qkv[:, width:]

        copies[7].wait()
        for i in range(frames // 4):
            pad(i, raw_ref, x_ref)
        copies[0].start()
        normed = ready(0)
        for i in range(frames // 4):
            following = ready(i + 1) if i + 1 < frames // 4 else None
            project(i, normed)
            normed = following
        for copy in copies[4:7]:
            copy.start()
        for copy in copies[:4]:
            copy.wait()
        for i in range(frames // 4):
            pad(i, raw_ref, cp_ref)

    low = lax.broadcasted_iota(jnp.int32, (ROWS, 128), 1) < 64
    lane = lax.broadcasted_iota(jnp.int32, (1, 128), 1)
    scale = LOG2E / math.sqrt(width // HEADS)
    twins = HEADS // 2
    flags, windows = [], []
    for sub in range(2):
        frame = 2 * step + sub
        here = tm * frames + frame
        own = clip_ref[here]
        before = jnp.where(here > 0, clip_ref[jnp.maximum(here - 1, 0)], -1)
        after = jnp.where(here < 2 * frames - 1, clip_ref[jnp.minimum(here + 1, 2 * frames - 1)], -1)
        none = jnp.float32(-1e30)
        row = jnp.where(lane == 0, 1.0, 0.0)
        row = jnp.where(lane == 1 + frame % 4, jnp.where(before == own, 0.0, none), row)
        row = jnp.where(lane == 1 + (frame + 2) % 4, jnp.where(after == own, 0.0, none), row)
        row = jnp.where(lane == 1 + (frame + 3) % 4, none, row)
        flags.append(jnp.broadcast_to(row.astype(bf16), (2 * ROWS, 128))[:, :EXTRA])
        windows.append(pl.ds(pl.multiple_of(frame * ROWS, 16), WIN))

    def score(t):
        sub, pair = divmod(t, twins)
        cols = slice(pair * 128, pair * 128 + 128)
        q = q_ref[2 * step + sub, :, cols]
        zero = jnp.zeros_like(q)
        both = jnp.concatenate([jnp.where(low, q, zero), jnp.where(low, zero, q)], axis=0)
        k = jnp.concatenate([kv_ref[windows[sub], cols], flag_ref[windows[sub], :EXTRA]], axis=1)
        s_ref[t % 3] = mm_nt(jnp.concatenate([both, flags[sub]], axis=1), k)

    inverses = {}

    def soften(t):
        sub, pair = divmod(t, twins)
        s = s_ref[t % 3]
        top = jnp.max(s, axis=-1, keepdims=True)
        e = jnp.exp2((s - top) * scale)
        inverses[t] = 1.0 / jnp.sum(e, axis=-1, keepdims=True)
        prob_ref[sub, pair] = e.astype(bf16)

    def attend(t):
        sub, pair = divmod(t, twins)
        at = pair * 128
        o = mm(prob_ref[sub, pair], kv_ref[windows[sub], width + at : width + at + 128])
        inverse = jnp.where(low, inverses[t][:ROWS], inverses[t][ROWS:])
        rows = slice(sub * ROWS, (sub + 1) * ROWS)
        o_ref[rows, at : at + 128] = jnp.where(low, o[:ROWS], o[ROWS:]) * inverse
        li_ref[sub, :, at : at + 128] = inverse

    score(0)
    for t in range(2 * twins + 1):
        if t + 1 < 2 * twins:
            score(t + 1)
        if t >= 1:
            attend(t - 1)
        if t < 2 * twins:
            soften(t)

    att = o_ref[...].astype(bf16)
    both = pl.ds(2 * step, 2)
    x = x_ref[both].reshape(2 * ROWS, width).astype(f32)
    resid = x + mm(att, wout_ref[...]) + biaso
    n2, inv2 = normed_of(resid)
    mlp_in = (n2 * gain2 + shift2).astype(bf16)
    cot = cp_ref[both].reshape(2 * ROWS, width)
    chunk = 512
    chunks = [slice(c, c + chunk) for c in range(0, hidden, chunk)]
    held = {}

    def start(c):
        held[c] = mm(mlp_in, w1_ref[:, chunks[c]]), mm_nt(cot, w2_ref[chunks[c], :])

    def middle(c):
        pre, ghid = held[c]
        pre = pre + bias1[:, chunks[c]]
        cdf = 0.5 + 0.5 * lax.erf(pre * (1.0 / math.sqrt(2.0)))
        dens = jnp.exp2(pre * pre * (-0.5 * LOG2E)) * (1.0 / math.sqrt(2.0 * math.pi))
        gpre = (ghid * (cdf + pre * dens)).astype(bf16)
        sb1_ref[:, chunks[c]] += fold8(gpre.astype(f32))
        held[c] = (pre * cdf).astype(bf16), gpre

    def weights(c):
        gw2_ref[:, chunks[c]] += mm_tn(cot, held[c][0])
        gw1_ref[:, chunks[c]] += mm_tn(mlp_in, held[c][1])

    start(0)
    for c in range(len(chunks)):
        if c + 1 < len(chunks):
            start(c + 1)
        middle(c)
    hid = jnp.concatenate([held[c][0] for c in range(len(chunks))], axis=1)
    gpre = jnp.concatenate([held[c][1] for c in range(len(chunks))], axis=1)
    up = mm_nt(gpre, w1_ref[...])
    cot32 = cot.astype(f32)
    gres = cot32 + norm_back(up, n2, inv2, gain2)
    gres_ref[...] = gres.reshape(2, ROWS, width)
    branch = gres.astype(bf16)
    weights(0)
    g = mm_nt(branch, wout_ref[...]).astype(bf16)
    for c in range(1, len(chunks) - 1):
        weights(c)
    g32 = g.astype(f32)
    inverse = li_ref[...].reshape(2 * ROWS, width)
    gs_ref[...] = (g32 * inverse).astype(bf16).reshape(2, ROWS, width)
    qs_ref[...] = (q_ref[both].reshape(2 * ROWS, width).astype(f32) * inverse).astype(bf16).reshape(2, ROWS, width)
    dots = g32 * o_ref[...]
    some = lax.broadcasted_iota(jnp.int32, (2 * ROWS, EXTRA), 1)
    for sub in range(2):
        for pair in range(twins):
            rows, cols = slice(sub * ROWS, (sub + 1) * ROWS), slice(128 * pair, 128 * pair + 128)
            d = dots[rows, cols]
            even = jnp.sum(jnp.where(low, d, 0.0), axis=-1, keepdims=True)
            odd = jnp.sum(jnp.where(low, 0.0, d), axis=-1, keepdims=True)
            less = jnp.broadcast_to(-jnp.concatenate([even, odd], axis=0), (2 * ROWS, EXTRA))
            one = less.astype(bf16).astype(f32)
            two = (less - one).astype(bf16).astype(f32)
            three = less - one - two
            ga_ref[sub, pair, :, 128 : 128 + EXTRA] = jnp.where(
                some == 0, one, jnp.where(some == 1, two, jnp.where(some == 2, three, 0.0))
            ).astype(bf16)
            gp = g[rows, cols]
            zero = jnp.zeros_like(gp)
            ga_ref[sub, pair, :ROWS, :128] = jnp.where(low, gp, zero)
            ga_ref[sub, pair, ROWS:, :128] = jnp.where(low, zero, gp)
    s384_ref[0] += fold8(up * n2)
    s384_ref[1] += fold8(up)
    s384_ref[2] += fold8(branch.astype(f32))
    s384_ref[3] += fold8(cot32)
    weights(len(chunks) - 1)
    gwo_ref[...] += mm_tn(att, branch)
    out = resid + bias2 + mm(hid, w2_ref[...])
    narrow_into(flat_ref, step % 2 * 2 * FRAME, out)

    @pl.when(step % 2 == 1)
    def _():
        out_ref[...] = flat_ref[...].astype(bf16)

    @pl.when(step == steps - 1)
    def _():
        at = pack_matrix(pack_ref, 0, gw1_ref[...])
        at = pack_matrix(pack_ref, at, gw2_ref[...])
        at = pack_matrix(pack_ref, at, gwo_ref[...])
        pack_rows(pack_ref, at, [colsum(s384_ref[i]) for i in range(4)] + [colsum(sb1_ref[...])])
        for copy in copies[4:7]:
            copy.wait()


class Rows:
    def __init__(self, stages, boards, sent, came):
        self.stages, self.boards, self.sent, self.came = stages, boards, sent, came
        self.first = [sum(s[2] - 1 for s in stages[:i]) for i in range(len(stages) + 1)]

    def _copies(self, i):
        stage = self.stages[i]
        here = self.boards[i].at[digit(stage)]
        for turn in range(1, stage[2]):
            slot = self.first[i] + turn - 1
            yield pltpu.make_async_remote_copy(
                src_ref=here,
                dst_ref=here,
                send_sem=self.sent.at[slot],
                recv_sem=self.came.at[slot],
                device_id=partner(stage, turn),
                device_id_type=MESH,
            )

    def spread(self, i, tile):
        self.boards[i][digit(self.stages[i])] = tile
        for copy in self._copies(i):
            copy.start()

    def settle(self, i):
        for copy in self._copies(i):
            copy.wait()
        total = self.boards[i][0]
        for j in range(1, self.stages[i][2]):
            total = total + self.boards[i][j]
        return total


def rows_scratch(stages):
    copies = sum(s[2] - 1 for s in stages)
    return [pltpu.VMEM((s[2], 16, 128), f32) for s in stages] + [pltpu.SemaphoreType.DMA((copies,))] * 2


def shares(units, devices):
    blocks = units // devices
    side = max(1, round(blocks / 7))
    first = -(-(blocks - side) // 2)
    return first * devices, (blocks - side - first) * devices, side * devices


def turned(stages):
    return stages[:1] + stages[:0:-1]


def back_kernel(stages, prob_ref, kv_hbm, ga_ref, gs_ref, qs_ref, li_ref, x_hbm, ain_hbm, gres_ref, row_ref,
                wqkv_hbm, pack_hbm, in_ref, res_hbm, res2_ref, rows_ref,
                acc_ref, d_ref, ds_ref, dq_ref, sq_ref, s384_ref, own_ref, sum_ref, own2_ref, sum2_ref,
                ghost_ref, got_ref, kv_ref, x_ref, ain_ref, wqkv_ref, ghost_sems, load_sems, *rest):
    step = pl.program_id(0)
    width = gs_ref.shape[-1]
    frames = x_hbm.shape[0]
    steps = frames + 1 + frames // 2
    tm = lax.axis_index("tm")
    inv_scale = 1.0 / math.sqrt(width // HEADS)
    count = len(stages)
    last = count - 1
    devices = 2
    for stage in stages[1:]:
        devices *= stage[2]
    first, second, _ = shares(own_ref.shape[0], devices)
    both = first + second
    tiles = width // 16
    early_cols = 3 * width // 128 // 2 * 128
    cut2 = units_for(early_cols // 128 * tiles, devices)
    sums = []
    for n, (route, own, res) in enumerate(
        (
            (stages, own_ref.at[:first], sum_ref.at[:first]),
            (stages, own_ref.at[first:both], sum_ref.at[first:both]),
            (turned(stages), own_ref.at[both:], sum_ref.at[both:]),
            (stages, own2_ref.at[:cut2], sum2_ref.at[:cut2]),
            (stages, own2_ref.at[cut2:], sum2_ref.at[cut2:]),
        )
    ):
        mine = rest[n * (count + 2) : (n + 1) * (count + 2)]
        sums.append(Sum(route, own, res, mine[:count], *mine[count:]))
    one, two, side, three, four = sums
    extra = rest[5 * (count + 2) :]
    rows = Rows(stages, extra[:count], *extra[count:])
    near = 6 * ROWS
    loads = [
        pltpu.make_async_copy(src, dst, load_sems.at[i])
        for i, (src, dst) in enumerate(
            (
                (pack_hbm, own_ref),
                (kv_hbm.at[:near], kv_ref.at[:near]),
                (kv_hbm.at[near:], kv_ref.at[near:]),
                (x_hbm, x_ref),
                (ain_hbm, ain_ref),
                (wqkv_hbm, wqkv_ref),
            )
        )
    ]
    keep = pltpu.make_async_copy(sum_ref, res_hbm, load_sems.at[6])
    swap = pltpu.make_async_remote_copy(
        src_ref=ghost_ref,
        dst_ref=got_ref,
        send_sem=ghost_sems.at[0],
        recv_sem=ghost_sems.at[1],
        device_id=partner(stages[0], 1),
        device_id_type=MESH,
    )

    @pl.when(step == 0)
    def _():
        for load in loads[:2]:
            load.start()
        greet(stages)
        loads[0].wait()
        one.send(0)
        side.send(0)
        two.send(0)
        for load in loads[2:]:
            load.start()
        acc_ref[: 2 * ROWS] = jnp.zeros((2 * ROWS, 2 * width), f32)
        sq_ref[...] = jnp.zeros_like(sq_ref)
        s384_ref[...] = jnp.zeros_like(s384_ref)
        loads[1].wait()

    @pl.when(step == 1)
    def _():
        loads[2].wait()

    def at(when, *todo):
        @pl.when(step == when)
        def _():
            for act, i in todo:
                act(i)

    def scatter(total):
        return [t for i in range(1, last) for t in ((total.take, i), (total.send, i + 1))]

    def gather(total):
        return [t for i in range(last, 1, -1) for t in ((total.settle, i), (total.spread, i - 1))]

    norm_step = frames + 1
    at(1, (one.take, 0), (one.send, 1), (side.take, 0), (side.send, 1), (two.take, 0))
    at(4, (two.send, 1), *scatter(side))
    at(6, *scatter(one))
    at(8, *scatter(two), (side.take, last), (side.spread, last))
    at(9, (one.take, last), (one.spread, last))
    at(10, *gather(side))
    at(11, (two.take, last), (two.spread, last))
    at(13, *gather(one))
    at(15, *gather(two), (side.settle, 1), (side.spread, 0))

    low = lax.broadcasted_iota(jnp.int32, (ROWS, 128), 1) < 64
    ones = jnp.ones((WIN, EXTRA), bf16)
    edge_rows = pl.ds(pl.multiple_of(jnp.where(tm == 0, frames, 1) * ROWS, 16), ROWS)
    ghost_rows = pl.ds(pl.multiple_of(jnp.where(tm == 0, frames + 1, 0) * ROWS, 16), ROWS)

    @pl.when(step < frames)
    def _():
        window = pl.ds(pl.multiple_of(step * ROWS, 16), WIN)
        seen = pl.ds(pl.multiple_of(step * ROWS, 16), 2 * ROWS)
        fresh = pl.ds(pl.multiple_of((step + 2) * ROWS, 16), ROWS)

        def differ(t):
            at = width + t * 128
            v = jnp.concatenate([kv_ref[window, at : at + 128], ones], axis=1)
            d_ref[t % 3] = mm_nt(ga_ref[0, t], v)

        def weigh(t):
            ds_ref[t % 3] = (prob_ref[0, t].astype(f32) * d_ref[t % 3]).astype(bf16)

        def spend(t):
            cols = slice(t * 128, t * 128 + 128)
            vcols = slice(width + t * 128, width + t * 128 + 128)
            ds = ds_ref[t % 3]
            dq = mm(ds, kv_ref[window, cols])
            dq = jnp.where(low, dq[:ROWS], dq[ROWS:]) * (li_ref[0, :, cols] * inv_scale)
            dq_ref[pl.ds(pl.multiple_of(step * ROWS, 16), ROWS), cols] = dq.astype(bf16)
            prob = prob_ref[0, t]
            for left, right, into in ((qs_ref, ds, cols), (gs_ref, prob, vcols)):
                turned = left[0, :, cols].T
                grad = jnp.concatenate([mm(turned[:64], right[:ROWS]), mm(turned[64:], right[ROWS:])], axis=0).T
                acc_ref[seen, into] += grad[: 2 * ROWS]
                acc_ref[fresh, into] = grad[2 * ROWS : 3 * ROWS]

        twins = HEADS // 2
        differ(0)
        for t in range(twins + 1):
            if t + 1 < twins:
                differ(t + 1)
            if t >= 1:
                spend(t - 1)
            if t < twins:
                weigh(t)

    @pl.when(step == frames - 1)
    def _():
        ghost_ref[:, :width] = (acc_ref[ghost_rows, :width] * inv_scale).astype(bf16)
        ghost_ref[:, width:] = acc_ref[ghost_rows, width:].astype(bf16)
        swap.start()
        for load in loads[3:]:
            load.wait()

    def grads_of(start, size, lo, hi):
        here = pl.ds(pl.multiple_of(start, 16), size)
        below = pl.ds(pl.multiple_of(start + ROWS, 16), size)
        parts = []
        if lo < width:
            parts.append(dq_ref[here, lo : min(hi, width)])
        if lo < 2 * width and hi > width:
            parts.append((acc_ref[below, max(lo - width, 0) : min(hi, 2 * width) - width] * inv_scale).astype(bf16))
        if hi > 2 * width:
            parts.append(acc_ref[below, max(lo, 2 * width) - width : hi - width].astype(bf16))
        return jnp.concatenate(parts, axis=1)

    @pl.when(step == frames)
    def _():
        swap.wait()
        got = got_ref[...].astype(f32)
        acc_ref[edge_rows, :width] += got[:, :width] * (1.0 / inv_scale)
        acc_ref[edge_rows, width:] += got[:, width:]

        def weights(lo, hi):
            total = 0.0
            for i in range(frames // 4):
                grads = grads_of(4 * i * ROWS, 4 * ROWS, lo, hi)
                total = total + mm_tn(ain_ref[4 * i : 4 * i + 4].reshape(4 * ROWS, width), grads)
                sq_ref[:, lo:hi] += fold8(grads.astype(f32))
            return total

        def pad(end, stop):
            if end < stop:
                own2_ref[end:stop] = jnp.zeros((stop - end, 16, 128), bf16)

        pad(pack_matrix(own2_ref, 0, weights(0, early_cols)), cut2)
        three.send(0)
        late = weights(early_cols, 3 * width)
        three.take(0)
        three.send(1)
        pad(pack_matrix(own2_ref, cut2, late), own2_ref.shape[0])
        four.send(0)

    at(norm_step + 1, (four.take, 0), (four.send, 1), (one.settle, 1), (one.spread, 0))
    at(norm_step + 4, (three.take, 1), (three.send, 2), (two.settle, 1), (two.spread, 0))

    @pl.when(step == norm_step + 6)
    def _():
        for total in (one, two, side):
            total.settle(0)
        keep.start()

    at(norm_step + 7, (four.take, 1), (four.send, 2))

    @pl.when(step > frames)
    def _():
        i = step - norm_step
        block = 2 * ROWS
        x = x_ref[pl.ds(2 * i, 2)].reshape(block, width).astype(f32)
        n, inverse = normed_of(x)
        up = mm_nt(grads_of(i * block, block, 0, 3 * width), wqkv_ref[...])
        gres = gres_ref[...].reshape(block, width)
        narrow_into(in_ref, 0, gres + norm_back(up, n, inverse, row_ref[:, :width]))
        s384_ref[0] += fold8(up * n)
        s384_ref[1] += fold8(up)

    @pl.when(step == steps - 1)
    def _():
        sq = colsum(sq_ref[...])
        parts = [colsum(s384_ref[0]), colsum(s384_ref[1]), sq[:, :width], sq[:, 2 * width :]]
        lines = [v[:, c : c + 128] for v in parts for c in range(0, width, 128)]
        lines += [jnp.zeros((1, 128), f32)] * (16 - len(lines))
        rows.spread(last, jnp.concatenate(lines, axis=0))
        for i in range(2, count):
            for total in (three, four):
                total.take(i)
                if i < last:
                    total.send(i + 1)
                else:
                    total.spread(last)
        for i in range(last, 0, -1):
            tile = rows.settle(i)
            rows.spread(i - 1, tile)
            for total in (three, four):
                total.settle(i)
                total.spread(i - 1)
        rows_ref[...] = rows.settle(0)
        three.settle(0)
        four.settle(0)
        res2_ref[...] = sum2_ref[...]
        keep.wait()


def unpack_kernel(cut2, in_hbm, res_hbm, res2_ref, rows_ref, out_hbm, gg1, gb1, gqkv_hbm, gqv, gwo_hbm, gbo, gg2, gb2, gw1_hbm,
                  gbf1, gw2_hbm, gbf2, gqkv, gwo, gw1, gw2, res_ref, mid_ref, sems):
    width, hidden = gw1.shape
    tiles = width // 16
    across = hidden // 128 * tiles
    pieces = 4
    piece = in_hbm.shape[0] // pieces
    come, go = [], []
    for i in range(pieces):
        rows = slice(i * piece, (i + 1) * piece)
        come.append(pltpu.make_async_copy(in_hbm.at[rows], mid_ref.at[rows], sems.at[7 + i]))
        go.append(pltpu.make_async_copy(mid_ref.at[rows], out_hbm.at[rows], sems.at[7 + pieces + i]))
    parts = (0, across, 2 * across, res_hbm.shape[0])
    loads = [
        pltpu.make_async_copy(res_hbm.at[lo:hi], res_ref.at[lo:hi], sems.at[i])
        for i, (lo, hi) in enumerate(zip(parts, parts[1:]))
    ]
    stores = [
        pltpu.make_async_copy(src, dst, sems.at[3 + i])
        for i, (src, dst) in enumerate(((gqkv, gqkv_hbm), (gwo, gwo_hbm), (gw1, gw1_hbm), (gw2, gw2_hbm)))
    ]
    for copy in come + loads:
        copy.start()
    for i in range(pieces):
        come[i].wait()
        go[i].start()
    early = 3 * width // 128 // 2
    for c in range(3 * width // 128):
        at = c * tiles if c < early else cut2 + (c - early) * tiles
        gqkv[:, 128 * c : 128 * c + 128] = res2_ref[at : at + tiles].reshape(width, 128).astype(f32)
    stores[0].start()
    loads[0].wait()
    at = 0
    for c in range(hidden // 128):
        gw1[:, 128 * c : 128 * c + 128] = res_ref[at : at + tiles].reshape(width, 128).astype(f32)
        at += tiles
    stores[2].start()
    loads[1].wait()
    for c in range(hidden // 128):
        gw2[128 * c : 128 * c + 128, :] = res_ref[at : at + tiles].reshape(width, 128).astype(f32).T
        at += tiles
    stores[3].start()
    loads[2].wait()
    for c in range(width // 128):
        gwo[:, 128 * c : 128 * c + 128] = res_ref[at : at + tiles].reshape(width, 128).astype(f32)
        at += tiles
    stores[1].start()
    row = 0
    for out in (gg2, gb2, gbo, gbf2, gbf1):
        for c in range(out.shape[0] // 128):
            out[128 * c : 128 * c + 128] = res_ref[at + row // 16].astype(f32)[row % 16]
            row += 1
    rows = rows_ref[...]
    each = width // 128
    for i, out in enumerate((gg1, gb1)):
        for c in range(each):
            out[128 * c : 128 * c + 128] = rows[i * each + c]
    for i in range(2):
        for c in range(each):
            gqv[i : i + 1, 128 * c : 128 * c + 128] = rows[(i + 2) * each + c : (i + 2) * each + c + 1]
    for copy in stores + go:
        copy.wait()


def whole(shape):
    return pl.BlockSpec(shape, lambda i: (0,) * len(shape), pipeline_mode=pl.Buffered(1))


def pairs(shape):
    return pl.BlockSpec((2,) + shape, lambda i: (i,) + (0,) * len(shape))


def single(shape):
    return pl.BlockSpec((1,) + shape, lambda i: (i,) + (0,) * len(shape))


def params(collective=None):
    if collective is None:
        return pltpu.CompilerParams(vmem_limit_bytes=60 * 2**20)
    return pltpu.CompilerParams(vmem_limit_bytes=60 * 2**20, collective_id=collective, has_side_effects=True)


def per_device(tokens, frame_clip, ln1_gain, ln1_bias, w_qkv, qv_bias, w_out, b_out, ln2_gain, ln2_bias,
               w_fc1, b_fc1, w_fc2, b_fc2, cotangent):
    count, width = tokens.shape
    hidden = w_fc1.shape[1]
    frames = count // FRAME
    steps = frames // 2
    tm = lax.axis_index("tm")
    edge = jnp.where(tm == 0, tokens[count - ROWS :], tokens[:ROWS])
    ghost = lax.ppermute(edge, "tm", [(0, 1), (1, 0)])
    in_vmem = pl.BlockSpec(memory_space=pltpu.VMEM)
    in_hbm = pl.BlockSpec(memory_space=pl.ANY)
    kv_rows = (frames + 2) * ROWS + WIN - 3 * ROWS
    shape = jax.ShapeDtypeStruct
    stages = stages_of(lax.axis_size("clips"))
    devices = 2 * lax.axis_size("clips")
    tiles = width // 16
    units = units_for((2 * hidden + width) // 128 * tiles + 2, devices)
    across2 = 3 * width // 128
    first2 = units_for(across2 // 2 * tiles, devices)
    second2 = units_for((across2 - across2 // 2) * tiles, devices)
    units2 = first2 + second2
    x_pad, ain, kv, prob, block_out, qs, ga, gs, gres, li, row, pack = pl.pallas_call(
        forward_kernel,
        grid=(steps,),
        in_specs=[
            pl.BlockSpec(memory_space=pltpu.SMEM),
            in_hbm,
            in_vmem,
            whole((width,)),
            whole((width,)),
            whole((2, width)),
            whole((width,)),
            whole((width,)),
            whole((width,)),
            whole((hidden,)),
            whole((width,)),
            whole((width, 3 * width)),
            in_hbm,
            in_hbm,
            in_hbm,
            in_hbm,
        ],
        out_specs=[
            in_hbm,
            in_hbm,
            in_hbm,
            pairs((HEADS // 2, 2 * ROWS, WIN)),
            pl.BlockSpec((4 * FRAME, width), lambda i: (i // 2, 0)),
            pairs((ROWS, width)),
            pairs((HEADS // 2, 2 * ROWS, 128 + EXTRA)),
            pairs((ROWS, width)),
            pairs((ROWS, width)),
            pairs((ROWS, width)),
            whole((1, 9 * width + hidden)),
            whole((units, 16, 128)),
        ],
        out_shape=[
            shape((frames, ROWS, width), bf16),
            shape((frames, ROWS, width), bf16),
            shape((kv_rows, 2 * width), bf16),
            shape((frames, HEADS // 2, 2 * ROWS, WIN), bf16),
            shape((count, width), bf16),
            shape((frames, ROWS, width), bf16),
            shape((frames, HEADS // 2, 2 * ROWS, 128 + EXTRA), bf16),
            shape((frames, ROWS, width), bf16),
            shape((frames, ROWS, width), f32),
            shape((frames, ROWS, width), f32),
            shape((1, 9 * width + hidden), f32),
            shape((units, 16, 128), bf16),
        ],
        scratch_shapes=[
            pltpu.VMEM((frames, ROWS, width), bf16),
            pltpu.VMEM((frames, ROWS, width), bf16),
            pltpu.VMEM((kv_rows, 2 * width), bf16),
            pltpu.VMEM((count, width), bf16),
            pltpu.VMEM((width, width), bf16),
            pltpu.VMEM((width, hidden), bf16),
            pltpu.VMEM((hidden, width), bf16),
            pltpu.VMEM((frames, ROWS, width), bf16),
            pltpu.VMEM((frames, ROWS, width), bf16),
            pltpu.VMEM((kv_rows, 128), bf16),
            pltpu.VMEM((3, 2 * ROWS, WIN), f32),
            pltpu.VMEM((2 * ROWS, width), f32),
            pltpu.VMEM((4 * FRAME, width), f32),
            pltpu.VMEM((width, hidden), f32),
            pltpu.VMEM((width, hidden), f32),
            pltpu.VMEM((width, width), f32),
            pltpu.VMEM((8, hidden), f32),
            pltpu.VMEM((4, 8, width), f32),
            pltpu.SemaphoreType.DMA((8,)),
        ],
        compiler_params=params(),
    )(frame_clip, tokens, ghost, ln1_gain, ln1_bias, qv_bias, b_out, ln2_gain, ln2_bias, b_fc1, b_fc2, w_qkv, cotangent,
      w_out, w_fc1, w_fc2)

    first, second, side = shares(units, devices)
    early = lambda sh: pl.BlockSpec((1,) + sh, lambda i: (jnp.minimum(i, frames - 1),) + (0,) * len(sh))
    late = lambda i: jnp.maximum(i - frames - 1, 0)
    input_grad, res, res2, sums = pl.pallas_call(
        functools.partial(back_kernel, stages),
        grid=(frames + 1 + steps,),
        in_specs=[
            early((HEADS // 2, 2 * ROWS, WIN)),
            in_hbm,
            early((HEADS // 2, 2 * ROWS, 128 + EXTRA)),
            early((ROWS, width)),
            early((ROWS, width)),
            early((ROWS, width)),
            in_hbm,
            in_hbm,
            pl.BlockSpec((2, ROWS, width), lambda i: (late(i), 0, 0)),
            whole(row.shape),
            in_hbm,
            in_hbm,
        ],
        out_specs=[
            pl.BlockSpec((2 * FRAME, width), lambda i: (late(i), 0)),
            in_hbm,
            whole((units2, 16, 128)),
            whole((16, 128)),
        ],
        out_shape=[
            shape((count, width), f32),
            shape((units, 16, 128), bf16),
            shape((units2, 16, 128), bf16),
            shape((16, 128), f32),
        ],
        scratch_shapes=[
            pltpu.VMEM((kv_rows, 2 * width), f32),
            pltpu.VMEM((3, 2 * ROWS, WIN), f32),
            pltpu.VMEM((3, 2 * ROWS, WIN), bf16),
            pltpu.VMEM((frames * ROWS, width), bf16),
            pltpu.VMEM((8, 3 * width), f32),
            pltpu.VMEM((2, 8, width), f32),
            pltpu.VMEM((units, 16, 128), bf16),
            pltpu.VMEM((units, 16, 128), bf16),
            pltpu.VMEM((units2, 16, 128), bf16),
            pltpu.VMEM((units2, 16, 128), bf16),
            pltpu.VMEM((ROWS, 2 * width), bf16),
            pltpu.VMEM((ROWS, 2 * width), bf16),
            pltpu.VMEM((kv_rows, 2 * width), bf16),
            pltpu.VMEM((frames, ROWS, width), bf16),
            pltpu.VMEM((frames, ROWS, width), bf16),
            pltpu.VMEM((width, 3 * width), bf16),
            pltpu.SemaphoreType.DMA((2,)),
            pltpu.SemaphoreType.DMA((7,)),
        ]
        + sum_scratch(stages, first)
        + sum_scratch(stages, second)
        + sum_scratch(turned(stages), side)
        + sum_scratch(stages, first2)
        + sum_scratch(stages, second2)
        + rows_scratch(stages),
        compiler_params=params(0),
    )(prob, kv, ga, gs, qs, li, x_pad, ain, gres, row, w_qkv, pack)

    sizes = [(width,), (width,), (width, 3 * width), (2, width), (width, width), (width,), (width,), (width,),
             (width, hidden), (hidden,), (hidden, width), (width,)]
    big = [len(z) == 2 and z[0] > 2 for z in sizes]
    outs = pl.pallas_call(
        functools.partial(unpack_kernel, first2),
        in_specs=[in_hbm, in_hbm, in_vmem, in_vmem],
        out_specs=[in_hbm] + [in_hbm if far else in_vmem for far in big],
        out_shape=[shape((count, width), f32)] + [shape(z, f32) for z in sizes],
        scratch_shapes=[
            pltpu.VMEM((width, 3 * width), f32),
            pltpu.VMEM((width, width), f32),
            pltpu.VMEM((width, hidden), f32),
            pltpu.VMEM((hidden, width), f32),
            pltpu.VMEM((units, 16, 128), bf16),
            pltpu.VMEM((count, width), f32),
            pltpu.SemaphoreType.DMA((15,)),
        ],
        compiler_params=params(),
    )(input_grad, res, res2, sums)
    return (block_out,) + tuple(outs)


def solution(mesh):
    rows = P(("clips", "tm"), None)
    rep = P()
    return jax.shard_map(
        per_device,
        mesh=mesh,
        in_specs=(rows, P("clips")) + (rep,) * 12 + (rows,),
        out_specs=(rows, rows) + (rep,) * 12,
        check_vma=False,
    )
```
